32 devices in a mesh: cases: 2 (over y), circ: 4 (over x, core), lat: 4 (over z).
Axes of the slice: x: 2, y: 2, z: 4, core: 2. Of those that a mesh axis runs over, the one named last changes fastest.
Arguments:
- disp: float32 [3, 1024, 512], P(None, ('cases', 'circ'), 'lat'), parts along dimension 1, may hold values from -6 to 6
- stiff: float32 [2, 1024, 512], P(None, ('cases', 'circ'), 'lat'), parts along dimension 1, may hold values from 1 to 4
- spin: float32 [2], P('cases'), parts along dimension 0, may hold values from 0.2 to 0.8
- load: float32 [3, 1024, 512], P(None, ('cases', 'circ'), 'lat'), parts along dimension 1, may hold values from -6 to 6
- foot_node: int32 [32768], P(('cases', 'circ', 'lat')), parts along dimension 0, may hold values from 0 to 16383, as said below
- foot_dest: int32 [32768], P(('cases', 'circ', 'lat')), parts along dimension 0, may hold values from 0 to 15, as said below
- foot_slot: int32 [32768], P(('cases', 'circ', 'lat')), parts along dimension 0, may hold values from 0 to 511
- foot_count: int32 [32], P(('cases', 'circ', 'lat')), parts along dimension 0, may hold values from 0 to 1024, as said below
- road: float32 [16384], P(('cases', 'circ', 'lat')), parts along dimension 0, may hold values from -6 to 6
- active: int32 [16384], P(('cases', 'circ', 'lat')), parts along dimension 0, may hold values 0 or 1
- influence: float32 [32, 512, 512], P(('cases', 'circ', 'lat')), parts along dimension 0, may hold values from 0 to 4, as said below
Outputs:
- new_disp: float32 [3, 1024, 512], P(None, ('cases', 'circ'), 'lat'), parts along dimension 1
- pressure: float32 [16384], P(('cases', 'circ', 'lat')), parts along dimension 0
The draws below stay inside these ranges and needn't reach their ends.
There are 2 independent parts, one for each index of `cases`. The reference program is written for one: setup_inputs(seed, part) draws one part's arguments, and reference() takes and returns one part's arrays. A program takes and returns all parts, laid end to end along the dimension named above; each array names one. Nothing has to cross between parts.
Inputs may be any that keep to these rules, and one draw needn't show every extreme that they name: Rows past a device's foot_count are ignored; among live rows every pair (foot_dest, foot_slot) occurs exactly once over all devices, so each patch receives exactly 512 rows; at most 128 live rows go from one device to one owner, and some device sends exactly 128 to some owner. `foot_node`: a device's live rows name distinct nodes. `foot_count`: counts sum to 8192. `influence`: symmetric positive definite.
All inputs are finite; a program needn't handle non-finite values. No bound on the sum of `active` on one device may be relied on, other than what follows from the above.
Results may differ from the reference program's by a relative error of at most 0.00002.
Values sent between devices are 32-bit elements; how exact they have to be, the bound alone decides.
No kernel may reach another device: no remote copies, remote signals or barrier semaphores. Data moves between devices by JAX's collectives and lax.ppermute only.
A program may use at most 128 MiB of HBM per device.

```python
import math
import jax
import jax.numpy as jnp
from jax import lax

CC = 128
CL = 128
PATCH = 512
GROUP = 128
ROWS_DEV = 1024
PATCHES = 16
NC = 512
NL = 512
N_CIRC = 4
N_LAT = 4


def node_pick(key):
    return jax.random.permutation(key, CC * CL)[:ROWS_DEV].astype(jnp.int32)


def routing(key):
    keys = jax.random.split(key, 5)
    half = PATCHES // 2
    total = PATCHES * PATCH
    order = jax.random.permutation(keys[0], PATCHES)
    spread = jax.random.randint(keys[1], (half,), 0, PATCH + 1).at[0].set(PATCH)
    sizes_all = jnp.concatenate([PATCH + spread, PATCH - spread]).astype(jnp.int32)
    counts = jnp.zeros((PATCHES,), jnp.int32).at[order].set(sizes_all)
    starts = jnp.cumsum(counts) - counts
    rows = (starts[:, None] + jnp.arange(ROWS_DEV, dtype=jnp.int32)[None, :]) % total
    block = rows // GROUP
    patch_id = block % PATCHES
    position = block // PATCHES * GROUP + rows % GROUP
    owners = jax.random.permutation(keys[2], PATCHES).astype(jnp.int32)
    turns = jax.random.randint(keys[3], (PATCHES,), 0, PATCH)
    dest = owners[patch_id]
    slot = (position + turns[patch_id]) % PATCH
    nodes = jax.vmap(node_pick)(jax.random.split(keys[4], PATCHES))
    return (counts, nodes.reshape(-1), dest.reshape(-1).astype(jnp.int32), slot.reshape(-1).astype(jnp.int32))


def draw_foot_count(key, part):
    return routing(key)[0]


def draw_foot_node(key, part):
    return routing(key)[1]


def draw_foot_dest(key, part):
    return routing(key)[2]


def draw_foot_slot(key, part):
    return routing(key)[3]


def harmonic_table():
    table = [0.0]
    running = 0.0
    for place in range(1, PATCH):
        running = running + 1.0 / (1.0 + place)
        table.append(running)
    return table


def draw_influence(key, part):
    key = jax.random.fold_in(key, 7)
    first, second = jax.random.split(key)
    table = harmonic_table()
    kernel_scale = 1.0 / table[PATCH // 2]
    row_bound = [1.2 * kernel_scale * (table[place] + table[PATCH - 1 - place]) for place in range(PATCH)]
    bound_row = jnp.asarray(row_bound, dtype=jnp.float32)
    diagonal = bound_row[None, :] * jax.random.uniform(first, (PATCHES, PATCH), jnp.float32, 1.02, 1.3)
    raw = jax.random.uniform(second, (PATCHES, PATCH, PATCH), jnp.float32, 0.8, 1.2)
    index = jnp.arange(PATCH, dtype=jnp.float32)
    distance = jnp.abs(index[:, None] - index[None, :])
    kernel = kernel_scale / (1.0 + distance)
    off = (raw + jnp.swapaxes(raw, 1, 2)) * 0.5 * kernel[None]
    eye = jnp.eye(PATCH, dtype=jnp.float32)
    return off * (1.0 - eye)[None] + diagonal[:, :, None] * eye[None]


def plant(result, own_key, smallest, top_value):
    spot = [jax.random.randint(jax.random.fold_in(own_key, axis), (), 0, length) for axis, length in enumerate(result.shape)]
    longest = result.shape.index(max(result.shape))
    beside = spot[:longest] + [(spot[longest] + 1) % result.shape[longest]] + spot[longest + 1:]
    return result.at[tuple(spot)].set(smallest).at[tuple(beside)].set(top_value)


def shard_levels(stream_key, extent, cuts, low, largest):
    def one(axis_at, blocks):
        steps = jax.random.uniform(jax.random.fold_in(jax.random.fold_in(stream_key, 6), axis_at), (blocks,), jnp.float32, low / len(cuts), largest / len(cuts))
        return jnp.repeat(jnp.exp(steps), extent[axis_at] // blocks).reshape((-1,) + (1,) * (len(extent) - axis_at - 1))

    gain = one(*cuts[0])
    for cut in cuts[1:]:
        gain = gain * one(*cut)
    return gain


def centred(stream_key, shape, width, limit, pieces=(), kind=jnp.bfloat16):
    drawn = jax.random.normal(stream_key, shape, jnp.float32) * width
    if len(pieces) > 0:
        drawn = shard_levels(stream_key, shape, pieces, -0.22, 0.18) * drawn
    return jnp.clip(drawn, min=-limit, max=limit).astype(kind)


def setup_inputs(seed: int = 0, part: int = 0) -> dict:
    key_list = jax.random.split(jax.random.key(seed), 12)
    part_keys = jax.random.split(jax.random.fold_in(key_list[11], part), 12)
    disp = centred(part_keys[0], (3, NC, NL), 1.0, 6.0, ((1, 4), (2, 4)), jnp.float32)
    stiff = jnp.clip(jnp.exp(math.log(4.0) - 1.3862944 * jax.random.uniform(part_keys[1], (2, NC, NL), jnp.float32) ** shard_levels(part_keys[1], (2, NC, NL), ((1, 4), (2, 4)), -0.2, 0.2)), 1.0, 4.0)
    spin = jnp.clip(jax.random.uniform(part_keys[2], (1,), jnp.float32, 0.2, 0.8), 0.2, 0.8)
    load = centred(part_keys[3], (3, NC, NL), 1.0, 6.0, ((1, 4), (2, 4)), jnp.float32)
    foot_node = draw_foot_node(jax.random.fold_in(jax.random.fold_in(key_list[11], part), 71), part)
    foot_dest = draw_foot_dest(jax.random.fold_in(jax.random.fold_in(key_list[11], part), 71), part)
    foot_slot = draw_foot_slot(jax.random.fold_in(jax.random.fold_in(key_list[11], part), 71), part)
    foot_count = draw_foot_count(jax.random.fold_in(jax.random.fold_in(key_list[11], part), 71), part)
    road = centred(part_keys[8], (PATCHES * PATCH,), 1.0, 6.0, ((0, 16),), jnp.float32)
    active = plant((jax.random.randint(part_keys[9], (PATCHES * PATCH,), 0, 4) < 3).astype(jnp.int32), jax.random.fold_in(part_keys[9], 1), 0, 1)
    influence = draw_influence(jax.random.fold_in(jax.random.fold_in(key_list[11], part), 71), part)
    return dict(disp=disp, stiff=stiff, spin=spin, load=load, foot_node=foot_node, foot_dest=foot_dest, foot_slot=foot_slot, foot_count=foot_count, road=road, active=active, influence=influence)


def reference(disp, stiff, spin, load, foot_node, foot_dest, foot_slot, foot_count, road, active, influence):
    kc = stiff[0] - spin[0]
    kl = stiff[1]
    u_next = jnp.roll(disp, -1, axis=1)
    u_prev = jnp.roll(disp, 1, axis=1)
    padded = jnp.pad(disp, ((0, 0), (0, 0), (1, 1)))
    u_right = padded[:, :, 2:]
    u_left = padded[:, :, :-2]
    stiff_force = kc * (2.0 * disp - u_next - u_prev) + kl * (2.0 * disp - u_right - u_left) + 0.5 * disp
    resid = load - stiff_force
    diag_k = 2.0 * kc + 2.0 * kl + 0.5
    trial = disp + resid / diag_k
    devices = N_CIRC * N_LAT
    owner_dev = jnp.repeat(jnp.arange(devices, dtype=jnp.int32), ROWS_DEV)
    row_pos = jnp.tile(jnp.arange(ROWS_DEV, dtype=jnp.int32), devices)
    live = row_pos < foot_count[owner_dev]
    circ_i = owner_dev // N_LAT * CC + foot_node // CL
    lat_i = owner_dev % N_LAT * CL + foot_node % CL
    w_rows = trial[2][circ_i, lat_i]
    k_rows = diag_k[circ_i, lat_i]
    target = jnp.where(live, foot_dest * PATCH + foot_slot, devices * PATCH).astype(jnp.int32)
    patch_w = jnp.zeros((devices * PATCH,), jnp.float32).at[target].add(w_rows, mode='drop').reshape(devices, PATCH)
    patch_k = jnp.zeros((devices * PATCH,), jnp.float32).at[target].add(k_rows, mode='drop').reshape(devices, PATCH)
    mask = active.reshape(devices, PATCH).astype(jnp.float32)
    eye = jnp.eye(PATCH, dtype=jnp.float32)
    g_mat = influence + eye[None] * (1.0 / patch_k)[:, :, None]
    g_act = mask[:, :, None] * mask[:, None, :] * g_mat + eye[None] * (1.0 - mask)[:, :, None]
    rhs = (mask * (patch_w - road.reshape(devices, PATCH)))[:, :, None]
    factor = jnp.linalg.cholesky(g_act)
    half_sol = lax.linalg.triangular_solve(factor, rhs, left_side=True, lower=True)
    press = lax.linalg.triangular_solve(factor, half_sol, left_side=True, lower=True, transpose_a=True)
    pressure = press.reshape(devices * PATCH)
    pick = jnp.where(live, foot_dest * PATCH + foot_slot, 0).astype(jnp.int32)
    p_rows = pressure[pick] * live.astype(jnp.float32)
    contact_force = jnp.zeros(diag_k.shape, jnp.float32).at[circ_i, lat_i].add(p_rows)
    new_disp = trial.at[2].add(-contact_force / diag_k)
    return (new_disp, pressure)
```

```python
import functools

import jax
import jax.numpy as jnp
from jax import lax
from jax.experimental import pallas as pl
from jax.experimental.pallas import tpu as pltpu
from jax.sharding import PartitionSpec as P

F32 = jnp.float32
BF16 = jnp.bfloat16
I32 = jnp.int32
LANES = 128
CG_STEPS = 40
CG_STOP = 1e-13
TRUE_STOP = 1e-12


def log2(value):
    assert value > 0 and value & (value - 1) == 0
    return value.bit_length() - 1


def thirds(x):
    high = x.astype(BF16).astype(F32)
    rest = x - high
    mid = rest.astype(BF16).astype(F32)
    return high, mid, rest - mid


def iota(shape, axis):
    return lax.broadcasted_iota(I32, shape, axis)


def wide(ref, first, count):
    return jnp.concatenate([ref[i : i + 1, :] for i in range(first, first + count)], axis=1)


def shifted(u):
    rows, cols = u.shape
    row, col = iota(u.shape, 0), iota(u.shape, 1)
    return (
        jnp.where(row == rows - 1, 0.0, pltpu.roll(u, rows - 1, 0)),
        jnp.where(row == 0, 0.0, pltpu.roll(u, 1, 0)),
        jnp.where(col == cols - 1, 0.0, pltpu.roll(u, cols - 1, 1)),
        jnp.where(col == 0, 0.0, pltpu.roll(u, 1, 1)),
    )


def edges(u):
    rows, cols = u.shape
    turned = u.T
    return [u[0:1, :], u[rows - 1 : rows, :], turned[0:1, :], turned[cols - 1 : cols, :]]


def pack_kernel(count, spin, disp, stiff, load, node, dest, slot, send, late):
    owners = send.shape[0]
    rows, cols = disp.shape[1:]
    chunks = node.shape[0]
    size = 4 * LANES
    kc = stiff[0] - spin[0]
    kl = stiff[1]
    u = disp[2]
    u_next, u_prev, u_right, u_left = shifted(u)
    force = kc * (2.0 * u - u_next - u_prev) + kl * (2.0 * u - u_right - u_left) + 0.5 * u
    inner = u + (load[2] - force) / (2.0 * kc + 2.0 * kl + 0.5)
    table = jnp.concatenate(
        [jnp.concatenate(thirds(x), axis=1) for x in (inner, kc, kl)], axis=0
    ).astype(BF16)
    step = 2 if chunks % 2 == 0 else 1
    span = step * LANES
    left, right = [], []
    for first in range(0, chunks, step):
        nodes = wide(node, first, step)
        owner = wide(dest, first, step)
        live = iota((1, span), 1) + first * LANES < count[0]
        owner = jnp.where(live, owner, -1)
        circ = nodes >> log2(cols)
        lat = nodes & (cols - 1)
        one_lat = (iota((cols, span), 0) == lat).astype(BF16)
        picked = jnp.dot(
            table, jnp.concatenate([one_lat] * 3, axis=0), preferred_element_type=F32
        )
        one_circ = iota((rows, span), 0) == circ
        pieces = []
        for k in range(3):
            block = picked[k * rows : (k + 1) * rows]
            pieces += thirds(jnp.sum(jnp.where(one_circ, block, 0.0), axis=0, keepdims=True))
        pieces += [(circ * cols).astype(F32), lat.astype(F32)]
        to = iota((owners, span), 0) == owner
        left.append(
            jnp.concatenate([jnp.where(to, x, 0.0) for x in pieces], axis=0).astype(BF16)
        )
        right.append((iota((size, span), 0) == wide(slot, first, step)).astype(BF16))
    spread = lax.dot_general(
        jnp.concatenate(left, axis=1),
        jnp.concatenate(right, axis=1),
        (((1,), (1,)), ((), ())),
        preferred_element_type=F32,
    )
    part = [spread[i * owners : (i + 1) * owners] for i in range(11)]
    values = [sum(part[3 * k + 1 : 3 * k + 3], part[3 * k]) for k in range(3)] + [part[9] + part[10]]
    for v in range(4):
        for j in range(4):
            send[:, 4 * v + j, :] = values[v][:, j * LANES : (j + 1) * LANES]
    for t, edge in enumerate(edges(u) + edges(disp[0])):
        send[:, 16 + t, :] = jnp.broadcast_to(edge, (owners, LANES))
    for t, edge in enumerate(edges(disp[1])):
        late[t : t + 1, :] = edge


def column(row):
    return jnp.broadcast_to(row, (LANES, row.shape[1])).T


def patch_system(lats, got, road, active):
    owners = got.shape[0]
    rows = cols = LANES
    size = 4 * LANES
    total = jnp.sum(got[:, 0:16, :], axis=0)
    here = got[:, 4:8, :] > 0.0
    sender = jnp.sum(jnp.where(here, lax.broadcasted_iota(I32, here.shape, 0), 0), axis=0)
    w, kc, kl, node = [wide(total, 4 * v, 4) for v in range(4)]
    node = node.astype(I32)
    sender = wide(sender, 0, 4)
    circ = node >> log2(cols)
    lat = node & (cols - 1)
    after = sender + lats
    after = jnp.where(after >= owners, after - owners, after)
    before = sender - lats
    before = jnp.where(before < 0, before + owners, before)
    side = sender & (lats - 1)
    from_circ = jnp.where(
        circ == rows - 1, after * 8, jnp.where(circ == 0, before * 8 + 1, -1)
    )
    from_lat = jnp.where(
        (lat == cols - 1) & (side < lats - 1),
        sender * 8 + 10,
        jnp.where((lat == 0) & (side > 0), sender * 8 - 5, -1),
    )
    layers = got[:, 16:24, :].reshape(owners * 8, LANES)
    layers = jnp.concatenate(thirds(layers), axis=1).astype(BF16)

    def pick(high, low):
        one = (iota((LANES, size), 0) == low).astype(BF16)
        found = jnp.dot(layers, jnp.concatenate([one] * 3, axis=0), preferred_element_type=F32)
        return jnp.sum(
            jnp.where(iota((owners * 8, size), 0) == high, found, 0.0), axis=0, keepdims=True
        )

    diag_k = 2.0 * kc + 2.0 * kl + 0.5
    w = w + (kc * pick(from_circ, lat) + kl * pick(from_lat, circ)) / diag_k
    mask = wide(active, 0, 4).astype(F32)
    return mask, mask * (w - wide(road, 0, 4)), 1.0 / diag_k


def factor_solve(block, mask, rhs, soft, work, press):
    size = rhs.shape[1]
    row = iota((size, 1), 0)
    lane = iota((1, LANES), 1)
    down = column(mask)
    for t in range(size // LANES):
        part = slice(t * LANES, (t + 1) * LANES)
        on = row == lane + t * LANES
        live = mask[:, part]
        work[:, part] = down * live * (block[:, part] + jnp.where(on, soft[:, part], 0.0)) + (
            jnp.where(on, 1.0 - live, 0.0)
        )
    work[:, size:] = column(rhs)
    place = iota((1, size), 1)

    def eliminate(j, carry):
        pivot_row = work[pl.ds(j, 1), :]
        pivot = jnp.sum(jnp.where(place == j, pivot_row[:, :size], 0.0), axis=1, keepdims=True)
        start = pl.multiple_of((j >> log2(LANES)) << log2(LANES), LANES)
        tile = work[:, pl.ds(start, LANES)]
        below = jnp.sum(jnp.where(lane == j - start, tile, 0.0), axis=1, keepdims=True)
        ratio = jnp.where(row > j, below / pivot, 0.0)
        work[...] = work[...] - ratio * pivot_row
        return carry

    lax.fori_loop(0, size, eliminate, 0)

    def substitute(step, x):
        j = size - 1 - step
        now = work[pl.ds(j, 1), :]
        upper = now[:, :size]
        pivot = jnp.sum(jnp.where(place == j, upper, 0.0), axis=1, keepdims=True)
        known = jnp.sum(upper * x, axis=1, keepdims=True)
        return jnp.where(place == j, (now[:, size : size + 1] - known) / pivot, x)

    press[...] = lax.fori_loop(0, size, substitute, jnp.zeros((1, size), F32))


def over(top, bottom):
    return jnp.where(bottom > 0.0, top / bottom, 0.0)


def dot(a, b):
    return jnp.sum(a * b, axis=1, keepdims=True)


def solve_kernel(lats, got, road, active, late, block, send, pressure, work, press):
    size = 4 * LANES
    mask, rhs, soft = patch_system(lats, got, road, active)
    factor_solve(block, mask, rhs, soft, work, press)
    answer = press[...]
    for j in range(4):
        part = answer[:, j * LANES : (j + 1) * LANES]
        pressure[j : j + 1, :] = part
        send[:, j, :] = jnp.broadcast_to(part, (send.shape[0], LANES))
        send[:, 4 + j, :] = jnp.broadcast_to(late[j : j + 1, :], (send.shape[0], LANES))


def finish_kernel(
    axes, count, spin, disp, stiff, load, node, dest, slot, got, back, out
):
    circs, lats = axes
    owners = got.shape[0]
    rows, cols = disp.shape[1:]
    chunks = node.shape[0]
    size = 4 * LANES
    my_circ, my_lat = lax.axis_index("circ"), lax.axis_index("lat")
    me = my_circ * lats + my_lat
    after = jnp.where(my_circ == circs - 1, my_lat, me + lats)
    before = jnp.where(my_circ == 0, (circs - 1) * lats + my_lat, me - lats)
    right_dev = jnp.minimum(me + 1, owners - 1)
    left_dev = jnp.maximum(me - 1, 0)
    kc = stiff[0] - spin[0]
    kl = stiff[1]
    diag_k = 2.0 * kc + 2.0 * kl + 0.5
    row, col = iota((rows, cols), 0), iota((rows, cols), 1)
    trial = []
    for c in range(3):
        u = disp[c]
        source, base = ((got, 20), (back, 4), (got, 16))[c]
        u_next, u_prev, u_right, u_left = shifted(u)
        u_next = jnp.where(row == rows - 1, source[after, base : base + 1, :], u_next)
        u_prev = jnp.where(row == 0, source[before, base + 1 : base + 2, :], u_prev)
        from_right = jnp.where(my_lat < lats - 1, source[right_dev, base + 2 : base + 3, :], 0.0)
        from_left = jnp.where(my_lat > 0, source[left_dev, base + 3 : base + 4, :], 0.0)
        u_right = jnp.where(col == cols - 1, column(from_right), u_right)
        u_left = jnp.where(col == 0, column(from_left), u_left)
        force = kc * (2.0 * u - u_next - u_prev) + kl * (2.0 * u - u_right - u_left) + 0.5 * u
        trial.append(u + (load[c] - force) / diag_k)
    out[0] = trial[0]
    out[1] = trial[1]

    answers = jnp.concatenate([back[:, j, :] for j in range(4)], axis=1)
    answers = jnp.concatenate(thirds(answers), axis=0).astype(BF16)
    step = 2 if chunks % 2 == 0 else 1
    span = step * LANES
    left, right = [], []
    for first in range(0, chunks, step):
        nodes = wide(node, first, step)
        owner = wide(dest, first, step)
        live = iota((1, span), 1) + first * LANES < count[0]
        owner = jnp.where(live, owner, -1)
        circ = nodes >> log2(cols)
        lat = nodes & (cols - 1)
        one_slot = (iota((size, span), 0) == wide(slot, first, step)).astype(BF16)
        found = jnp.dot(answers, one_slot, preferred_element_type=F32)
        found = found[:owners] + found[owners : 2 * owners] + found[2 * owners :]
        push = jnp.sum(
            jnp.where(iota((owners, span), 0) == owner, found, 0.0), axis=0, keepdims=True
        )
        one_circ = iota((rows, span), 0) == circ
        left.append(
            jnp.concatenate(
                [jnp.where(one_circ, x, 0.0) for x in thirds(push)], axis=0
            ).astype(BF16)
        )
        right.append((iota((cols, span), 0) == lat).astype(BF16))
    force = lax.dot_general(
        jnp.concatenate(left, axis=1),
        jnp.concatenate(right, axis=1),
        (((1,), (1,)), ((), ())),
        preferred_element_type=F32,
    )
    force = force[:rows] + force[rows : 2 * rows] + force[2 * rows :]
    out[2] = trial[2] - force / diag_k


def shards(
    disp, stiff, spin, load, foot_node, foot_dest, foot_slot, foot_count, road, active, influence
):
    circs, lats = lax.axis_size("circ"), lax.axis_size("lat")
    owners = circs * lats
    size = road.shape[0]
    rows, cols = disp.shape[1:]
    assert rows == cols == LANES and size == 4 * LANES
    scalar = pl.BlockSpec(memory_space=pltpu.SMEM)
    block = pl.BlockSpec(memory_space=pltpu.VMEM)
    params = pltpu.CompilerParams(vmem_limit_bytes=48 * 1024 * 1024)
    lists = [x.reshape(-1, LANES) for x in (foot_node, foot_dest, foot_slot)]
    send, late = pl.pallas_call(
        pack_kernel,
        in_specs=[scalar, scalar] + [block] * 6,
        out_specs=[block, block],
        out_shape=[
            jax.ShapeDtypeStruct((owners, 24, LANES), F32),
            jax.ShapeDtypeStruct((4, LANES), F32),
        ],
        compiler_params=params,
        name="pack_rows",
    )(foot_count, spin, disp, stiff, load, *lists)
    got = lax.all_to_all(send, ("circ", "lat"), split_axis=0, concat_axis=0, tiled=True)
    reply, pressure = pl.pallas_call(
        functools.partial(solve_kernel, lats),
        in_specs=[block] * 5,
        out_specs=[block, block],
        out_shape=[
            jax.ShapeDtypeStruct((owners, 8, LANES), F32),
            jax.ShapeDtypeStruct((4, LANES), F32),
        ],
        scratch_shapes=[pltpu.VMEM((size, size + LANES), F32), pltpu.VMEM((1, size), F32)],
        compiler_params=params,
        name="solve_patch",
    )(got, road.reshape(4, LANES), active.reshape(4, LANES), late, influence[0])
    back = lax.all_to_all(reply, ("circ", "lat"), split_axis=0, concat_axis=0, tiled=True)
    new_disp = pl.pallas_call(
        functools.partial(finish_kernel, (circs, lats)),
        in_specs=[scalar, scalar] + [block] * 8,
        out_specs=block,
        out_shape=jax.ShapeDtypeStruct(disp.shape, F32),
        compiler_params=params,
        name="finish_nodes",
    )(foot_count, spin, disp, stiff, load, *lists, got, back)
    return (new_disp, pressure.reshape(size))


def solution(mesh):
    return jax.shard_map(
        shards,
        mesh=mesh,
        in_specs=(
            P(None, ("cases", "circ"), "lat"),
            P(None, ("cases", "circ"), "lat"),
            P("cases"),
            P(None, ("cases", "circ"), "lat"),
            P(("cases", "circ", "lat")),
            P(("cases", "circ", "lat")),
            P(("cases", "circ", "lat")),
            P(("cases", "circ", "lat")),
            P(("cases", "circ", "lat")),
            P(("cases", "circ", "lat")),
            P(("cases", "circ", "lat"), None, None),
        ),
        out_specs=(P(None, ("cases", "circ"), "lat"), P(("cases", "circ", "lat"))),
        check_vma=False,
    )
```

```python
import functools

import jax
import jax.numpy as jnp
from jax import lax
from jax.experimental import pallas as pl
from jax.experimental.pallas import tpu as pltpu
from jax.sharding import PartitionSpec as P

F32 = jnp.float32
BF16 = jnp.bfloat16
I32 = jnp.int32
LANES = 128
CG_STEPS = 40
CG_STOP = 1e-13
TRUE_STOP = 1e-12


def log2(value):
    assert value > 0 and value & (value - 1) == 0
    return value.bit_length() - 1


def thirds(x):
    high = x.astype(BF16).astype(F32)
    rest = x - high
    mid = rest.astype(BF16).astype(F32)
    return high, mid, rest - mid


def iota(shape, axis):
    return lax.broadcasted_iota(I32, shape, axis)


def wide(ref, first, count):
    return jnp.concatenate([ref[i : i + 1, :] for i in range(first, first + count)], axis=1)


def shifted(u):
    rows, cols = u.shape
    row, col = iota(u.shape, 0), iota(u.shape, 1)
    return (
        jnp.where(row == rows - 1, 0.0, pltpu.roll(u, rows - 1, 0)),
        jnp.where(row == 0, 0.0, pltpu.roll(u, 1, 0)),
        jnp.where(col == cols - 1, 0.0, pltpu.roll(u, cols - 1, 1)),
        jnp.where(col == 0, 0.0, pltpu.roll(u, 1, 1)),
    )


def edges(u):
    rows, cols = u.shape
    turned = u.T
    return [u[0:1, :], u[rows - 1 : rows, :], turned[0:1, :], turned[cols - 1 : cols, :]]


def pack_kernel(count, spin, disp, stiff, load, node, dest, slot, send, late):
    owners = send.shape[0]
    rows, cols = disp.shape[1:]
    chunks = node.shape[0]
    size = 4 * LANES
    kc = stiff[0] - spin[0]
    kl = stiff[1]
    u = disp[2]
    u_next, u_prev, u_right, u_left = shifted(u)
    force = kc * (2.0 * u - u_next - u_prev) + kl * (2.0 * u - u_right - u_left) + 0.5 * u
    inner = u + (load[2] - force) / (2.0 * kc + 2.0 * kl + 0.5)
    table = jnp.concatenate(
        [jnp.concatenate(thirds(x), axis=1) for x in (inner, kc, kl)], axis=0
    ).astype(BF16)
    step = 2 if chunks % 2 == 0 else 1
    span = step * LANES
    left, right = [], []
    for first in range(0, chunks, step):
        nodes = wide(node, first, step)
        owner = wide(dest, first, step)
        live = iota((1, span), 1) + first * LANES < count[0]
        owner = jnp.where(live, owner, -1)
        circ = nodes >> log2(cols)
        lat = nodes & (cols - 1)
        one_lat = (iota((cols, span), 0) == lat).astype(BF16)
        picked = jnp.dot(
            table, jnp.concatenate([one_lat] * 3, axis=0), preferred_element_type=F32
        )
        one_circ = iota((rows, span), 0) == circ
        pieces = []
        for k in range(3):
            block = picked[k * rows : (k + 1) * rows]
            pieces += thirds(jnp.sum(jnp.where(one_circ, block, 0.0), axis=0, keepdims=True))
        pieces += [(circ * cols).astype(F32), lat.astype(F32)]
        to = iota((owners, span), 0) == owner
        left.append(
            jnp.concatenate([jnp.where(to, x, 0.0) for x in pieces], axis=0).astype(BF16)
        )
        right.append((iota((size, span), 0) == wide(slot, first, step)).astype(BF16))
    spread = lax.dot_general(
        jnp.concatenate(left, axis=1),
        jnp.concatenate(right, axis=1),
        (((1,), (1,)), ((), ())),
        preferred_element_type=F32,
    )
    part = [spread[i * owners : (i + 1) * owners] for i in range(11)]
    values = [sum(part[3 * k + 1 : 3 * k + 3], part[3 * k]) for k in range(3)] + [part[9] + part[10]]
    for v in range(4):
        for j in range(4):
            send[:, 4 * v + j, :] = values[v][:, j * LANES : (j + 1) * LANES]
    for t, edge in enumerate(edges(u) + edges(disp[0])):
        send[:, 16 + t, :] = jnp.broadcast_to(edge, (owners, LANES))
    for t, edge in enumerate(edges(disp[1])):
        late[t : t + 1, :] = edge


def column(row):
    return jnp.broadcast_to(row, (LANES, row.shape[1])).T


def patch_system(lats, got, road, active):
    owners = got.shape[0]
    rows = cols = LANES
    size = 4 * LANES
    total = jnp.sum(got[:, 0:16, :], axis=0)
    here = got[:, 4:8, :] > 0.0
    sender = jnp.sum(jnp.where(here, lax.broadcasted_iota(I32, here.shape, 0), 0), axis=0)
    w, kc, kl, node = [wide(total, 4 * v, 4) for v in range(4)]
    node = node.astype(I32)
    sender = wide(sender, 0, 4)
    circ = node >> log2(cols)
    lat = node & (cols - 1)
    after = sender + lats
    after = jnp.where(after >= owners, after - owners, after)
    before = sender - lats
    before = jnp.where(before < 0, before + owners, before)
    side = sender & (lats - 1)
    from_circ = jnp.where(
        circ == rows - 1, after * 8, jnp.where(circ == 0, before * 8 + 1, -1)
    )
    from_lat = jnp.where(
        (lat == cols - 1) & (side < lats - 1),
        sender * 8 + 10,
        jnp.where((lat == 0) & (side > 0), sender * 8 - 5, -1),
    )
    layers = got[:, 16:24, :].reshape(owners * 8, LANES)
    layers = jnp.concatenate(thirds(layers), axis=1).astype(BF16)

    def pick(high, low):
        one = (iota((LANES, size), 0) == low).astype(BF16)
        found = jnp.dot(layers, jnp.concatenate([one] * 3, axis=0), preferred_element_type=F32)
        return jnp.sum(
            jnp.where(iota((owners * 8, size), 0) == high, found, 0.0), axis=0, keepdims=True
        )

    diag_k = 2.0 * kc + 2.0 * kl + 0.5
    w = w + (kc * pick(from_circ, lat) + kl * pick(from_lat, circ)) / diag_k
    mask = wide(active, 0, 4).astype(F32)
    return mask, mask * (w - wide(road, 0, 4)), 1.0 / diag_k


def factor_solve(block, mask, rhs, soft, work, press):
    size = rhs.shape[1]
    row = iota((size, 1), 0)
    lane = iota((1, LANES), 1)
    down = column(mask)
    for t in range(size // LANES):
        part = slice(t * LANES, (t + 1) * LANES)
        on = row == lane + t * LANES
        live = mask[:, part]
        work[:, part] = down * live * (block[:, part] + jnp.where(on, soft[:, part], 0.0)) + (
            jnp.where(on, 1.0 - live, 0.0)
        )
    work[:, size:] = column(rhs)
    place = iota((1, size), 1)

    def eliminate(j, carry):
        pivot_row = work[pl.ds(j, 1), :]
        pivot = jnp.sum(jnp.where(place == j, pivot_row[:, :size], 0.0), axis=1, keepdims=True)
        start = pl.multiple_of((j >> log2(LANES)) << log2(LANES), LANES)
        tile = work[:, pl.ds(start, LANES)]
        below = jnp.sum(jnp.where(lane == j - start, tile, 0.0), axis=1, keepdims=True)
        ratio = jnp.where(row > j, below / pivot, 0.0)
        work[...] = work[...] - ratio * pivot_row
        return carry

    lax.fori_loop(0, size, eliminate, 0)

    def substitute(step, x):
        j = size - 1 - step
        now = work[pl.ds(j, 1), :]
        upper = now[:, :size]
        pivot = jnp.sum(jnp.where(place == j, upper, 0.0), axis=1, keepdims=True)
        known = jnp.sum(upper * x, axis=1, keepdims=True)
        return jnp.where(place == j, (now[:, size : size + 1] - known) / pivot, x)

    press[...] = lax.fori_loop(0, size, substitute, jnp.zeros((1, size), F32))


def over(top, bottom):
    return jnp.where(bottom > 0.0, top / bottom, 0.0)


def dot(a, b):
    return jnp.sum(a * b, axis=1, keepdims=True)


def times(block, u, mask, soft):
    down = column(u)
    parts = [
        jnp.sum(block[:, first : first + LANES] * down, axis=0, keepdims=True)
        for first in range(0, u.shape[1], LANES)
    ]
    return mask * (jnp.concatenate(parts, axis=1) + soft * u)


def solve_kernel(lats, got, road, active, late, block, send, pressure, work, press):
    size = 4 * LANES
    mask, rhs, soft = patch_system(lats, got, road, active)
    square = iota((LANES, LANES), 0) == iota((LANES, LANES), 1)
    diagonal = jnp.concatenate(
        [
            jnp.sum(
                jnp.where(square, block[i : i + LANES, i : i + LANES], 0.0), axis=0, keepdims=True
            )
            for i in range(0, size, LANES)
        ],
        axis=1,
    )
    scale = mask / (diagonal + soft)
    start = dot(rhs, scale * rhs)

    def advance(x, r, p, s, norm, alpha):
        u = scale * r
        w = times(block, u, mask, soft)
        now = dot(r, u)
        beta = over(now, norm)
        alpha = over(now, dot(w, u) - over(beta * now, alpha))
        p = u + beta * p
        s = w + beta * s
        return x + alpha * p, r - alpha * s, p, s, now, alpha

    def going(state):
        step, norm = state[0], state[5]
        return (step < CG_STEPS) & (norm[0, 0] > CG_STOP * start[0, 0])

    def body(state):
        return (state[0] + 2,) + advance(*advance(*state[1:]))

    zero = jnp.zeros((1, size), F32)
    none = jnp.zeros((1, 1), F32)
    x = lax.while_loop(going, body, (0, zero, rhs, zero, zero, start, none))[1]
    gap = rhs - times(block, x, mask, soft)
    press[...] = x

    @pl.when(jnp.logical_not(dot(gap, scale * gap)[0, 0] <= TRUE_STOP * start[0, 0]))
    def _():
        factor_solve(block, mask, rhs, soft, work, press)

    answer = press[...]
    for j in range(4):
        part = answer[:, j * LANES : (j + 1) * LANES]
        pressure[j : j + 1, :] = part
        send[:, j, :] = jnp.broadcast_to(part, (send.shape[0], LANES))
        send[:, 4 + j, :] = jnp.broadcast_to(late[j : j + 1, :], (send.shape[0], LANES))


def finish_kernel(
    axes, count, spin, disp, stiff, load, node, dest, slot, got, back, out
):
    circs, lats = axes
    owners = got.shape[0]
    rows, cols = disp.shape[1:]
    chunks = node.shape[0]
    size = 4 * LANES
    my_circ, my_lat = lax.axis_index("circ"), lax.axis_index("lat")
    me = my_circ * lats + my_lat
    after = jnp.where(my_circ == circs - 1, my_lat, me + lats)
    before = jnp.where(my_circ == 0, (circs - 1) * lats + my_lat, me - lats)
    right_dev = jnp.minimum(me + 1, owners - 1)
    left_dev = jnp.maximum(me - 1, 0)
    kc = stiff[0] - spin[0]
    kl = stiff[1]
    diag_k = 2.0 * kc + 2.0 * kl + 0.5
    row, col = iota((rows, cols), 0), iota((rows, cols), 1)
    trial = []
    for c in range(3):
        u = disp[c]
        source, base = ((got, 20), (back, 4), (got, 16))[c]
        u_next, u_prev, u_right, u_left = shifted(u)
        u_next = jnp.where(row == rows - 1, source[after, base : base + 1, :], u_next)
        u_prev = jnp.where(row == 0, source[before, base + 1 : base + 2, :], u_prev)
        from_right = jnp.where(my_lat < lats - 1, source[right_dev, base + 2 : base + 3, :], 0.0)
        from_left = jnp.where(my_lat > 0, source[left_dev, base + 3 : base + 4, :], 0.0)
        u_right = jnp.where(col == cols - 1, column(from_right), u_right)
        u_left = jnp.where(col == 0, column(from_left), u_left)
        force = kc * (2.0 * u - u_next - u_prev) + kl * (2.0 * u - u_right - u_left) + 0.5 * u
        trial.append(u + (load[c] - force) / diag_k)
    out[0] = trial[0]
    out[1] = trial[1]

    answers = jnp.concatenate([back[:, j, :] for j in range(4)], axis=1)
    answers = jnp.concatenate(thirds(answers), axis=0).astype(BF16)
    step = 2 if chunks % 2 == 0 else 1
    span = step * LANES
    left, right = [], []
    for first in range(0, chunks, step):
        nodes = wide(node, first, step)
        owner = wide(dest, first, step)
        live = iota((1, span), 1) + first * LANES < count[0]
        owner = jnp.where(live, owner, -1)
        circ = nodes >> log2(cols)
        lat = nodes & (cols - 1)
        one_slot = (iota((size, span), 0) == wide(slot, first, step)).astype(BF16)
        found = jnp.dot(answers, one_slot, preferred_element_type=F32)
        found = found[:owners] + found[owners : 2 * owners] + found[2 * owners :]
        push = jnp.sum(
            jnp.where(iota((owners, span), 0) == owner, found, 0.0), axis=0, keepdims=True
        )
        one_circ = iota((rows, span), 0) == circ
        left.append(
            jnp.concatenate(
                [jnp.where(one_circ, x, 0.0) for x in thirds(push)], axis=0
            ).astype(BF16)
        )
        right.append((iota((cols, span), 0) == lat).astype(BF16))
    force = lax.dot_general(
        jnp.concatenate(left, axis=1),
        jnp.concatenate(right, axis=1),
        (((1,), (1,)), ((), ())),
        preferred_element_type=F32,
    )
    force = force[:rows] + force[rows : 2 * rows] + force[2 * rows :]
    out[2] = trial[2] - force / diag_k


def shards(
    disp, stiff, spin, load, foot_node, foot_dest, foot_slot, foot_count, road, active, influence
):
    circs, lats = lax.axis_size("circ"), lax.axis_size("lat")
    owners = circs * lats
    size = road.shape[0]
    rows, cols = disp.shape[1:]
    assert rows == cols == LANES and size == 4 * LANES
    scalar = pl.BlockSpec(memory_space=pltpu.SMEM)
    block = pl.BlockSpec(memory_space=pltpu.VMEM)
    params = pltpu.CompilerParams(vmem_limit_bytes=48 * 1024 * 1024)
    lists = [x.reshape(-1, LANES) for x in (foot_node, foot_dest, foot_slot)]
    send, late = pl.pallas_call(
        pack_kernel,
        in_specs=[scalar, scalar] + [block] * 6,
        out_specs=[block, block],
        out_shape=[
            jax.ShapeDtypeStruct((owners, 24, LANES), F32),
            jax.ShapeDtypeStruct((4, LANES), F32),
        ],
        compiler_params=params,
        name="pack_rows",
    )(foot_count, spin, disp, stiff, load, *lists)
    got = lax.all_to_all(send, ("circ", "lat"), split_axis=0, concat_axis=0, tiled=True)
    reply, pressure = pl.pallas_call(
        functools.partial(solve_kernel, lats),
        in_specs=[block] * 5,
        out_specs=[block, block],
        out_shape=[
            jax.ShapeDtypeStruct((owners, 8, LANES), F32),
            jax.ShapeDtypeStruct((4, LANES), F32),
        ],
        scratch_shapes=[pltpu.VMEM((size, size + LANES), F32), pltpu.VMEM((1, size), F32)],
        compiler_params=params,
        name="solve_patch",
    )(got, road.reshape(4, LANES), active.reshape(4, LANES), late, influence[0])
    back = lax.all_to_all(reply, ("circ", "lat"), split_axis=0, concat_axis=0, tiled=True)
    new_disp = pl.pallas_call(
        functools.partial(finish_kernel, (circs, lats)),
        in_specs=[scalar, scalar] + [block] * 8,
        out_specs=block,
        out_shape=jax.ShapeDtypeStruct(disp.shape, F32),
        compiler_params=params,
        name="finish_nodes",
    )(foot_count, spin, disp, stiff, load, *lists, got, back)
    return (new_disp, pressure.reshape(size))


def solution(mesh):
    return jax.shard_map(
        shards,
        mesh=mesh,
        in_specs=(
            P(None, ("cases", "circ"), "lat"),
            P(None, ("cases", "circ"), "lat"),
            P("cases"),
            P(None, ("cases", "circ"), "lat"),
            P(("cases", "circ", "lat")),
            P(("cases", "circ", "lat")),
            P(("cases", "circ", "lat")),
            P(("cases", "circ", "lat")),
            P(("cases", "circ", "lat")),
            P(("cases", "circ", "lat")),
            P(("cases", "circ", "lat"), None, None),
        ),
        out_specs=(P(None, ("cases", "circ"), "lat"), P(("cases", "circ", "lat"))),
        check_vma=False,
    )
```

```python
import functools

import jax
import jax.numpy as jnp
from jax import lax
from jax.experimental import pallas as pl
from jax.experimental.pallas import tpu as pltpu
from jax.sharding import PartitionSpec as P

F32 = jnp.float32
BF16 = jnp.bfloat16
I32 = jnp.int32
LANES = 128
CG_STEPS = 40
CG_STOP = 1e-13
TRUE_STOP = 1e-12


def log2(value):
    assert value > 0 and value & (value - 1) == 0
    return value.bit_length() - 1


def thirds(x):
    high = x.astype(BF16).astype(F32)
    rest = x - high
    mid = rest.astype(BF16).astype(F32)
    return high, mid, rest - mid


def iota(shape, axis):
    return lax.broadcasted_iota(I32, shape, axis)


def wide(ref, first, count):
    return jnp.concatenate([ref[i : i + 1, :] for i in range(first, first + count)], axis=1)


def shifted(u):
    rows, cols = u.shape
    row, col = iota(u.shape, 0), iota(u.shape, 1)
    return (
        jnp.where(row == rows - 1, 0.0, pltpu.roll(u, rows - 1, 0)),
        jnp.where(row == 0, 0.0, pltpu.roll(u, 1, 0)),
        jnp.where(col == cols - 1, 0.0, pltpu.roll(u, cols - 1, 1)),
        jnp.where(col == 0, 0.0, pltpu.roll(u, 1, 1)),
    )


def edges(u):
    rows, cols = u.shape
    turned = u.T
    return [u[0:1, :], u[rows - 1 : rows, :], turned[0:1, :], turned[cols - 1 : cols, :]]


def pack_kernel(
    axes, disp, stiff, load, node, dest, slot, count, spin, road, active, block,
    send, trial, near, nodes, owner, slots, roads, actives, blocks,
    u, springs, loads, dests, counts, spins, sems,
):
    circs, lats = axes
    owners = send.shape[0]
    rows, cols = disp.shape[1:]
    chunks = node.shape[0]
    pairs = [
        (count, counts), (spin, spins), (node, nodes), (dest, dests), (slot, slots),
        (stiff, springs), (disp, u), (load, loads), (road, roads), (active, actives),
        (block, blocks),
    ]
    copies = [pltpu.make_async_copy(a, b, sems.at[i]) for i, (a, b) in enumerate(pairs)]
    for copy in copies:
        copy.start()
    for copy in copies[:5]:
        copy.wait()

    width = 2 * LANES if chunks % 2 == 0 else LANES
    step = width // LANES
    to, tos = [], []
    for i in range(chunks):
        live = iota((1, LANES), 1) + i * LANES < counts[0]
        target = jnp.where(live, dests[i : i + 1, :], -1)
        owner[i : i + 1, :] = target
        to.append(iota((owners, LANES), 0) == target)
        tos.append(to[i].astype(F32).astype(BF16))
    before = iota((LANES, 2 * LANES), 0) < iota((LANES, 2 * LANES), 1)
    ranks = jnp.dot(
        jnp.concatenate(tos, axis=0), before.astype(F32).astype(BF16), preferred_element_type=F32
    )
    passed = jnp.zeros((owners, LANES), F32)
    right = []
    for i in range(chunks):
        mine = ranks[i * owners : (i + 1) * owners]
        rank = jnp.sum(
            jnp.where(to[i], mine[:, :LANES] + passed, 0.0), axis=0, keepdims=True
        ).astype(I32)
        passed = passed + mine[:, LANES:]
        right.append((iota((LANES, LANES), 0) == rank).astype(F32).astype(BF16))

    for copy in copies[5:8]:
        copy.wait()
    kc = springs[0] - spins[0]
    kl = springs[1]
    diag_k = 2.0 * kc + 2.0 * kl + 0.5
    near[0] = kc
    near[1] = kl
    near[2] = diag_k
    for c in range(3):
        own = u[c]
        u_next, u_prev, u_right, u_left = shifted(own)
        force = kc * (2.0 * own - u_next - u_prev) + kl * (2.0 * own - u_right - u_left) + 0.5 * own
        trial[c] = own + (loads[c] - force) / diag_k
    table = jnp.concatenate(
        [jnp.concatenate(thirds(x), axis=1) for x in (trial[2], kc, kl)], axis=0
    ).astype(BF16)
    left = []
    for first in range(0, chunks, step):
        place = wide(nodes, first, step)
        circ = place >> log2(cols)
        lat = place & (cols - 1)
        one_lat = (iota((cols, width), 0) == lat).astype(F32).astype(BF16)
        picked = jnp.dot(
            table, jnp.concatenate([one_lat] * 3, axis=0), preferred_element_type=F32
        )
        one_circ = iota((rows, width), 0) == circ
        pieces = []
        for k in range(3):
            found = picked[k * rows : (k + 1) * rows]
            pieces += thirds(jnp.sum(jnp.where(one_circ, found, 0.0), axis=0, keepdims=True))
        where = wide(slots, first, step)
        low = where & (LANES - 1)
        pieces += [x.astype(F32) for x in (circ * cols, lat, where - low, low)]
        here = jnp.concatenate(to[first : first + step], axis=1)
        left.append(
            jnp.concatenate([jnp.where(here, x, 0.0) for x in pieces], axis=0).astype(BF16)
        )
    spread = lax.dot_general(
        jnp.concatenate(left, axis=1),
        jnp.concatenate(right, axis=1),
        (((1,), (1,)), ((), ())),
        preferred_element_type=F32,
    )
    part = [spread[i * owners : (i + 1) * owners] for i in range(13)]
    for v in range(3):
        send[:, 0, v, :] = part[3 * v] + part[3 * v + 1] + part[3 * v + 2]
    send[:, 0, 3, :] = part[9] + part[10]
    send[:, 2, 0, :] = part[11] + part[12]

    my_circ, my_lat = lax.axis_index("circ"), lax.axis_index("lat")
    me = my_circ * lats + my_lat
    after = jnp.where(my_circ == circs - 1, my_lat, me + lats)
    prior = jnp.where(my_circ == 0, (circs - 1) * lats + my_lat, me - lats)
    east = jnp.where(my_lat < lats - 1, me + 1, -1)
    west = jnp.where(my_lat > 0, me - 1, -1)
    device = iota((owners, LANES), 0)
    for c in range(3):
        layers = edges(u[c])
        lacks = jnp.zeros((owners, LANES), F32)
        for layer, reader in zip(layers, (prior, after, west, east)):
            lacks = jnp.where(device == reader, layer, lacks)
        send[:, 2, 1 + c, :] = lacks
        if c == 2:
            for t, layer in enumerate(layers):
                send[:, 1, t, :] = jnp.broadcast_to(layer, (owners, LANES))
    for copy in copies[8:]:
        copy.wait()


def column(row):
    return jnp.broadcast_to(row, (LANES, row.shape[1])).T


def patch_system(lats, got, road, active, rowed, layered):
    owners = got.shape[0]
    rows = cols = LANES
    size = 4 * LANES
    group = 16
    total = jnp.zeros((4 * group, LANES), F32)
    for first in range(0, owners, group):
        some = slice(first, first + group)
        w, kc, kl, node = [got[some, 0, v, :] for v in range(4)]
        slot = got[some, 2, 0, :].astype(I32)
        node = node.astype(I32)
        lat = node & (cols - 1)
        sender = jnp.where(kc > 0.0, iota(kc.shape, 0) + first, 0)
        pieces = thirds(w) + thirds(kc) + thirds(kl)
        pieces += tuple(x.astype(F32) for x in (node - lat, lat, sender))
        for p, piece in enumerate(pieces):
            rowed[p] = piece
        rowed[12] = (slot >> log2(LANES)).astype(F32)
        rowed[13] = (slot & (LANES - 1)).astype(F32)
        rowed[14:16] = jnp.zeros((2,) + kc.shape, F32)
        left, right = [], []
        for d in range(group):
            stack = rowed[:, d, :]
            high, low = stack[12:13, :], stack[13:14, :]
            left.append(
                jnp.concatenate(
                    [jnp.where(high == float(h), stack, 0.0) for h in range(4)], axis=0
                ).astype(BF16)
            )
            right.append(
                (iota((LANES, LANES), 0) == low.astype(I32)).astype(F32).astype(BF16)
            )
        total = total + lax.dot_general(
            jnp.concatenate(left, axis=1),
            jnp.concatenate(right, axis=1),
            (((1,), (1,)), ((), ())),
            preferred_element_type=F32,
        )
    values = []
    for at in ((0, 1, 2), (3, 4, 5), (6, 7, 8), (9, 10), (10,), (11,)):
        strips = []
        for h in range(4):
            strip = total[group * h + at[0] : group * h + at[0] + 1, :]
            for p in at[1:]:
                strip = strip + total[group * h + p : group * h + p + 1, :]
            strips.append(strip)
        values.append(jnp.concatenate(strips, axis=1))
    w, kc, kl = values[:3]
    node, lat, sender = [x.astype(I32) for x in values[3:]]
    circ = node >> log2(cols)
    after = sender + lats
    after = jnp.where(after >= owners, after - owners, after)
    before = sender - lats
    before = jnp.where(before < 0, before + owners, before)
    side = sender & (lats - 1)
    from_circ = jnp.where(
        circ == rows - 1, after, jnp.where(circ == 0, before + owners, -1)
    )
    from_lat = jnp.where(
        (lat == cols - 1) & (side < lats - 1),
        sender + 1 + 2 * owners,
        jnp.where((lat == 0) & (side > 0), sender - 1 + 3 * owners, -1),
    )
    for t in range(4):
        layered[t] = got[:, 1, t, :]
    layers = layered[...].reshape(owners * 4, LANES)
    layers = jnp.concatenate(thirds(layers), axis=1).astype(BF16)

    def pick(high, low):
        one = (iota((LANES, size), 0) == low).astype(F32).astype(BF16)
        found = jnp.dot(layers, jnp.concatenate([one] * 3, axis=0), preferred_element_type=F32)
        return jnp.sum(
            jnp.where(iota((owners * 4, size), 0) == high, found, 0.0), axis=0, keepdims=True
        )

    diag_k = 2.0 * kc + 2.0 * kl + 0.5
    w = w + (kc * pick(from_circ, lat) + kl * pick(from_lat, circ)) / diag_k
    mask = wide(active, 0, 4).astype(F32)
    return mask, mask * (w - wide(road, 0, 4)), 1.0 / diag_k


def factor_solve(block, mask, rhs, soft, work, press):
    size = rhs.shape[1]
    row = iota((size, 1), 0)
    lane = iota((1, LANES), 1)
    down = column(mask)
    for t in range(size // LANES):
        part = slice(t * LANES, (t + 1) * LANES)
        on = row == lane + t * LANES
        live = mask[:, part]
        work[:, part] = down * live * (block[:, part] + jnp.where(on, soft[:, part], 0.0)) + (
            jnp.where(on, 1.0 - live, 0.0)
        )
    work[:, size:] = column(rhs)
    place = iota((1, size), 1)

    def eliminate(j, carry):
        pivot_row = work[pl.ds(j, 1), :]
        pivot = jnp.sum(jnp.where(place == j, pivot_row[:, :size], 0.0), axis=1, keepdims=True)
        start = pl.multiple_of((j >> log2(LANES)) << log2(LANES), LANES)
        tile = work[:, pl.ds(start, LANES)]
        below = jnp.sum(jnp.where(lane == j - start, tile, 0.0), axis=1, keepdims=True)
        ratio = jnp.where(row > j, below / pivot, 0.0)
        work[...] = work[...] - ratio * pivot_row
        return carry

    lax.fori_loop(0, size, eliminate, 0)

    def substitute(step, x):
        j = size - 1 - step
        now = work[pl.ds(j, 1), :]
        upper = now[:, :size]
        pivot = jnp.sum(jnp.where(place == j, upper, 0.0), axis=1, keepdims=True)
        known = jnp.sum(upper * x, axis=1, keepdims=True)
        return jnp.where(place == j, (now[:, size : size + 1] - known) / pivot, x)

    press[...] = lax.fori_loop(0, size, substitute, jnp.zeros((1, size), F32))


def over(top, bottom):
    return jnp.where(bottom > 0.0, top / bottom, 0.0)


def dot(a, b):
    return jnp.sum(a * b, axis=1, keepdims=True)


def times(block, u, mask, soft):
    down = column(u)
    parts = [
        jnp.sum(block[:, first : first + LANES] * down, axis=0, keepdims=True)
        for first in range(0, u.shape[1], LANES)
    ]
    return mask * (jnp.concatenate(parts, axis=1) + soft * u)


def solve_kernel(
    lats, got, road, active, block, send, pressure, work, press, rowed, layered
):
    size = 4 * LANES
    mask, rhs, soft = patch_system(lats, got, road, active, rowed, layered)
    square = iota((LANES, LANES), 0) == iota((LANES, LANES), 1)
    diagonal = jnp.concatenate(
        [
            jnp.sum(
                jnp.where(square, block[i : i + LANES, i : i + LANES], 0.0), axis=0, keepdims=True
            )
            for i in range(0, size, LANES)
        ],
        axis=1,
    )
    scale = mask / (diagonal + soft)
    start = dot(rhs, scale * rhs)

    def advance(x, r, p, s, norm, alpha):
        u = scale * r
        w = times(block, u, mask, soft)
        now = dot(r, u)
        beta = over(now, norm)
        alpha = over(now, dot(w, u) - over(beta * now, alpha))
        p = u + beta * p
        s = w + beta * s
        return x + alpha * p, r - alpha * s, p, s, now, alpha

    def going(state):
        step, norm = state[0], state[5]
        return (step < CG_STEPS) & (norm[0, 0] > CG_STOP * start[0, 0])

    def body(state):
        return (state[0] + 2,) + advance(*advance(*state[1:]))

    zero = jnp.zeros((1, size), F32)
    none = jnp.zeros((1, 1), F32)
    x = lax.while_loop(going, body, (0, zero, rhs, zero, zero, start, none))[1]
    gap = rhs - times(block, x, mask, soft)
    press[...] = x

    @pl.when(jnp.logical_not(dot(gap, scale * gap)[0, 0] <= TRUE_STOP * start[0, 0]))
    def _():
        factor_solve(block, mask, rhs, soft, work, press)

    answer = press[...]
    for j in range(4):
        part = answer[:, j * LANES : (j + 1) * LANES]
        pressure[j : j + 1, :] = part
        send[:, j, :] = jnp.broadcast_to(part, (send.shape[0], LANES))


def finish_kernel(axes, trial, near, node, owner, slot, got, back, out):
    circs, lats = axes
    owners = got.shape[0]
    rows, cols = trial.shape[1:]
    chunks = node.shape[0]
    my_circ, my_lat = lax.axis_index("circ"), lax.axis_index("lat")
    me = my_circ * lats + my_lat
    after = jnp.where(my_circ == circs - 1, my_lat, me + lats)
    before = jnp.where(my_circ == 0, (circs - 1) * lats + my_lat, me - lats)
    right_dev = jnp.minimum(me + 1, owners - 1)
    left_dev = jnp.maximum(me - 1, 0)
    kc, kl, diag_k = near[0], near[1], near[2]
    row, col = iota((rows, cols), 0), iota((rows, cols), 1)
    for c in range(3):
        down, up = got[after, 2, 1 + c : 2 + c, :], got[before, 2, 1 + c : 2 + c, :]
        east, west = got[right_dev, 2, 1 + c : 2 + c, :], got[left_dev, 2, 1 + c : 2 + c, :]
        east = jnp.where(my_lat < lats - 1, east, 0.0)
        west = jnp.where(my_lat > 0, west, 0.0)
        circ_in = jnp.where(row == rows - 1, down, jnp.where(row == 0, up, 0.0))
        lat_in = jnp.where(
            col == cols - 1, column(east), jnp.where(col == 0, column(west), 0.0)
        )
        out[c] = trial[c] + (kc * circ_in + kl * lat_in) / diag_k

    answers = jnp.concatenate([back[:, j, :] for j in range(4)], axis=0)
    answers = jnp.concatenate(thirds(answers), axis=1).astype(BF16)
    step = 2 if chunks % 2 == 0 else 1
    span = step * LANES
    left, right = [], []
    for first in range(0, chunks, step):
        nodes = wide(node, first, step)
        where = wide(slot, first, step)
        device = wide(owner, first, step)
        low = where & (LANES - 1)
        source = jnp.where(device < 0, -1, (where >> log2(LANES)) * owners + device)
        one_low = (iota((LANES, span), 0) == low).astype(F32).astype(BF16)
        found = jnp.dot(
            answers, jnp.concatenate([one_low] * 3, axis=0), preferred_element_type=F32
        )
        push = jnp.sum(
            jnp.where(iota((4 * owners, span), 0) == source, found, 0.0), axis=0, keepdims=True
        )
        one_circ = iota((rows, span), 0) == nodes >> log2(cols)
        left.append(
            jnp.concatenate(
                [jnp.where(one_circ, x, 0.0) for x in thirds(push)], axis=0
            ).astype(BF16)
        )
        right.append((iota((cols, span), 0) == (nodes & (cols - 1))).astype(F32).astype(BF16))
    force = lax.dot_general(
        jnp.concatenate(left, axis=1),
        jnp.concatenate(right, axis=1),
        (((1,), (1,)), ((), ())),
        preferred_element_type=F32,
    )
    force = force[:rows] + force[rows : 2 * rows] + force[2 * rows :]
    out[2] = out[2] - force / diag_k


def shards(
    disp, stiff, spin, load, foot_node, foot_dest, foot_slot, foot_count, road, active, influence
):
    circs, lats = lax.axis_size("circ"), lax.axis_size("lat")
    owners = circs * lats
    size = road.shape[0]
    rows, cols = disp.shape[1:]
    assert rows == cols == LANES and size == 4 * LANES and circs > 2 and owners % 16 == 0
    anywhere = pl.BlockSpec(memory_space=pl.ANY)
    block = pl.BlockSpec(memory_space=pltpu.VMEM)
    params = pltpu.CompilerParams(vmem_limit_bytes=32 * 1024 * 1024)
    lists = [x.reshape(-1, LANES) for x in (foot_node, foot_dest, foot_slot)]
    listed = jax.ShapeDtypeStruct(lists[0].shape, I32)
    strip = (4, LANES)
    send, trial, near, nodes, owner, slots, roads, actives, blocks = pl.pallas_call(
        functools.partial(pack_kernel, (circs, lats)),
        in_specs=[anywhere] * 11,
        out_specs=[block] * 9,
        out_shape=[
            jax.ShapeDtypeStruct((owners, 3, 4, LANES), F32),
            jax.ShapeDtypeStruct((3, rows, cols), F32),
            jax.ShapeDtypeStruct((3, rows, cols), F32),
            listed,
            listed,
            listed,
            jax.ShapeDtypeStruct(strip, F32),
            jax.ShapeDtypeStruct(strip, I32),
            jax.ShapeDtypeStruct((size, size), F32),
        ],
        scratch_shapes=[
            pltpu.VMEM((3, rows, cols), F32),
            pltpu.VMEM((2, rows, cols), F32),
            pltpu.VMEM((3, rows, cols), F32),
            pltpu.VMEM(lists[0].shape, I32),
            pltpu.SMEM((1,), I32),
            pltpu.SMEM((1,), F32),
            pltpu.SemaphoreType.DMA((11,)),
        ],
        compiler_params=params,
        name="pack_rows",
    )(
        disp, stiff, load, *lists, foot_count, spin,
        road.reshape(strip), active.reshape(strip), influence[0],
    )
    got = lax.all_to_all(send, ("circ", "lat"), split_axis=0, concat_axis=0, tiled=True)
    reply, pressure = pl.pallas_call(
        functools.partial(solve_kernel, lats),
        in_specs=[block] * 4,
        out_specs=[block, block],
        out_shape=[
            jax.ShapeDtypeStruct((owners,) + strip, F32),
            jax.ShapeDtypeStruct(strip, F32),
        ],
        scratch_shapes=[
            pltpu.VMEM((size, size + LANES), F32),
            pltpu.VMEM((1, size), F32),
            pltpu.VMEM((16, 16, LANES), F32),
            pltpu.VMEM((4, owners, LANES), F32),
        ],
        compiler_params=params,
        name="solve_patch",
    )(got, roads, actives, blocks)
    back = lax.all_to_all(reply, ("circ", "lat"), split_axis=0, concat_axis=0, tiled=True)
    new_disp = pl.pallas_call(
        functools.partial(finish_kernel, (circs, lats)),
        in_specs=[block] * 7,
        out_specs=block,
        out_shape=jax.ShapeDtypeStruct(disp.shape, F32),
        compiler_params=params,
        name="finish_nodes",
    )(trial, near, nodes, owner, slots, got, back)
    return (new_disp, pressure.reshape(size))


def solution(mesh):
    return jax.shard_map(
        shards,
        mesh=mesh,
        in_specs=(
            P(None, ("cases", "circ"), "lat"),
            P(None, ("cases", "circ"), "lat"),
            P("cases"),
            P(None, ("cases", "circ"), "lat"),
            P(("cases", "circ", "lat")),
            P(("cases", "circ", "lat")),
            P(("cases", "circ", "lat")),
            P(("cases", "circ", "lat")),
            P(("cases", "circ", "lat")),
            P(("cases", "circ", "lat")),
            P(("cases", "circ", "lat"), None, None),
        ),
        out_specs=(P(None, ("cases", "circ"), "lat"), P(("cases", "circ", "lat"))),
        check_vma=False,
    )
```

```python
import functools

import jax
import jax.numpy as jnp
from jax import lax
from jax.experimental import pallas as pl
from jax.experimental.pallas import tpu as pltpu
from jax.sharding import PartitionSpec as P

F32 = jnp.float32
BF16 = jnp.bfloat16
I32 = jnp.int32
LANES = 128
CG_STEPS = 40
CG_STOP = 1e-13
TRUE_STOP = 1e-12


def log2(value):
    assert value > 0 and value & (value - 1) == 0
    return value.bit_length() - 1


def thirds(x):
    high = x.astype(BF16).astype(F32)
    rest = x - high
    mid = rest.astype(BF16).astype(F32)
    return high, mid, rest - mid


def iota(shape, axis):
    return lax.broadcasted_iota(I32, shape, axis)


def wide(ref, first, count):
    return jnp.concatenate([ref[i : i + 1, :] for i in range(first, first + count)], axis=1)


def shifted(u):
    rows, cols = u.shape
    row, col = iota(u.shape, 0), iota(u.shape, 1)
    return (
        jnp.where(row == rows - 1, 0.0, pltpu.roll(u, rows - 1, 0)),
        jnp.where(row == 0, 0.0, pltpu.roll(u, 1, 0)),
        jnp.where(col == cols - 1, 0.0, pltpu.roll(u, cols - 1, 1)),
        jnp.where(col == 0, 0.0, pltpu.roll(u, 1, 1)),
    )


def edges(u):
    rows, cols = u.shape
    turned = u.T
    return [u[0:1, :], u[rows - 1 : rows, :], turned[0:1, :], turned[cols - 1 : cols, :]]


def pack_kernel(
    axes, count, spin, node, dest, slot, stiff, disp, load, road, active, block,
    send, trial, near, nodes, owner, slots, roads, actives, blocks,
    u, springs, loads, dests, sems,
):
    circs, lats = axes
    owners = send.shape[0]
    rows, cols = disp.shape[1:]
    chunks = node.shape[0]
    pairs = [
        (node, nodes), (dest, dests), (slot, slots), (stiff, springs), (disp, u), (load, loads), (road, roads), (active, actives),
        (block, blocks),
    ]
    copies = [pltpu.make_async_copy(a, b, sems.at[i]) for i, (a, b) in enumerate(pairs)]
    for copy in copies:
        copy.start()
    for copy in copies[:3]:
        copy.wait()

    width = 2 * LANES if chunks % 2 == 0 else LANES
    step = width // LANES
    to, tos = [], []
    for i in range(chunks):
        live = iota((1, LANES), 1) + i * LANES < count[0]
        target = jnp.where(live, dests[i : i + 1, :], -1)
        owner[i : i + 1, :] = target
        to.append(iota((owners, LANES), 0) == target)
        tos.append(to[i].astype(F32).astype(BF16))
    before = iota((LANES, 2 * LANES), 0) < iota((LANES, 2 * LANES), 1)
    ranks = jnp.dot(
        jnp.concatenate(tos, axis=0), before.astype(F32).astype(BF16), preferred_element_type=F32
    )
    passed = jnp.zeros((owners, LANES), F32)
    right = []
    for i in range(chunks):
        mine = ranks[i * owners : (i + 1) * owners]
        rank = jnp.sum(
            jnp.where(to[i], mine[:, :LANES] + passed, 0.0), axis=0, keepdims=True
        ).astype(I32)
        passed = passed + mine[:, LANES:]
        right.append((iota((LANES, LANES), 0) == rank).astype(F32).astype(BF16))

    for copy in copies[3:6]:
        copy.wait()
    kc = springs[0] - spin[0]
    kl = springs[1]
    diag_k = 2.0 * kc + 2.0 * kl + 0.5
    near[0] = kc
    near[1] = kl
    near[2] = diag_k
    for c in range(3):
        own = u[c]
        u_next, u_prev, u_right, u_left = shifted(own)
        force = kc * (2.0 * own - u_next - u_prev) + kl * (2.0 * own - u_right - u_left) + 0.5 * own
        trial[c] = own + (loads[c] - force) / diag_k
    table = jnp.concatenate(
        [jnp.concatenate(thirds(x), axis=1) for x in (trial[2], kc, kl)], axis=0
    ).astype(BF16)
    left = []
    for first in range(0, chunks, step):
        place = wide(nodes, first, step)
        circ = place >> log2(cols)
        lat = place & (cols - 1)
        one_lat = (iota((cols, width), 0) == lat).astype(F32).astype(BF16)
        picked = jnp.dot(
            table, jnp.concatenate([one_lat] * 3, axis=0), preferred_element_type=F32
        )
        one_circ = iota((rows, width), 0) == circ
        pieces = []
        for k in range(3):
            found = picked[k * rows : (k + 1) * rows]
            pieces += thirds(jnp.sum(jnp.where(one_circ, found, 0.0), axis=0, keepdims=True))
        where = wide(slots, first, step)
        low = where & (LANES - 1)
        pieces += [x.astype(F32) for x in (circ * cols, lat, where - low, low)]
        here = jnp.concatenate(to[first : first + step], axis=1)
        left.append(
            jnp.concatenate([jnp.where(here, x, 0.0) for x in pieces], axis=0).astype(BF16)
        )
    spread = lax.dot_general(
        jnp.concatenate(left, axis=1),
        jnp.concatenate(right, axis=1),
        (((1,), (1,)), ((), ())),
        preferred_element_type=F32,
    )
    part = [spread[i * owners : (i + 1) * owners] for i in range(13)]
    for v in range(3):
        send[:, 0, v, :] = part[3 * v] + part[3 * v + 1] + part[3 * v + 2]
    send[:, 0, 3, :] = part[9] + part[10]
    send[:, 2, 0, :] = part[11] + part[12]

    my_circ, my_lat = lax.axis_index("circ"), lax.axis_index("lat")
    me = my_circ * lats + my_lat
    after = jnp.where(my_circ == circs - 1, my_lat, me + lats)
    prior = jnp.where(my_circ == 0, (circs - 1) * lats + my_lat, me - lats)
    east = jnp.where(my_lat < lats - 1, me + 1, -1)
    west = jnp.where(my_lat > 0, me - 1, -1)
    device = iota((owners, LANES), 0)
    for c in range(3):
        layers = edges(u[c])
        lacks = jnp.zeros((owners, LANES), F32)
        for layer, reader in zip(layers, (prior, after, west, east)):
            lacks = jnp.where(device == reader, layer, lacks)
        send[:, 2, 1 + c, :] = lacks
        if c == 2:
            for t, layer in enumerate(layers):
                send[:, 1, t, :] = jnp.broadcast_to(layer, (owners, LANES))
    for copy in copies[6:]:
        copy.wait()


def column(row):
    return jnp.broadcast_to(row, (LANES, row.shape[1])).T


def patch_system(lats, got, road, active, rowed, layered):
    owners = got.shape[0]
    rows = cols = LANES
    size = 4 * LANES
    group = 16
    total = jnp.zeros((4 * group, LANES), F32)
    for first in range(0, owners, group):
        some = slice(first, first + group)
        w, kc, kl, node = [got[some, 0, v, :] for v in range(4)]
        slot = got[some, 2, 0, :].astype(I32)
        node = node.astype(I32)
        lat = node & (cols - 1)
        sender = jnp.where(kc > 0.0, iota(kc.shape, 0) + first, 0)
        pieces = thirds(w) + thirds(kc) + thirds(kl)
        pieces += tuple(x.astype(F32) for x in (node - lat, lat, sender))
        for p, piece in enumerate(pieces):
            rowed[p] = piece
        rowed[12] = (slot >> log2(LANES)).astype(F32)
        rowed[13] = (slot & (LANES - 1)).astype(F32)
        rowed[14:16] = jnp.zeros((2,) + kc.shape, F32)
        left, right = [], []
        for d in range(group):
            stack = rowed[:, d, :]
            high, low = stack[12:13, :], stack[13:14, :]
            left.append(
                jnp.concatenate(
                    [jnp.where(high == float(h), stack, 0.0) for h in range(4)], axis=0
                ).astype(BF16)
            )
            right.append(
                (iota((LANES, LANES), 0) == low.astype(I32)).astype(F32).astype(BF16)
            )
        total = total + lax.dot_general(
            jnp.concatenate(left, axis=1),
            jnp.concatenate(right, axis=1),
            (((1,), (1,)), ((), ())),
            preferred_element_type=F32,
        )
    values = []
    for at in ((0, 1, 2), (3, 4, 5), (6, 7, 8), (9, 10), (10,), (11,)):
        strips = []
        for h in range(4):
            strip = total[group * h + at[0] : group * h + at[0] + 1, :]
            for p in at[1:]:
                strip = strip + total[group * h + p : group * h + p + 1, :]
            strips.append(strip)
        values.append(jnp.concatenate(strips, axis=1))
    w, kc, kl = values[:3]
    node, lat, sender = [x.astype(I32) for x in values[3:]]
    circ = node >> log2(cols)
    after = sender + lats
    after = jnp.where(after >= owners, after - owners, after)
    before = sender - lats
    before = jnp.where(before < 0, before + owners, before)
    side = sender & (lats - 1)
    from_circ = jnp.where(
        circ == rows - 1, after, jnp.where(circ == 0, before + owners, -1)
    )
    from_lat = jnp.where(
        (lat == cols - 1) & (side < lats - 1),
        sender + 1 + 2 * owners,
        jnp.where((lat == 0) & (side > 0), sender - 1 + 3 * owners, -1),
    )
    for t in range(4):
        layered[t] = got[:, 1, t, :]
    layers = layered[...].reshape(owners * 4, LANES)
    layers = jnp.concatenate(thirds(layers), axis=1).astype(BF16)

    def pick(high, low):
        one = (iota((LANES, size), 0) == low).astype(F32).astype(BF16)
        found = jnp.dot(layers, jnp.concatenate([one] * 3, axis=0), preferred_element_type=F32)
        return jnp.sum(
            jnp.where(iota((owners * 4, size), 0) == high, found, 0.0), axis=0, keepdims=True
        )

    diag_k = 2.0 * kc + 2.0 * kl + 0.5
    w = w + (kc * pick(from_circ, lat) + kl * pick(from_lat, circ)) / diag_k
    mask = wide(active, 0, 4).astype(F32)
    return mask, mask * (w - wide(road, 0, 4)), 1.0 / diag_k


def factor_solve(block, mask, rhs, soft, work, press):
    size = rhs.shape[1]
    row = iota((size, 1), 0)
    lane = iota((1, LANES), 1)
    down = column(mask)
    for t in range(size // LANES):
        part = slice(t * LANES, (t + 1) * LANES)
        on = row == lane + t * LANES
        live = mask[:, part]
        work[:, part] = down * live * (block[:, part] + jnp.where(on, soft[:, part], 0.0)) + (
            jnp.where(on, 1.0 - live, 0.0)
        )
    work[:, size:] = column(rhs)
    place = iota((1, size), 1)

    def eliminate(j, carry):
        pivot_row = work[pl.ds(j, 1), :]
        pivot = jnp.sum(jnp.where(place == j, pivot_row[:, :size], 0.0), axis=1, keepdims=True)
        start = pl.multiple_of((j >> log2(LANES)) << log2(LANES), LANES)
        tile = work[:, pl.ds(start, LANES)]
        below = jnp.sum(jnp.where(lane == j - start, tile, 0.0), axis=1, keepdims=True)
        ratio = jnp.where(row > j, below / pivot, 0.0)
        work[...] = work[...] - ratio * pivot_row
        return carry

    lax.fori_loop(0, size, eliminate, 0)

    def substitute(step, x):
        j = size - 1 - step
        now = work[pl.ds(j, 1), :]
        upper = now[:, :size]
        pivot = jnp.sum(jnp.where(place == j, upper, 0.0), axis=1, keepdims=True)
        known = jnp.sum(upper * x, axis=1, keepdims=True)
        return jnp.where(place == j, (now[:, size : size + 1] - known) / pivot, x)

    press[...] = lax.fori_loop(0, size, substitute, jnp.zeros((1, size), F32))


def over(top, bottom):
    return jnp.where(bottom > 0.0, top / bottom, 0.0)


def dot(a, b):
    return jnp.sum(a * b, axis=1, keepdims=True)


def times(block, u, mask, soft):
    down = column(u)
    parts = [
        jnp.sum(block[:, first : first + LANES] * down, axis=0, keepdims=True)
        for first in range(0, u.shape[1], LANES)
    ]
    return mask * (jnp.concatenate(parts, axis=1) + soft * u)


def solve_kernel(
    lats, got, road, active, block, send, pressure, work, press, rowed, layered
):
    size = 4 * LANES
    mask, rhs, soft = patch_system(lats, got, road, active, rowed, layered)
    square = iota((LANES, LANES), 0) == iota((LANES, LANES), 1)
    diagonal = jnp.concatenate(
        [
            jnp.sum(
                jnp.where(square, block[i : i + LANES, i : i + LANES], 0.0), axis=0, keepdims=True
            )
            for i in range(0, size, LANES)
        ],
        axis=1,
    )
    scale = mask / (diagonal + soft)
    start = dot(rhs, scale * rhs)

    def advance(x, r, p, s, norm, alpha):
        u = scale * r
        w = times(block, u, mask, soft)
        now = dot(r, u)
        beta = over(now, norm)
        alpha = over(now, dot(w, u) - over(beta * now, alpha))
        p = u + beta * p
        s = w + beta * s
        return x + alpha * p, r - alpha * s, p, s, now, alpha

    def going(state):
        step, norm = state[0], state[5]
        return (step < CG_STEPS) & (norm[0, 0] > CG_STOP * start[0, 0])

    def body(state):
        return (state[0] + 2,) + advance(*advance(*state[1:]))

    zero = jnp.zeros((1, size), F32)
    none = jnp.zeros((1, 1), F32)
    x = lax.while_loop(going, body, (0, zero, rhs, zero, zero, start, none))[1]
    gap = rhs - times(block, x, mask, soft)
    press[...] = x

    @pl.when(jnp.logical_not(dot(gap, scale * gap)[0, 0] <= TRUE_STOP * start[0, 0]))
    def _():
        factor_solve(block, mask, rhs, soft, work, press)

    answer = press[...]
    for j in range(4):
        part = answer[:, j * LANES : (j + 1) * LANES]
        pressure[j : j + 1, :] = part
        send[:, j, :] = jnp.broadcast_to(part, (send.shape[0], LANES))


def finish_kernel(axes, trial, near, node, owner, slot, got, back, out):
    circs, lats = axes
    owners = got.shape[0]
    rows, cols = trial.shape[1:]
    chunks = node.shape[0]
    my_circ, my_lat = lax.axis_index("circ"), lax.axis_index("lat")
    me = my_circ * lats + my_lat
    after = jnp.where(my_circ == circs - 1, my_lat, me + lats)
    before = jnp.where(my_circ == 0, (circs - 1) * lats + my_lat, me - lats)
    right_dev = jnp.minimum(me + 1, owners - 1)
    left_dev = jnp.maximum(me - 1, 0)
    kc, kl, diag_k = near[0], near[1], near[2]
    row, col = iota((rows, cols), 0), iota((rows, cols), 1)
    for c in range(3):
        down, up = got[after, 2, 1 + c : 2 + c, :], got[before, 2, 1 + c : 2 + c, :]
        east, west = got[right_dev, 2, 1 + c : 2 + c, :], got[left_dev, 2, 1 + c : 2 + c, :]
        east = jnp.where(my_lat < lats - 1, east, 0.0)
        west = jnp.where(my_lat > 0, west, 0.0)
        circ_in = jnp.where(row == rows - 1, down, jnp.where(row == 0, up, 0.0))
        lat_in = jnp.where(
            col == cols - 1, column(east), jnp.where(col == 0, column(west), 0.0)
        )
        out[c] = trial[c] + (kc * circ_in + kl * lat_in) / diag_k

    answers = jnp.concatenate([back[:, j, :] for j in range(4)], axis=0)
    answers = jnp.concatenate(thirds(answers), axis=1).astype(BF16)
    step = 2 if chunks % 2 == 0 else 1
    span = step * LANES
    left, right = [], []
    for first in range(0, chunks, step):
        nodes = wide(node, first, step)
        where = wide(slot, first, step)
        device = wide(owner, first, step)
        low = where & (LANES - 1)
        source = jnp.where(device < 0, -1, (where >> log2(LANES)) * owners + device)
        one_low = (iota((LANES, span), 0) == low).astype(F32).astype(BF16)
        found = jnp.dot(
            answers, jnp.concatenate([one_low] * 3, axis=0), preferred_element_type=F32
        )
        push = jnp.sum(
            jnp.where(iota((4 * owners, span), 0) == source, found, 0.0), axis=0, keepdims=True
        )
        one_circ = iota((rows, span), 0) == nodes >> log2(cols)
        left.append(
            jnp.concatenate(
                [jnp.where(one_circ, x, 0.0) for x in thirds(push)], axis=0
            ).astype(BF16)
        )
        right.append((iota((cols, span), 0) == (nodes & (cols - 1))).astype(F32).astype(BF16))
    force = lax.dot_general(
        jnp.concatenate(left, axis=1),
        jnp.concatenate(right, axis=1),
        (((1,), (1,)), ((), ())),
        preferred_element_type=F32,
    )
    force = force[:rows] + force[rows : 2 * rows] + force[2 * rows :]
    out[2] = out[2] - force / diag_k


def shards(
    disp, stiff, spin, load, foot_node, foot_dest, foot_slot, foot_count, road, active, influence
):
    circs, lats = lax.axis_size("circ"), lax.axis_size("lat")
    owners = circs * lats
    size = road.shape[0]
    rows, cols = disp.shape[1:]
    assert rows == cols == LANES and size == 4 * LANES and circs > 2 and owners % 16 == 0
    anywhere = pl.BlockSpec(memory_space=pltpu.HBM)
    block = pl.BlockSpec(memory_space=pltpu.VMEM)
    params = pltpu.CompilerParams(vmem_limit_bytes=32 * 1024 * 1024)
    lists = [x.reshape(-1, LANES) for x in (foot_node, foot_dest, foot_slot)]
    listed = jax.ShapeDtypeStruct(lists[0].shape, I32)
    strip = (4, LANES)
    send, trial, near, nodes, owner, slots, roads, actives, blocks = pl.pallas_call(
        functools.partial(pack_kernel, (circs, lats)),
        in_specs=[pl.BlockSpec(memory_space=pltpu.SMEM)] * 2 + [anywhere] * 9,
        out_specs=[block] * 9,
        out_shape=[
            jax.ShapeDtypeStruct((owners, 3, 4, LANES), F32),
            jax.ShapeDtypeStruct((3, rows, cols), F32),
            jax.ShapeDtypeStruct((3, rows, cols), F32),
            listed,
            listed,
            listed,
            jax.ShapeDtypeStruct(strip, F32),
            jax.ShapeDtypeStruct(strip, I32),
            jax.ShapeDtypeStruct((size, size), F32),
        ],
        scratch_shapes=[
            pltpu.VMEM((3, rows, cols), F32),
            pltpu.VMEM((2, rows, cols), F32),
            pltpu.VMEM((3, rows, cols), F32),
            pltpu.VMEM(lists[0].shape, I32),
            pltpu.SemaphoreType.DMA((9,)),
        ],
        compiler_params=params,
        name="pack_rows",
    )(
        foot_count, spin,
        *[
            pltpu.with_memory_space_constraint(x, pltpu.HBM)
            for x in (
                *lists, stiff, disp, load, road.reshape(strip), active.reshape(strip), influence[0]
            )
        ]
    )
    got = lax.all_to_all(send, ("circ", "lat"), split_axis=0, concat_axis=0, tiled=True)
    reply, pressure = pl.pallas_call(
        functools.partial(solve_kernel, lats),
        in_specs=[block] * 4,
        out_specs=[block, block],
        out_shape=[
            jax.ShapeDtypeStruct((owners,) + strip, F32),
            jax.ShapeDtypeStruct(strip, F32),
        ],
        scratch_shapes=[
            pltpu.VMEM((size, size + LANES), F32),
            pltpu.VMEM((1, size), F32),
            pltpu.VMEM((16, 16, LANES), F32),
            pltpu.VMEM((4, owners, LANES), F32),
        ],
        compiler_params=params,
        name="solve_patch",
    )(got, roads, actives, blocks)
    back = lax.all_to_all(reply, ("circ", "lat"), split_axis=0, concat_axis=0, tiled=True)
    new_disp = pl.pallas_call(
        functools.partial(finish_kernel, (circs, lats)),
        in_specs=[block] * 7,
        out_specs=block,
        out_shape=jax.ShapeDtypeStruct(disp.shape, F32),
        compiler_params=params,
        name="finish_nodes",
    )(trial, near, nodes, owner, slots, got, back)
    return (new_disp, pressure.reshape(size))


def solution(mesh):
    return jax.shard_map(
        shards,
        mesh=mesh,
        in_specs=(
            P(None, ("cases", "circ"), "lat"),
            P(None, ("cases", "circ"), "lat"),
            P("cases"),
            P(None, ("cases", "circ"), "lat"),
            P(("cases", "circ", "lat")),
            P(("cases", "circ", "lat")),
            P(("cases", "circ", "lat")),
            P(("cases", "circ", "lat")),
            P(("cases", "circ", "lat")),
            P(("cases", "circ", "lat")),
            P(("cases", "circ", "lat"), None, None),
        ),
        out_specs=(P(None, ("cases", "circ"), "lat"), P(("cases", "circ", "lat"))),
        check_vma=False,
    )
```

```python
import functools

import jax
import jax.numpy as jnp
from jax import lax
from jax.experimental import pallas as pl
from jax.experimental.pallas import tpu as pltpu
from jax.sharding import PartitionSpec as P

F32 = jnp.float32
BF16 = jnp.bfloat16
I32 = jnp.int32
LANES = 128
CG_FIRST = 3
CG_AGAIN = 4
CG_STEPS = 40
CG_STOP = 1e-13
TRUE_STOP = 1e-12


def log2(value):
    assert value > 0 and value & (value - 1) == 0
    return value.bit_length() - 1


def thirds(x):
    high = x.astype(BF16).astype(F32)
    rest = x - high
    mid = rest.astype(BF16).astype(F32)
    return high, mid, rest - mid


def iota(shape, axis):
    return lax.broadcasted_iota(I32, shape, axis)


def wide(ref, first, count):
    return jnp.concatenate([ref[i : i + 1, :] for i in range(first, first + count)], axis=1)


def shifted(u):
    rows, cols = u.shape
    row, col = iota(u.shape, 0), iota(u.shape, 1)
    return (
        jnp.where(row == rows - 1, 0.0, pltpu.roll(u, rows - 1, 0)),
        jnp.where(row == 0, 0.0, pltpu.roll(u, 1, 0)),
        jnp.where(col == cols - 1, 0.0, pltpu.roll(u, cols - 1, 1)),
        jnp.where(col == 0, 0.0, pltpu.roll(u, 1, 1)),
    )


def edges(u):
    rows, cols = u.shape
    turned = u.T
    return [u[0:1, :], u[rows - 1 : rows, :], turned[0:1, :], turned[cols - 1 : cols, :]]


def pack_kernel(
    axes, count, spin, node, dest, slot, stiff, disp, load, road, active, block,
    send, trial, near, nodes, owner, slots, roads, actives, blocks,
    u, springs, loads, dests, sems,
):
    circs, lats = axes
    owners = send.shape[0]
    rows, cols = disp.shape[1:]
    chunks = node.shape[0]
    pairs = [
        (node, nodes), (dest, dests), (slot, slots), (stiff, springs), (disp, u), (load, loads), (road, roads), (active, actives),
        (block, blocks),
    ]
    copies = [pltpu.make_async_copy(a, b, sems.at[i]) for i, (a, b) in enumerate(pairs)]
    for copy in copies:
        copy.start()
    for copy in copies[:3]:
        copy.wait()

    width = 2 * LANES if chunks % 2 == 0 else LANES
    step = width // LANES
    to, tos = [], []
    for i in range(chunks):
        live = iota((1, LANES), 1) + i * LANES < count[0]
        target = jnp.where(live, dests[i : i + 1, :], -1)
        owner[i : i + 1, :] = target
        to.append(iota((owners, LANES), 0) == target)
        tos.append(to[i].astype(F32).astype(BF16))
    before = iota((LANES, 2 * LANES), 0) < iota((LANES, 2 * LANES), 1)
    ranks = jnp.dot(
        jnp.concatenate(tos, axis=0), before.astype(F32).astype(BF16), preferred_element_type=F32
    )
    passed = jnp.zeros((owners, LANES), F32)
    right = []
    for i in range(chunks):
        mine = ranks[i * owners : (i + 1) * owners]
        rank = jnp.sum(
            jnp.where(to[i], mine[:, :LANES] + passed, 0.0), axis=0, keepdims=True
        ).astype(I32)
        passed = passed + mine[:, LANES:]
        right.append((iota((LANES, LANES), 0) == rank).astype(F32).astype(BF16))

    for copy in copies[3:6]:
        copy.wait()
    kc = springs[0] - spin[0]
    kl = springs[1]
    diag_k = 2.0 * kc + 2.0 * kl + 0.5
    near[0] = kc
    near[1] = kl
    near[2] = diag_k
    for c in range(3):
        own = u[c]
        u_next, u_prev, u_right, u_left = shifted(own)
        force = kc * (2.0 * own - u_next - u_prev) + kl * (2.0 * own - u_right - u_left) + 0.5 * own
        trial[c] = own + (loads[c] - force) / diag_k
    table = jnp.concatenate(
        [jnp.concatenate(thirds(x), axis=1) for x in (trial[2], kc, kl)], axis=0
    ).astype(BF16)
    left = []
    for first in range(0, chunks, step):
        place = wide(nodes, first, step)
        circ = place >> log2(cols)
        lat = place & (cols - 1)
        one_lat = (iota((cols, width), 0) == lat).astype(F32).astype(BF16)
        picked = jnp.dot(
            table, jnp.concatenate([one_lat] * 3, axis=0), preferred_element_type=F32
        )
        one_circ = iota((rows, width), 0) == circ
        pieces = []
        for k in range(3):
            found = picked[k * rows : (k + 1) * rows]
            pieces += thirds(jnp.sum(jnp.where(one_circ, found, 0.0), axis=0, keepdims=True))
        where = wide(slots, first, step)
        low = where & (LANES - 1)
        pieces += [x.astype(F32) for x in (circ * cols, lat, where - low, low)]
        here = jnp.concatenate(to[first : first + step], axis=1)
        left.append(
            jnp.concatenate([jnp.where(here, x, 0.0) for x in pieces], axis=0).astype(BF16)
        )
    spread = lax.dot_general(
        jnp.concatenate(left, axis=1),
        jnp.concatenate(right, axis=1),
        (((1,), (1,)), ((), ())),
        preferred_element_type=F32,
    )
    part = [spread[i * owners : (i + 1) * owners] for i in range(13)]
    for v in range(3):
        send[:, 0, v, :] = part[3 * v] + part[3 * v + 1] + part[3 * v + 2]
    send[:, 0, 3, :] = part[9] + part[10]
    send[:, 2, 0, :] = part[11] + part[12]

    my_circ, my_lat = lax.axis_index("circ"), lax.axis_index("lat")
    me = my_circ * lats + my_lat
    after = jnp.where(my_circ == circs - 1, my_lat, me + lats)
    prior = jnp.where(my_circ == 0, (circs - 1) * lats + my_lat, me - lats)
    east = jnp.where(my_lat < lats - 1, me + 1, -1)
    west = jnp.where(my_lat > 0, me - 1, -1)
    device = iota((owners, LANES), 0)
    for c in range(3):
        layers = edges(u[c])
        lacks = jnp.zeros((owners, LANES), F32)
        for layer, reader in zip(layers, (prior, after, west, east)):
            lacks = jnp.where(device == reader, layer, lacks)
        send[:, 2, 1 + c, :] = lacks
        if c == 2:
            for t, layer in enumerate(layers):
                send[:, 1, t, :] = jnp.broadcast_to(layer, (owners, LANES))
    for copy in copies[6:]:
        copy.wait()


def column(row):
    return jnp.broadcast_to(row, (LANES, row.shape[1])).T


def patch_system(lats, got, road, active, rowed, layered):
    owners = got.shape[0]
    rows = cols = LANES
    size = 4 * LANES
    group = 16
    total = jnp.zeros((4 * group, LANES), F32)
    for first in range(0, owners, group):
        some = slice(first, first + group)
        w, kc, kl, node = [got[some, 0, v, :] for v in range(4)]
        slot = got[some, 2, 0, :].astype(I32)
        node = node.astype(I32)
        lat = node & (cols - 1)
        sender = jnp.where(kc > 0.0, iota(kc.shape, 0) + first, 0)
        pieces = thirds(w) + thirds(kc) + thirds(kl)
        pieces += tuple(x.astype(F32) for x in (node - lat, lat, sender))
        for p, piece in enumerate(pieces):
            rowed[p] = piece
        rowed[12] = (slot >> log2(LANES)).astype(F32)
        rowed[13] = (slot & (LANES - 1)).astype(F32)
        rowed[14:16] = jnp.zeros((2,) + kc.shape, F32)
        left, right = [], []
        for d in range(group):
            stack = rowed[:, d, :]
            high, low = stack[12:13, :], stack[13:14, :]
            left.append(
                jnp.concatenate(
                    [jnp.where(high == float(h), stack, 0.0) for h in range(4)], axis=0
                ).astype(BF16)
            )
            right.append(
                (iota((LANES, LANES), 0) == low.astype(I32)).astype(F32).astype(BF16)
            )
        total = total + lax.dot_general(
            jnp.concatenate(left, axis=1),
            jnp.concatenate(right, axis=1),
            (((1,), (1,)), ((), ())),
            preferred_element_type=F32,
        )
    values = []
    for at in ((0, 1, 2), (3, 4, 5), (6, 7, 8), (9, 10), (10,), (11,)):
        strips = []
        for h in range(4):
            strip = total[group * h + at[0] : group * h + at[0] + 1, :]
            for p in at[1:]:
                strip = strip + total[group * h + p : group * h + p + 1, :]
            strips.append(strip)
        values.append(jnp.concatenate(strips, axis=1))
    w, kc, kl = values[:3]
    node, lat, sender = [x.astype(I32) for x in values[3:]]
    circ = node >> log2(cols)
    after = sender + lats
    after = jnp.where(after >= owners, after - owners, after)
    before = sender - lats
    before = jnp.where(before < 0, before + owners, before)
    side = sender & (lats - 1)
    from_circ = jnp.where(
        circ == rows - 1, after, jnp.where(circ == 0, before + owners, -1)
    )
    from_lat = jnp.where(
        (lat == cols - 1) & (side < lats - 1),
        sender + 1 + 2 * owners,
        jnp.where((lat == 0) & (side > 0), sender - 1 + 3 * owners, -1),
    )
    for t in range(4):
        layered[t] = got[:, 1, t, :]
    layers = layered[...].reshape(owners * 4, LANES)
    layers = jnp.concatenate(thirds(layers), axis=1).astype(BF16)

    def pick(high, low):
        one = (iota((LANES, size), 0) == low).astype(F32).astype(BF16)
        found = jnp.dot(layers, jnp.concatenate([one] * 3, axis=0), preferred_element_type=F32)
        return jnp.sum(
            jnp.where(iota((owners * 4, size), 0) == high, found, 0.0), axis=0, keepdims=True
        )

    diag_k = 2.0 * kc + 2.0 * kl + 0.5
    w = w + (kc * pick(from_circ, lat) + kl * pick(from_lat, circ)) / diag_k
    mask = wide(active, 0, 4).astype(F32)
    return mask, mask * (w - wide(road, 0, 4)), 1.0 / diag_k


def factor_solve(block, mask, rhs, soft, work, press):
    size = rhs.shape[1]
    row = iota((size, 1), 0)
    lane = iota((1, LANES), 1)
    down = column(mask)
    for t in range(size // LANES):
        part = slice(t * LANES, (t + 1) * LANES)
        on = row == lane + t * LANES
        live = mask[:, part]
        work[:, part] = down * live * (block[:, part] + jnp.where(on, soft[:, part], 0.0)) + (
            jnp.where(on, 1.0 - live, 0.0)
        )
    work[:, size:] = column(rhs)
    place = iota((1, size), 1)

    def eliminate(j, carry):
        pivot_row = work[pl.ds(j, 1), :]
        pivot = jnp.sum(jnp.where(place == j, pivot_row[:, :size], 0.0), axis=1, keepdims=True)
        start = pl.multiple_of((j >> log2(LANES)) << log2(LANES), LANES)
        tile = work[:, pl.ds(start, LANES)]
        below = jnp.sum(jnp.where(lane == j - start, tile, 0.0), axis=1, keepdims=True)
        ratio = jnp.where(row > j, below / pivot, 0.0)
        work[...] = work[...] - ratio * pivot_row
        return carry

    lax.fori_loop(0, size, eliminate, 0)

    def substitute(step, x):
        j = size - 1 - step
        now = work[pl.ds(j, 1), :]
        upper = now[:, :size]
        pivot = jnp.sum(jnp.where(place == j, upper, 0.0), axis=1, keepdims=True)
        known = jnp.sum(upper * x, axis=1, keepdims=True)
        return jnp.where(place == j, (now[:, size : size + 1] - known) / pivot, x)

    press[...] = lax.fori_loop(0, size, substitute, jnp.zeros((1, size), F32))


def over(top, bottom):
    return jnp.where(bottom > 0.0, top / bottom, 0.0)


def dot(a, b):
    return jnp.sum(a * b, axis=1, keepdims=True)


def times(block, u, mask, soft):
    size = u.shape[1]
    parts = [jnp.zeros((8, LANES), F32)] * (size // LANES)
    for i in range(0, size, LANES):
        down = column(u[:, i : i + LANES])
        for k in range(size // LANES):
            tile = block[i : i + LANES, k * LANES : (k + 1) * LANES] * down
            parts[k] = parts[k] + jnp.sum(tile.reshape(LANES // 8, 8, LANES), axis=0)
    parts = [jnp.sum(part, axis=0, keepdims=True) for part in parts]
    return mask * (jnp.concatenate(parts, axis=1) + soft * u)


def solve_kernel(
    lats, got, road, active, block, send, pressure, work, press, rowed, layered
):
    size = 4 * LANES
    mask, rhs, soft = patch_system(lats, got, road, active, rowed, layered)
    square = iota((LANES, LANES), 0) == iota((LANES, LANES), 1)
    diagonal = jnp.concatenate(
        [
            jnp.sum(
                jnp.where(square, block[i : i + LANES, i : i + LANES], 0.0), axis=0, keepdims=True
            )
            for i in range(0, size, LANES)
        ],
        axis=1,
    )
    scale = mask / (diagonal + soft)
    start = dot(rhs, scale * rhs)
    zero = jnp.zeros((1, size), F32)
    none = jnp.zeros((1, 1), F32)

    def begin(x, r):
        u = scale * r
        return x, r, u, times(block, u, mask, soft), zero, zero, zero, zero, none, none

    def advance(x, r, u, w, z, q, s, p, norm, alpha):
        m = scale * w
        n = times(block, m, mask, soft)
        now = dot(r, u)
        beta = over(now, norm)
        alpha = over(now, dot(w, u) - over(beta * now, alpha))
        z = n + beta * z
        q = m + beta * q
        s = w + beta * s
        p = u + beta * p
        x, r, u, w = x + alpha * p, r - alpha * s, u - alpha * q, w - alpha * z
        return x, r, u, w, z, q, s, p, now, alpha

    def finish(x):
        press[...] = x
        for j in range(4):
            part = x[:, j * LANES : (j + 1) * LANES]
            pressure[j : j + 1, :] = part
            send[:, j, :] = jnp.broadcast_to(part, (send.shape[0], LANES))

    def gap(x):
        return rhs - times(block, x, mask, soft)

    def small(r):
        return dot(r, scale * r)[0, 0] <= TRUE_STOP * start[0, 0]

    state = begin(zero, rhs)
    for _ in range(CG_FIRST):
        state = advance(*state)
    state = begin(state[0], gap(state[0]))
    for _ in range(CG_AGAIN):
        state = advance(*state)
    first, rest = state[:2]
    finish(first)

    @pl.when(jnp.logical_not(small(rest)))
    def _():
        def going(state):
            step, norm = state[0], state[9]
            return (step < CG_STEPS) & ((step == 0) | (norm[0, 0] > CG_STOP * start[0, 0]))

        def body(state):
            return (state[0] + 1,) + advance(*state[1:])

        x = lax.while_loop(going, body, (0,) + begin(first, gap(first)))[1]
        finish(x)

        @pl.when(jnp.logical_not(small(gap(x))))
        def _():
            factor_solve(block, mask, rhs, soft, work, press)
            finish(press[...])


def finish_kernel(axes, trial, near, node, owner, slot, got, back, out):
    circs, lats = axes
    owners = got.shape[0]
    rows, cols = trial.shape[1:]
    chunks = node.shape[0]
    my_circ, my_lat = lax.axis_index("circ"), lax.axis_index("lat")
    me = my_circ * lats + my_lat
    after = jnp.where(my_circ == circs - 1, my_lat, me + lats)
    before = jnp.where(my_circ == 0, (circs - 1) * lats + my_lat, me - lats)
    right_dev = jnp.minimum(me + 1, owners - 1)
    left_dev = jnp.maximum(me - 1, 0)
    kc, kl, diag_k = near[0], near[1], near[2]
    row, col = iota((rows, cols), 0), iota((rows, cols), 1)
    for c in range(3):
        down, up = got[after, 2, 1 + c : 2 + c, :], got[before, 2, 1 + c : 2 + c, :]
        east, west = got[right_dev, 2, 1 + c : 2 + c, :], got[left_dev, 2, 1 + c : 2 + c, :]
        east = jnp.where(my_lat < lats - 1, east, 0.0)
        west = jnp.where(my_lat > 0, west, 0.0)
        circ_in = jnp.where(row == rows - 1, down, jnp.where(row == 0, up, 0.0))
        lat_in = jnp.where(
            col == cols - 1, column(east), jnp.where(col == 0, column(west), 0.0)
        )
        out[c] = trial[c] + (kc * circ_in + kl * lat_in) / diag_k

    answers = jnp.concatenate([back[:, j, :] for j in range(4)], axis=0)
    answers = jnp.concatenate(thirds(answers), axis=1).astype(BF16)
    step = 2 if chunks % 2 == 0 else 1
    span = step * LANES
    left, right = [], []
    for first in range(0, chunks, step):
        nodes = wide(node, first, step)
        where = wide(slot, first, step)
        device = wide(owner, first, step)
        low = where & (LANES - 1)
        source = jnp.where(device < 0, -1, (where >> log2(LANES)) * owners + device)
        one_low = (iota((LANES, span), 0) == low).astype(F32).astype(BF16)
        found = jnp.dot(
            answers, jnp.concatenate([one_low] * 3, axis=0), preferred_element_type=F32
        )
        push = jnp.sum(
            jnp.where(iota((4 * owners, span), 0) == source, found, 0.0), axis=0, keepdims=True
        )
        one_circ = iota((rows, span), 0) == nodes >> log2(cols)
        left.append(
            jnp.concatenate(
                [jnp.where(one_circ, x, 0.0) for x in thirds(push)], axis=0
            ).astype(BF16)
        )
        right.append((iota((cols, span), 0) == (nodes & (cols - 1))).astype(F32).astype(BF16))
    force = lax.dot_general(
        jnp.concatenate(left, axis=1),
        jnp.concatenate(right, axis=1),
        (((1,), (1,)), ((), ())),
        preferred_element_type=F32,
    )
    force = force[:rows] + force[rows : 2 * rows] + force[2 * rows :]
    out[2] = out[2] - force / diag_k


def shards(
    disp, stiff, spin, load, foot_node, foot_dest, foot_slot, foot_count, road, active, influence
):
    circs, lats = lax.axis_size("circ"), lax.axis_size("lat")
    owners = circs * lats
    size = road.shape[0]
    rows, cols = disp.shape[1:]
    assert rows == cols == LANES and size == 4 * LANES and circs > 2 and owners % 16 == 0
    anywhere = pl.BlockSpec(memory_space=pltpu.HBM)
    block = pl.BlockSpec(memory_space=pltpu.VMEM)
    params = pltpu.CompilerParams(vmem_limit_bytes=32 * 1024 * 1024)
    lists = [x.reshape(-1, LANES) for x in (foot_node, foot_dest, foot_slot)]
    listed = jax.ShapeDtypeStruct(lists[0].shape, I32)
    strip = (4, LANES)
    send, trial, near, nodes, owner, slots, roads, actives, blocks = pl.pallas_call(
        functools.partial(pack_kernel, (circs, lats)),
        in_specs=[pl.BlockSpec(memory_space=pltpu.SMEM)] * 2 + [anywhere] * 9,
        out_specs=[block] * 9,
        out_shape=[
            jax.ShapeDtypeStruct((owners, 3, 4, LANES), F32),
            jax.ShapeDtypeStruct((3, rows, cols), F32),
            jax.ShapeDtypeStruct((3, rows, cols), F32),
            listed,
            listed,
            listed,
            jax.ShapeDtypeStruct(strip, F32),
            jax.ShapeDtypeStruct(strip, I32),
            jax.ShapeDtypeStruct((size, size), F32),
        ],
        scratch_shapes=[
            pltpu.VMEM((3, rows, cols), F32),
            pltpu.VMEM((2, rows, cols), F32),
            pltpu.VMEM((3, rows, cols), F32),
            pltpu.VMEM(lists[0].shape, I32),
            pltpu.SemaphoreType.DMA((9,)),
        ],
        compiler_params=params,
        name="pack_rows",
    )(
        foot_count, spin,
        *[
            pltpu.with_memory_space_constraint(x, pltpu.HBM)
            for x in (
                *lists, stiff, disp, load, road.reshape(strip), active.reshape(strip), influence[0]
            )
        ]
    )
    got = lax.all_to_all(send, ("circ", "lat"), split_axis=0, concat_axis=0, tiled=True)
    reply, pressure = pl.pallas_call(
        functools.partial(solve_kernel, lats),
        in_specs=[block] * 4,
        out_specs=[block, block],
        out_shape=[
            jax.ShapeDtypeStruct((owners,) + strip, F32),
            jax.ShapeDtypeStruct(strip, F32),
        ],
        scratch_shapes=[
            pltpu.VMEM((size, size + LANES), F32),
            pltpu.VMEM((1, size), F32),
            pltpu.VMEM((16, 16, LANES), F32),
            pltpu.VMEM((4, owners, LANES), F32),
        ],
        compiler_params=params,
        name="solve_patch",
    )(got, roads, actives, blocks)
    back = lax.all_to_all(reply, ("circ", "lat"), split_axis=0, concat_axis=0, tiled=True)
    new_disp = pl.pallas_call(
        functools.partial(finish_kernel, (circs, lats)),
        in_specs=[block] * 7,
        out_specs=block,
        out_shape=jax.ShapeDtypeStruct(disp.shape, F32),
        compiler_params=params,
        name="finish_nodes",
    )(trial, near, nodes, owner, slots, got, back)
    return (new_disp, pressure.reshape(size))


def solution(mesh):
    return jax.shard_map(
        shards,
        mesh=mesh,
        in_specs=(
            P(None, ("cases", "circ"), "lat"),
            P(None, ("cases", "circ"), "lat"),
            P("cases"),
            P(None, ("cases", "circ"), "lat"),
            P(("cases", "circ", "lat")),
            P(("cases", "circ", "lat")),
            P(("cases", "circ", "lat")),
            P(("cases", "circ", "lat")),
            P(("cases", "circ", "lat")),
            P(("cases", "circ", "lat")),
            P(("cases", "circ", "lat"), None, None),
        ),
        out_specs=(P(None, ("cases", "circ"), "lat"), P(("cases", "circ", "lat"))),
        check_vma=False,
    )
```

```python
import functools

import jax
import jax.numpy as jnp
from jax import lax
from jax.experimental import pallas as pl
from jax.experimental.pallas import tpu as pltpu
from jax.sharding import PartitionSpec as P

F32 = jnp.float32
BF16 = jnp.bfloat16
I32 = jnp.int32
LANES = 128
CG_FIRST = 3
CG_AGAIN = 4
CG_STEPS = 40
CG_STOP = 2e-14
TRUE_STOP = 4e-13


def log2(value):
    assert value > 0 and value & (value - 1) == 0
    return value.bit_length() - 1


def thirds(x):
    high = x.astype(BF16).astype(F32)
    rest = x - high
    mid = rest.astype(BF16).astype(F32)
    return high, mid, rest - mid


def iota(shape, axis):
    return lax.broadcasted_iota(I32, shape, axis)


def wide(ref, first, count):
    return jnp.concatenate([ref[i : i + 1, :] for i in range(first, first + count)], axis=1)


def shifted(u):
    rows, cols = u.shape
    row, col = iota(u.shape, 0), iota(u.shape, 1)
    return (
        jnp.where(row == rows - 1, 0.0, pltpu.roll(u, rows - 1, 0)),
        jnp.where(row == 0, 0.0, pltpu.roll(u, 1, 0)),
        jnp.where(col == cols - 1, 0.0, pltpu.roll(u, cols - 1, 1)),
        jnp.where(col == 0, 0.0, pltpu.roll(u, 1, 1)),
    )


def edges(u):
    rows, cols = u.shape
    turned = u.T
    return [u[0:1, :], u[rows - 1 : rows, :], turned[0:1, :], turned[cols - 1 : cols, :]]


def pack_kernel(
    axes, count, spin, node, dest, slot, stiff, disp, load, road, active, block,
    send, trial, near, nodes, owner, slots, roads, actives, blocks,
    u, springs, loads, dests, sems,
):
    circs, lats = axes
    owners = send.shape[0]
    rows, cols = disp.shape[1:]
    chunks = node.shape[0]
    pairs = [
        (node, nodes), (dest, dests), (slot, slots), (stiff, springs), (disp, u), (load, loads), (road, roads), (active, actives),
        (block, blocks),
    ]
    copies = [pltpu.make_async_copy(a, b, sems.at[i]) for i, (a, b) in enumerate(pairs)]
    for copy in copies:
        copy.start()
    for copy in copies[:3]:
        copy.wait()

    width = 2 * LANES if chunks % 2 == 0 else LANES
    step = width // LANES
    to, tos = [], []
    for i in range(chunks):
        live = iota((1, LANES), 1) + i * LANES < count[0]
        target = jnp.where(live, dests[i : i + 1, :], -1)
        owner[i : i + 1, :] = target
        to.append(iota((owners, LANES), 0) == target)
        tos.append(to[i].astype(F32).astype(BF16))
    before = iota((LANES, 2 * LANES), 0) < iota((LANES, 2 * LANES), 1)
    ranks = jnp.dot(
        jnp.concatenate(tos, axis=0), before.astype(F32).astype(BF16), preferred_element_type=F32
    )
    passed = jnp.zeros((owners, LANES), F32)
    right = []
    for i in range(chunks):
        mine = ranks[i * owners : (i + 1) * owners]
        rank = jnp.sum(
            jnp.where(to[i], mine[:, :LANES] + passed, 0.0), axis=0, keepdims=True
        ).astype(I32)
        passed = passed + mine[:, LANES:]
        right.append((iota((LANES, LANES), 0) == rank).astype(F32).astype(BF16))

    for copy in copies[3:6]:
        copy.wait()
    kc = springs[0] - spin[0]
    kl = springs[1]
    diag_k = 2.0 * kc + 2.0 * kl + 0.5
    near[0] = kc
    near[1] = kl
    near[2] = diag_k
    for c in range(3):
        own = u[c]
        u_next, u_prev, u_right, u_left = shifted(own)
        force = kc * (2.0 * own - u_next - u_prev) + kl * (2.0 * own - u_right - u_left) + 0.5 * own
        trial[c] = own + (loads[c] - force) / diag_k
    table = jnp.concatenate(
        [jnp.concatenate(thirds(x), axis=1) for x in (trial[2], kc, kl)], axis=0
    ).astype(BF16)
    left = []
    for first in range(0, chunks, step):
        place = wide(nodes, first, step)
        circ = place >> log2(cols)
        lat = place & (cols - 1)
        one_lat = (iota((cols, width), 0) == lat).astype(F32).astype(BF16)
        picked = jnp.dot(
            table, jnp.concatenate([one_lat] * 3, axis=0), preferred_element_type=F32
        )
        one_circ = iota((rows, width), 0) == circ
        pieces = []
        for k in range(3):
            found = picked[k * rows : (k + 1) * rows]
            pieces += thirds(jnp.sum(jnp.where(one_circ, found, 0.0), axis=0, keepdims=True))
        where = wide(slots, first, step)
        low = where & (LANES - 1)
        pieces += [x.astype(F32) for x in (circ * cols, lat, where - low, low)]
        here = jnp.concatenate(to[first : first + step], axis=1)
        left.append(
            jnp.concatenate([jnp.where(here, x, 0.0) for x in pieces], axis=0).astype(BF16)
        )
    spread = lax.dot_general(
        jnp.concatenate(left, axis=1),
        jnp.concatenate(right, axis=1),
        (((1,), (1,)), ((), ())),
        preferred_element_type=F32,
    )
    part = [spread[i * owners : (i + 1) * owners] for i in range(13)]
    for v in range(3):
        send[:, 0, v, :] = part[3 * v] + part[3 * v + 1] + part[3 * v + 2]
    send[:, 0, 3, :] = part[9] + part[10]
    send[:, 2, 0, :] = part[11] + part[12]

    my_circ, my_lat = lax.axis_index("circ"), lax.axis_index("lat")
    me = my_circ * lats + my_lat
    after = jnp.where(my_circ == circs - 1, my_lat, me + lats)
    prior = jnp.where(my_circ == 0, (circs - 1) * lats + my_lat, me - lats)
    east = jnp.where(my_lat < lats - 1, me + 1, -1)
    west = jnp.where(my_lat > 0, me - 1, -1)
    device = iota((owners, LANES), 0)
    for c in range(3):
        layers = edges(u[c])
        lacks = jnp.zeros((owners, LANES), F32)
        for layer, reader in zip(layers, (prior, after, west, east)):
            lacks = jnp.where(device == reader, layer, lacks)
        send[:, 2, 1 + c, :] = lacks
        if c == 2:
            for t, layer in enumerate(layers):
                send[:, 1, t, :] = jnp.broadcast_to(layer, (owners, LANES))
    for copy in copies[6:]:
        copy.wait()


def column(row):
    return jnp.broadcast_to(row, (LANES, row.shape[1])).T


def patch_system(lats, got, road, active, rowed, layered):
    owners = got.shape[0]
    rows = cols = LANES
    size = 4 * LANES
    group = 16
    total = jnp.zeros((4 * group, LANES), F32)
    for first in range(0, owners, group):
        some = slice(first, first + group)
        w, kc, kl, node = [got[some, 0, v, :] for v in range(4)]
        slot = got[some, 2, 0, :].astype(I32)
        node = node.astype(I32)
        lat = node & (cols - 1)
        sender = jnp.where(kc > 0.0, iota(kc.shape, 0) + first, 0)
        pieces = thirds(w) + thirds(kc) + thirds(kl)
        pieces += tuple(x.astype(F32) for x in (node - lat, lat, sender))
        for p, piece in enumerate(pieces):
            rowed[p] = piece
        rowed[12] = (slot >> log2(LANES)).astype(F32)
        rowed[13] = (slot & (LANES - 1)).astype(F32)
        rowed[14:16] = jnp.zeros((2,) + kc.shape, F32)
        left, right = [], []
        for d in range(group):
            stack = rowed[:, d, :]
            high, low = stack[12:13, :], stack[13:14, :]
            left.append(
                jnp.concatenate(
                    [jnp.where(high == float(h), stack, 0.0) for h in range(4)], axis=0
                ).astype(BF16)
            )
            right.append(
                (iota((LANES, LANES), 0) == low.astype(I32)).astype(F32).astype(BF16)
            )
        total = total + lax.dot_general(
            jnp.concatenate(left, axis=1),
            jnp.concatenate(right, axis=1),
            (((1,), (1,)), ((), ())),
            preferred_element_type=F32,
        )
    values = []
    for at in ((0, 1, 2), (3, 4, 5), (6, 7, 8), (9, 10), (10,), (11,)):
        strips = []
        for h in range(4):
            strip = total[group * h + at[0] : group * h + at[0] + 1, :]
            for p in at[1:]:
                strip = strip + total[group * h + p : group * h + p + 1, :]
            strips.append(strip)
        values.append(jnp.concatenate(strips, axis=1))
    w, kc, kl = values[:3]
    node, lat, sender = [x.astype(I32) for x in values[3:]]
    circ = node >> log2(cols)
    after = sender + lats
    after = jnp.where(after >= owners, after - owners, after)
    before = sender - lats
    before = jnp.where(before < 0, before + owners, before)
    side = sender & (lats - 1)
    from_circ = jnp.where(
        circ == rows - 1, after, jnp.where(circ == 0, before + owners, -1)
    )
    from_lat = jnp.where(
        (lat == cols - 1) & (side < lats - 1),
        sender + 1 + 2 * owners,
        jnp.where((lat == 0) & (side > 0), sender - 1 + 3 * owners, -1),
    )
    for t in range(4):
        layered[t] = got[:, 1, t, :]
    layers = layered[...].reshape(owners * 4, LANES)
    layers = jnp.concatenate(thirds(layers), axis=1).astype(BF16)

    def pick(high, low):
        one = (iota((LANES, size), 0) == low).astype(F32).astype(BF16)
        found = jnp.dot(layers, jnp.concatenate([one] * 3, axis=0), preferred_element_type=F32)
        return jnp.sum(
            jnp.where(iota((owners * 4, size), 0) == high, found, 0.0), axis=0, keepdims=True
        )

    diag_k = 2.0 * kc + 2.0 * kl + 0.5
    w = w + (kc * pick(from_circ, lat) + kl * pick(from_lat, circ)) / diag_k
    mask = wide(active, 0, 4).astype(F32)
    return mask, mask * (w - wide(road, 0, 4)), 1.0 / diag_k


def factor_solve(block, mask, rhs, soft, work, press):
    size = rhs.shape[1]
    row = iota((size, 1), 0)
    lane = iota((1, LANES), 1)
    down = column(mask)
    for t in range(size // LANES):
        part = slice(t * LANES, (t + 1) * LANES)
        on = row == lane + t * LANES
        live = mask[:, part]
        work[:, part] = down * live * (block[:, part] + jnp.where(on, soft[:, part], 0.0)) + (
            jnp.where(on, 1.0 - live, 0.0)
        )
    work[:, size:] = column(rhs)
    place = iota((1, size), 1)

    def eliminate(j, carry):
        pivot_row = work[pl.ds(j, 1), :]
        pivot = jnp.sum(jnp.where(place == j, pivot_row[:, :size], 0.0), axis=1, keepdims=True)
        start = pl.multiple_of((j >> log2(LANES)) << log2(LANES), LANES)
        tile = work[:, pl.ds(start, LANES)]
        below = jnp.sum(jnp.where(lane == j - start, tile, 0.0), axis=1, keepdims=True)
        ratio = jnp.where(row > j, below / pivot, 0.0)
        work[...] = work[...] - ratio * pivot_row
        return carry

    lax.fori_loop(0, size, eliminate, 0)

    def substitute(step, x):
        j = size - 1 - step
        now = work[pl.ds(j, 1), :]
        upper = now[:, :size]
        pivot = jnp.sum(jnp.where(place == j, upper, 0.0), axis=1, keepdims=True)
        known = jnp.sum(upper * x, axis=1, keepdims=True)
        return jnp.where(place == j, (now[:, size : size + 1] - known) / pivot, x)

    press[...] = lax.fori_loop(0, size, substitute, jnp.zeros((1, size), F32))


def over(top, bottom):
    return jnp.where(bottom > 0.0, top / bottom, 0.0)


def dot(a, b):
    return jnp.sum(a * b, axis=1, keepdims=True)


def times(block, u, mask, soft):
    size = u.shape[1]
    parts = [jnp.zeros((8, LANES), F32)] * (size // LANES)
    for i in range(0, size, LANES):
        down = column(u[:, i : i + LANES])
        for k in range(size // LANES):
            tile = block[i : i + LANES, k * LANES : (k + 1) * LANES] * down
            parts[k] = parts[k] + jnp.sum(tile.reshape(LANES // 8, 8, LANES), axis=0)
    parts = [jnp.sum(part, axis=0, keepdims=True) for part in parts]
    return mask * (jnp.concatenate(parts, axis=1) + soft * u)


def solve_kernel(
    lats, got, road, active, block, send, pressure, work, press, rowed, layered
):
    size = 4 * LANES
    mask, rhs, soft = patch_system(lats, got, road, active, rowed, layered)
    square = iota((LANES, LANES), 0) == iota((LANES, LANES), 1)
    diagonal = jnp.concatenate(
        [
            jnp.sum(
                jnp.where(square, block[i : i + LANES, i : i + LANES], 0.0), axis=0, keepdims=True
            )
            for i in range(0, size, LANES)
        ],
        axis=1,
    )
    scale = mask / (diagonal + soft)
    start = dot(rhs, scale * rhs)
    zero = jnp.zeros((1, size), F32)
    none = jnp.zeros((1, 1), F32)

    def begin(x, r):
        u = scale * r
        return x, r, u, times(block, u, mask, soft), zero, zero, zero, zero, none, none

    def advance(x, r, u, w, z, q, s, p, norm, alpha):
        m = scale * w
        n = times(block, m, mask, soft)
        now = dot(r, u)
        beta = over(now, norm)
        alpha = over(now, dot(w, u) - over(beta * now, alpha))
        z = n + beta * z
        q = m + beta * q
        s = w + beta * s
        p = u + beta * p
        x, r, u, w = x + alpha * p, r - alpha * s, u - alpha * q, w - alpha * z
        return x, r, u, w, z, q, s, p, now, alpha

    def finish(x):
        press[...] = x
        for j in range(4):
            part = x[:, j * LANES : (j + 1) * LANES]
            pressure[j : j + 1, :] = part
            send[:, j, :] = jnp.broadcast_to(part, (send.shape[0], LANES))

    def gap(x):
        return rhs - times(block, x, mask, soft)

    def small(r):
        return dot(r, scale * r)[0, 0] <= TRUE_STOP * start[0, 0]

    state = begin(zero, rhs)
    for _ in range(CG_FIRST):
        state = advance(*state)
    state = begin(state[0], gap(state[0]))
    for _ in range(CG_AGAIN):
        state = advance(*state)
    first, rest = state[:2]
    finish(first)

    @pl.when(jnp.logical_not(small(rest)))
    def _():
        def going(state):
            step, norm = state[0], state[9]
            return (step < CG_STEPS) & ((step == 0) | (norm[0, 0] > CG_STOP * start[0, 0]))

        def body(state):
            return (state[0] + 1,) + advance(*state[1:])

        x = lax.while_loop(going, body, (0,) + begin(first, gap(first)))[1]
        finish(x)

        @pl.when(jnp.logical_not(small(gap(x))))
        def _():
            def refine(step, x):
                factor_solve(block, mask, gap(x), soft, work, press)
                return x + press[...]

            finish(lax.fori_loop(0, 2, refine, zero))


def finish_kernel(axes, trial, near, node, owner, slot, got, back, out):
    circs, lats = axes
    owners = got.shape[0]
    rows, cols = trial.shape[1:]
    chunks = node.shape[0]
    my_circ, my_lat = lax.axis_index("circ"), lax.axis_index("lat")
    me = my_circ * lats + my_lat
    after = jnp.where(my_circ == circs - 1, my_lat, me + lats)
    before = jnp.where(my_circ == 0, (circs - 1) * lats + my_lat, me - lats)
    right_dev = jnp.minimum(me + 1, owners - 1)
    left_dev = jnp.maximum(me - 1, 0)
    kc, kl, diag_k = near[0], near[1], near[2]
    row, col = iota((rows, cols), 0), iota((rows, cols), 1)
    for c in range(3):
        down, up = got[after, 2, 1 + c : 2 + c, :], got[before, 2, 1 + c : 2 + c, :]
        east, west = got[right_dev, 2, 1 + c : 2 + c, :], got[left_dev, 2, 1 + c : 2 + c, :]
        east = jnp.where(my_lat < lats - 1, east, 0.0)
        west = jnp.where(my_lat > 0, west, 0.0)
        circ_in = jnp.where(row == rows - 1, down, jnp.where(row == 0, up, 0.0))
        lat_in = jnp.where(
            col == cols - 1, column(east), jnp.where(col == 0, column(west), 0.0)
        )
        out[c] = trial[c] + (kc * circ_in + kl * lat_in) / diag_k

    answers = jnp.concatenate([back[:, j, :] for j in range(4)], axis=0)
    answers = jnp.concatenate(thirds(answers), axis=1).astype(BF16)
    step = 2 if chunks % 2 == 0 else 1
    span = step * LANES
    left, right = [], []
    for first in range(0, chunks, step):
        nodes = wide(node, first, step)
        where = wide(slot, first, step)
        device = wide(owner, first, step)
        low = where & (LANES - 1)
        source = jnp.where(device < 0, -1, (where >> log2(LANES)) * owners + device)
        one_low = (iota((LANES, span), 0) == low).astype(F32).astype(BF16)
        found = jnp.dot(
            answers, jnp.concatenate([one_low] * 3, axis=0), preferred_element_type=F32
        )
        push = jnp.sum(
            jnp.where(iota((4 * owners, span), 0) == source, found, 0.0), axis=0, keepdims=True
        )
        one_circ = iota((rows, span), 0) == nodes >> log2(cols)
        left.append(
            jnp.concatenate(
                [jnp.where(one_circ, x, 0.0) for x in thirds(push)], axis=0
            ).astype(BF16)
        )
        right.append((iota((cols, span), 0) == (nodes & (cols - 1))).astype(F32).astype(BF16))
    force = lax.dot_general(
        jnp.concatenate(left, axis=1),
        jnp.concatenate(right, axis=1),
        (((1,), (1,)), ((), ())),
        preferred_element_type=F32,
    )
    force = force[:rows] + force[rows : 2 * rows] + force[2 * rows :]
    out[2] = out[2] - force / diag_k


def shards(
    disp, stiff, spin, load, foot_node, foot_dest, foot_slot, foot_count, road, active, influence
):
    circs, lats = lax.axis_size("circ"), lax.axis_size("lat")
    owners = circs * lats
    size = road.shape[0]
    rows, cols = disp.shape[1:]
    assert rows == cols == LANES and size == 4 * LANES and circs > 2 and owners % 16 == 0
    anywhere = pl.BlockSpec(memory_space=pltpu.HBM)
    block = pl.BlockSpec(memory_space=pltpu.VMEM)
    params = pltpu.CompilerParams(vmem_limit_bytes=32 * 1024 * 1024)
    lists = [x.reshape(-1, LANES) for x in (foot_node, foot_dest, foot_slot)]
    listed = jax.ShapeDtypeStruct(lists[0].shape, I32)
    strip = (4, LANES)
    send, trial, near, nodes, owner, slots, roads, actives, blocks = pl.pallas_call(
        functools.partial(pack_kernel, (circs, lats)),
        in_specs=[pl.BlockSpec(memory_space=pltpu.SMEM)] * 2 + [anywhere] * 9,
        out_specs=[block] * 9,
        out_shape=[
            jax.ShapeDtypeStruct((owners, 3, 4, LANES), F32),
            jax.ShapeDtypeStruct((3, rows, cols), F32),
            jax.ShapeDtypeStruct((3, rows, cols), F32),
            listed,
            listed,
            listed,
            jax.ShapeDtypeStruct(strip, F32),
            jax.ShapeDtypeStruct(strip, I32),
            jax.ShapeDtypeStruct((size, size), F32),
        ],
        scratch_shapes=[
            pltpu.VMEM((3, rows, cols), F32),
            pltpu.VMEM((2, rows, cols), F32),
            pltpu.VMEM((3, rows, cols), F32),
            pltpu.VMEM(lists[0].shape, I32),
            pltpu.SemaphoreType.DMA((9,)),
        ],
        compiler_params=params,
        name="pack_rows",
    )(
        foot_count, spin,
        *[
            pltpu.with_memory_space_constraint(x, pltpu.HBM)
            for x in (
                *lists, stiff, disp, load, road.reshape(strip), active.reshape(strip), influence[0]
            )
        ]
    )
    got = lax.all_to_all(send, ("circ", "lat"), split_axis=0, concat_axis=0, tiled=True)
    reply, pressure = pl.pallas_call(
        functools.partial(solve_kernel, lats),
        in_specs=[block] * 4,
        out_specs=[block, block],
        out_shape=[
            jax.ShapeDtypeStruct((owners,) + strip, F32),
            jax.ShapeDtypeStruct(strip, F32),
        ],
        scratch_shapes=[
            pltpu.VMEM((size, size + LANES), F32),
            pltpu.VMEM((1, size), F32),
            pltpu.VMEM((16, 16, LANES), F32),
            pltpu.VMEM((4, owners, LANES), F32),
        ],
        compiler_params=params,
        name="solve_patch",
    )(got, roads, actives, blocks)
    back = lax.all_to_all(reply, ("circ", "lat"), split_axis=0, concat_axis=0, tiled=True)
    new_disp = pl.pallas_call(
        functools.partial(finish_kernel, (circs, lats)),
        in_specs=[block] * 7,
        out_specs=block,
        out_shape=jax.ShapeDtypeStruct(disp.shape, F32),
        compiler_params=params,
        name="finish_nodes",
    )(trial, near, nodes, owner, slots, got, back)
    return (new_disp, pressure.reshape(size))


def solution(mesh):
    return jax.shard_map(
        shards,
        mesh=mesh,
        in_specs=(
            P(None, ("cases", "circ"), "lat"),
            P(None, ("cases", "circ"), "lat"),
            P("cases"),
            P(None, ("cases", "circ"), "lat"),
            P(("cases", "circ", "lat")),
            P(("cases", "circ", "lat")),
            P(("cases", "circ", "lat")),
            P(("cases", "circ", "lat")),
            P(("cases", "circ", "lat")),
            P(("cases", "circ", "lat")),
            P(("cases", "circ", "lat"), None, None),
        ),
        out_specs=(P(None, ("cases", "circ"), "lat"), P(("cases", "circ", "lat"))),
        check_vma=False,
    )
```

```python
import functools

import jax
import jax.numpy as jnp
from jax import lax
from jax.experimental import pallas as pl
from jax.experimental.pallas import tpu as pltpu
from jax.sharding import PartitionSpec as P

F32 = jnp.float32
BF16 = jnp.bfloat16
I32 = jnp.int32
LANES = 128
CG_FIRST = 3
CG_AGAIN = 4
CG_STEPS = 40
CG_STOP = 2e-14
TRUE_STOP = 4e-13


def log2(value):
    assert value > 0 and value & (value - 1) == 0
    return value.bit_length() - 1


def thirds(x):
    high = x.astype(BF16).astype(F32)
    rest = x - high
    mid = rest.astype(BF16).astype(F32)
    return high, mid, rest - mid


def iota(shape, axis):
    return lax.broadcasted_iota(I32, shape, axis)


def wide(ref, first, count):
    return jnp.concatenate([ref[i : i + 1, :] for i in range(first, first + count)], axis=1)


def shifted(u):
    rows, cols = u.shape
    row, col = iota(u.shape, 0), iota(u.shape, 1)
    return (
        jnp.where(row == rows - 1, 0.0, pltpu.roll(u, rows - 1, 0)),
        jnp.where(row == 0, 0.0, pltpu.roll(u, 1, 0)),
        jnp.where(col == cols - 1, 0.0, pltpu.roll(u, cols - 1, 1)),
        jnp.where(col == 0, 0.0, pltpu.roll(u, 1, 1)),
    )


def edges(u):
    rows, cols = u.shape
    turned = u.T
    return [u[0:1, :], u[rows - 1 : rows, :], turned[0:1, :], turned[cols - 1 : cols, :]]


def pack_kernel(
    axes, count, spin, node, dest, slot, stiff, disp, load, road, active, block,
    send, trial, near, nodes, owner, slots, roads, actives, blocks,
    u, springs, loads, dests, sems,
):
    circs, lats = axes
    owners = send.shape[0]
    rows, cols = disp.shape[1:]
    chunks = node.shape[0]
    pairs = [
        (node, nodes), (dest, dests), (slot, slots), (stiff, springs), (disp, u), (load, loads), (road, roads), (active, actives),
        (block, blocks),
    ]
    copies = [pltpu.make_async_copy(a, b, sems.at[i]) for i, (a, b) in enumerate(pairs)]
    for copy in copies:
        copy.start()
    for copy in copies[:3]:
        copy.wait()

    width = 2 * LANES if chunks % 2 == 0 else LANES
    step = width // LANES
    to, tos = [], []
    for i in range(chunks):
        live = iota((1, LANES), 1) + i * LANES < count[0]
        target = jnp.where(live, dests[i : i + 1, :], -1)
        owner[i : i + 1, :] = target
        to.append(iota((owners, LANES), 0) == target)
        tos.append(to[i].astype(F32).astype(BF16))
    before = iota((LANES, 2 * LANES), 0) < iota((LANES, 2 * LANES), 1)
    ranks = jnp.dot(
        jnp.concatenate(tos, axis=0), before.astype(F32).astype(BF16), preferred_element_type=F32
    )
    passed = jnp.zeros((owners, LANES), F32)
    right = []
    for i in range(chunks):
        mine = ranks[i * owners : (i + 1) * owners]
        rank = jnp.sum(
            jnp.where(to[i], mine[:, :LANES] + passed, 0.0), axis=0, keepdims=True
        ).astype(I32)
        passed = passed + mine[:, LANES:]
        right.append((iota((LANES, LANES), 0) == rank).astype(F32).astype(BF16))

    for copy in copies[3:6]:
        copy.wait()
    kc = springs[0] - spin[0]
    kl = springs[1]
    diag_k = 2.0 * kc + 2.0 * kl + 0.5
    near[0] = kc
    near[1] = kl
    near[2] = diag_k
    for c in range(3):
        own = u[c]
        u_next, u_prev, u_right, u_left = shifted(own)
        force = kc * (2.0 * own - u_next - u_prev) + kl * (2.0 * own - u_right - u_left) + 0.5 * own
        trial[c] = own + (loads[c] - force) / diag_k
    table = jnp.concatenate(
        [jnp.concatenate(thirds(x), axis=1) for x in (trial[2], kc, kl)], axis=0
    ).astype(BF16)
    left = []
    for first in range(0, chunks, step):
        place = wide(nodes, first, step)
        circ = place >> log2(cols)
        lat = place & (cols - 1)
        one_lat = (iota((cols, width), 0) == lat).astype(F32).astype(BF16)
        picked = jnp.dot(
            table, jnp.concatenate([one_lat] * 3, axis=0), preferred_element_type=F32
        )
        one_circ = iota((rows, width), 0) == circ
        pieces = []
        for k in range(3):
            found = picked[k * rows : (k + 1) * rows]
            pieces += thirds(jnp.sum(jnp.where(one_circ, found, 0.0), axis=0, keepdims=True))
        where = wide(slots, first, step)
        low = where & (LANES - 1)
        pieces += [x.astype(F32) for x in (circ * cols, lat, where - low, low)]
        here = jnp.concatenate(to[first : first + step], axis=1)
        left.append(
            jnp.concatenate([jnp.where(here, x, 0.0) for x in pieces], axis=0).astype(BF16)
        )
    spread = lax.dot_general(
        jnp.concatenate(left, axis=1),
        jnp.concatenate(right, axis=1),
        (((1,), (1,)), ((), ())),
        preferred_element_type=F32,
    )
    part = [spread[i * owners : (i + 1) * owners] for i in range(13)]
    for v in range(3):
        send[:, 0, v, :] = part[3 * v] + part[3 * v + 1] + part[3 * v + 2]
    send[:, 0, 3, :] = part[9] + part[10]
    send[:, 2, 0, :] = part[11] + part[12]

    my_circ, my_lat = lax.axis_index("circ"), lax.axis_index("lat")
    me = my_circ * lats + my_lat
    after = jnp.where(my_circ == circs - 1, my_lat, me + lats)
    prior = jnp.where(my_circ == 0, (circs - 1) * lats + my_lat, me - lats)
    east = jnp.where(my_lat < lats - 1, me + 1, -1)
    west = jnp.where(my_lat > 0, me - 1, -1)
    device = iota((owners, LANES), 0)
    for c in range(3):
        layers = edges(u[c])
        lacks = jnp.zeros((owners, LANES), F32)
        for layer, reader in zip(layers, (prior, after, west, east)):
            lacks = jnp.where(device == reader, layer, lacks)
        send[:, 2, 1 + c, :] = lacks
        if c == 2:
            for t, layer in enumerate(layers):
                send[:, 1, t, :] = jnp.broadcast_to(layer, (owners, LANES))
    for copy in copies[6:]:
        copy.wait()


def column(row):
    return jnp.broadcast_to(row, (LANES, row.shape[1])).T


def patch_system(lats, got, road, active, rowed, layered):
    owners = got.shape[0]
    rows = cols = LANES
    size = 4 * LANES
    group = 16
    total = jnp.zeros((4 * group, LANES), F32)
    for first in range(0, owners, group):
        some = slice(first, first + group)
        w, kc, kl, node = [got[some, 0, v, :] for v in range(4)]
        slot = got[some, 2, 0, :].astype(I32)
        node = node.astype(I32)
        lat = node & (cols - 1)
        sender = jnp.where(kc > 0.0, iota(kc.shape, 0) + first, 0)
        pieces = thirds(w) + thirds(kc) + thirds(kl)
        pieces += tuple(x.astype(F32) for x in (node - lat, lat, sender))
        for p, piece in enumerate(pieces):
            rowed[p] = piece
        rowed[12] = (slot >> log2(LANES)).astype(F32)
        rowed[13] = (slot & (LANES - 1)).astype(F32)
        rowed[14:16] = jnp.zeros((2,) + kc.shape, F32)
        left, right = [], []
        for d in range(group):
            stack = rowed[:, d, :]
            high, low = stack[12:13, :], stack[13:14, :]
            left.append(
                jnp.concatenate(
                    [jnp.where(high == float(h), stack, 0.0) for h in range(4)], axis=0
                ).astype(BF16)
            )
            right.append(
                (iota((LANES, LANES), 0) == low.astype(I32)).astype(F32).astype(BF16)
            )
        total = total + lax.dot_general(
            jnp.concatenate(left, axis=1),
            jnp.concatenate(right, axis=1),
            (((1,), (1,)), ((), ())),
            preferred_element_type=F32,
        )
    values = []
    for at in ((0, 1, 2), (3, 4, 5), (6, 7, 8), (9, 10), (10,), (11,)):
        strips = []
        for h in range(4):
            strip = total[group * h + at[0] : group * h + at[0] + 1, :]
            for p in at[1:]:
                strip = strip + total[group * h + p : group * h + p + 1, :]
            strips.append(strip)
        values.append(jnp.concatenate(strips, axis=1))
    w, kc, kl = values[:3]
    node, lat, sender = [x.astype(I32) for x in values[3:]]
    circ = node >> log2(cols)
    after = sender + lats
    after = jnp.where(after >= owners, after - owners, after)
    before = sender - lats
    before = jnp.where(before < 0, before + owners, before)
    side = sender & (lats - 1)
    from_circ = jnp.where(
        circ == rows - 1, after, jnp.where(circ == 0, before + owners, -1)
    )
    from_lat = jnp.where(
        (lat == cols - 1) & (side < lats - 1),
        sender + 1 + 2 * owners,
        jnp.where((lat == 0) & (side > 0), sender - 1 + 3 * owners, -1),
    )
    for t in range(4):
        layered[t] = got[:, 1, t, :]
    layers = layered[...].reshape(owners * 4, LANES)
    layers = jnp.concatenate(thirds(layers), axis=1).astype(BF16)

    def pick(high, low):
        one = (iota((LANES, size), 0) == low).astype(F32).astype(BF16)
        found = jnp.dot(layers, jnp.concatenate([one] * 3, axis=0), preferred_element_type=F32)
        return jnp.sum(
            jnp.where(iota((owners * 4, size), 0) == high, found, 0.0), axis=0, keepdims=True
        )

    diag_k = 2.0 * kc + 2.0 * kl + 0.5
    w = w + (kc * pick(from_circ, lat) + kl * pick(from_lat, circ)) / diag_k
    mask = wide(active, 0, 4).astype(F32)
    return mask, mask * (w - wide(road, 0, 4)), 1.0 / diag_k


def factor_solve(block, mask, rhs, soft, work, press):
    size = rhs.shape[1]
    row = iota((size, 1), 0)
    lane = iota((1, LANES), 1)
    down = column(mask)
    for t in range(size // LANES):
        part = slice(t * LANES, (t + 1) * LANES)
        on = row == lane + t * LANES
        live = mask[:, part]
        work[:, part] = down * live * (block[:, part] + jnp.where(on, soft[:, part], 0.0)) + (
            jnp.where(on, 1.0 - live, 0.0)
        )
    work[:, size:] = column(rhs)
    place = iota((1, size), 1)

    def eliminate(j, carry):
        pivot_row = work[pl.ds(j, 1), :]
        pivot = jnp.sum(jnp.where(place == j, pivot_row[:, :size], 0.0), axis=1, keepdims=True)
        start = pl.multiple_of((j >> log2(LANES)) << log2(LANES), LANES)
        tile = work[:, pl.ds(start, LANES)]
        below = jnp.sum(jnp.where(lane == j - start, tile, 0.0), axis=1, keepdims=True)
        ratio = jnp.where(row > j, below / pivot, 0.0)
        work[...] = work[...] - ratio * pivot_row
        return carry

    lax.fori_loop(0, size, eliminate, 0)

    def substitute(step, x):
        j = size - 1 - step
        now = work[pl.ds(j, 1), :]
        upper = now[:, :size]
        pivot = jnp.sum(jnp.where(place == j, upper, 0.0), axis=1, keepdims=True)
        known = jnp.sum(upper * x, axis=1, keepdims=True)
        return jnp.where(place == j, (now[:, size : size + 1] - known) / pivot, x)

    press[...] = lax.fori_loop(0, size, substitute, jnp.zeros((1, size), F32))


def over(top, bottom):
    return jnp.where(bottom > 0.0, top / bottom, 0.0)


def dot(a, b):
    return jnp.sum(a * b, axis=1, keepdims=True)


def times(block, u, mask, soft):
    size = u.shape[1]
    parts = [jnp.zeros((8, LANES), F32)] * (size // LANES)
    for i in range(0, size, LANES):
        down = column(u[:, i : i + LANES])
        for k in range(size // LANES):
            tile = block[i : i + LANES, k * LANES : (k + 1) * LANES] * down
            parts[k] = parts[k] + jnp.sum(tile.reshape(LANES // 8, 8, LANES), axis=0)
    parts = [jnp.sum(part, axis=0, keepdims=True) for part in parts]
    return mask * (jnp.concatenate(parts, axis=1) + soft * u)


def solve_kernel(
    lats, got, road, active, block, send, work, press, rowed, layered
):
    size = 4 * LANES
    mask, rhs, soft = patch_system(lats, got, road, active, rowed, layered)
    square = iota((LANES, LANES), 0) == iota((LANES, LANES), 1)
    diagonal = jnp.concatenate(
        [
            jnp.sum(
                jnp.where(square, block[i : i + LANES, i : i + LANES], 0.0), axis=0, keepdims=True
            )
            for i in range(0, size, LANES)
        ],
        axis=1,
    )
    scale = mask / (diagonal + soft)
    start = dot(rhs, scale * rhs)
    zero = jnp.zeros((1, size), F32)
    none = jnp.zeros((1, 1), F32)

    def begin(x, r):
        u = scale * r
        return x, r, u, times(block, u, mask, soft), zero, zero, zero, zero, none, none

    def advance(x, r, u, w, z, q, s, p, norm, alpha):
        m = scale * w
        n = times(block, m, mask, soft)
        now = dot(r, u)
        beta = over(now, norm)
        alpha = over(now, dot(w, u) - over(beta * now, alpha))
        z = n + beta * z
        q = m + beta * q
        s = w + beta * s
        p = u + beta * p
        x, r, u, w = x + alpha * p, r - alpha * s, u - alpha * q, w - alpha * z
        return x, r, u, w, z, q, s, p, now, alpha

    def finish(x):
        press[...] = x
        for j in range(4):
            part = x[:, j * LANES : (j + 1) * LANES]
            send[:, j, :] = jnp.broadcast_to(part, (send.shape[0], LANES))

    def gap(x):
        return rhs - times(block, x, mask, soft)

    def small(r):
        return dot(r, scale * r)[0, 0] <= TRUE_STOP * start[0, 0]

    state = begin(zero, rhs)
    for _ in range(CG_FIRST):
        state = advance(*state)
    state = begin(state[0], gap(state[0]))
    for _ in range(CG_AGAIN):
        state = advance(*state)
    first, rest = state[:2]
    finish(first)

    @pl.when(jnp.logical_not(small(rest)))
    def _():
        def going(state):
            step, norm = state[0], state[9]
            return (step < CG_STEPS) & ((step == 0) | (norm[0, 0] > CG_STOP * start[0, 0]))

        def body(state):
            return (state[0] + 1,) + advance(*state[1:])

        x = lax.while_loop(going, body, (0,) + begin(first, gap(first)))[1]
        finish(x)

        @pl.when(jnp.logical_not(small(gap(x))))
        def _():
            def refine(step, x):
                factor_solve(block, mask, gap(x), soft, work, press)
                return x + press[...]

            finish(lax.fori_loop(0, 2, refine, zero))


def finish_kernel(axes, trial, near, node, owner, slot, got, back, out, pressure):
    circs, lats = axes
    owners = got.shape[0]
    rows, cols = trial.shape[1:]
    chunks = node.shape[0]
    my_circ, my_lat = lax.axis_index("circ"), lax.axis_index("lat")
    me = my_circ * lats + my_lat
    after = jnp.where(my_circ == circs - 1, my_lat, me + lats)
    before = jnp.where(my_circ == 0, (circs - 1) * lats + my_lat, me - lats)
    right_dev = jnp.minimum(me + 1, owners - 1)
    left_dev = jnp.maximum(me - 1, 0)
    kc, kl, diag_k = near[0], near[1], near[2]
    row, col = iota((rows, cols), 0), iota((rows, cols), 1)
    for c in range(3):
        down, up = got[after, 2, 1 + c : 2 + c, :], got[before, 2, 1 + c : 2 + c, :]
        east, west = got[right_dev, 2, 1 + c : 2 + c, :], got[left_dev, 2, 1 + c : 2 + c, :]
        east = jnp.where(my_lat < lats - 1, east, 0.0)
        west = jnp.where(my_lat > 0, west, 0.0)
        circ_in = jnp.where(row == rows - 1, down, jnp.where(row == 0, up, 0.0))
        lat_in = jnp.where(
            col == cols - 1, column(east), jnp.where(col == 0, column(west), 0.0)
        )
        out[c] = trial[c] + (kc * circ_in + kl * lat_in) / diag_k

    pressure[...] = back[me]
    answers = jnp.concatenate([back[:, j, :] for j in range(4)], axis=0)
    answers = jnp.concatenate(thirds(answers), axis=1).astype(BF16)
    step = 2 if chunks % 2 == 0 else 1
    span = step * LANES
    left, right = [], []
    for first in range(0, chunks, step):
        nodes = wide(node, first, step)
        where = wide(slot, first, step)
        device = wide(owner, first, step)
        low = where & (LANES - 1)
        source = jnp.where(device < 0, -1, (where >> log2(LANES)) * owners + device)
        one_low = (iota((LANES, span), 0) == low).astype(F32).astype(BF16)
        found = jnp.dot(
            answers, jnp.concatenate([one_low] * 3, axis=0), preferred_element_type=F32
        )
        push = jnp.sum(
            jnp.where(iota((4 * owners, span), 0) == source, found, 0.0), axis=0, keepdims=True
        )
        one_circ = iota((rows, span), 0) == nodes >> log2(cols)
        left.append(
            jnp.concatenate(
                [jnp.where(one_circ, x, 0.0) for x in thirds(push)], axis=0
            ).astype(BF16)
        )
        right.append((iota((cols, span), 0) == (nodes & (cols - 1))).astype(F32).astype(BF16))
    force = lax.dot_general(
        jnp.concatenate(left, axis=1),
        jnp.concatenate(right, axis=1),
        (((1,), (1,)), ((), ())),
        preferred_element_type=F32,
    )
    force = force[:rows] + force[rows : 2 * rows] + force[2 * rows :]
    out[2] = out[2] - force / diag_k


def shards(
    disp, stiff, spin, load, foot_node, foot_dest, foot_slot, foot_count, road, active, influence
):
    circs, lats = lax.axis_size("circ"), lax.axis_size("lat")
    owners = circs * lats
    size = road.shape[0]
    rows, cols = disp.shape[1:]
    assert rows == cols == LANES and size == 4 * LANES and circs > 2 and owners % 16 == 0
    anywhere = pl.BlockSpec(memory_space=pltpu.HBM)
    block = pl.BlockSpec(memory_space=pltpu.VMEM)
    params = pltpu.CompilerParams(vmem_limit_bytes=32 * 1024 * 1024)
    lists = [x.reshape(-1, LANES) for x in (foot_node, foot_dest, foot_slot)]
    listed = jax.ShapeDtypeStruct(lists[0].shape, I32)
    strip = (4, LANES)
    send, trial, near, nodes, owner, slots, roads, actives, blocks = pl.pallas_call(
        functools.partial(pack_kernel, (circs, lats)),
        in_specs=[pl.BlockSpec(memory_space=pltpu.SMEM)] * 2 + [anywhere] * 9,
        out_specs=[block] * 9,
        out_shape=[
            jax.ShapeDtypeStruct((owners, 3, 4, LANES), F32),
            jax.ShapeDtypeStruct((3, rows, cols), F32),
            jax.ShapeDtypeStruct((3, rows, cols), F32),
            listed,
            listed,
            listed,
            jax.ShapeDtypeStruct(strip, F32),
            jax.ShapeDtypeStruct(strip, I32),
            jax.ShapeDtypeStruct((size, size), F32),
        ],
        scratch_shapes=[
            pltpu.VMEM((3, rows, cols), F32),
            pltpu.VMEM((2, rows, cols), F32),
            pltpu.VMEM((3, rows, cols), F32),
            pltpu.VMEM(lists[0].shape, I32),
            pltpu.SemaphoreType.DMA((9,)),
        ],
        compiler_params=params,
        name="pack_rows",
    )(
        foot_count, spin,
        *[
            pltpu.with_memory_space_constraint(x, pltpu.HBM)
            for x in (
                *lists, stiff, disp, load, road.reshape(strip), active.reshape(strip), influence[0]
            )
        ]
    )
    got = lax.all_to_all(send, ("circ", "lat"), split_axis=0, concat_axis=0, tiled=True)
    reply = pl.pallas_call(
        functools.partial(solve_kernel, lats),
        in_specs=[block] * 4,
        out_specs=block,
        out_shape=jax.ShapeDtypeStruct((owners,) + strip, F32),
        scratch_shapes=[
            pltpu.VMEM((size, size + LANES), F32),
            pltpu.VMEM((1, size), F32),
            pltpu.VMEM((16, 16, LANES), F32),
            pltpu.VMEM((4, owners, LANES), F32),
        ],
        compiler_params=params,
        name="solve_patch",
    )(got, roads, actives, blocks)
    back = lax.all_to_all(reply, ("circ", "lat"), split_axis=0, concat_axis=0, tiled=True)
    new_disp, pressure = pl.pallas_call(
        functools.partial(finish_kernel, (circs, lats)),
        in_specs=[block] * 7,
        out_specs=[block, block],
        out_shape=[
            jax.ShapeDtypeStruct(disp.shape, F32),
            jax.ShapeDtypeStruct(strip, F32),
        ],
        compiler_params=params,
        name="finish_nodes",
    )(trial, near, nodes, owner, slots, got, back)
    return (new_disp, pressure.reshape(size))


def solution(mesh):
    return jax.shard_map(
        shards,
        mesh=mesh,
        in_specs=(
            P(None, ("cases", "circ"), "lat"),
            P(None, ("cases", "circ"), "lat"),
            P("cases"),
            P(None, ("cases", "circ"), "lat"),
            P(("cases", "circ", "lat")),
            P(("cases", "circ", "lat")),
            P(("cases", "circ", "lat")),
            P(("cases", "circ", "lat")),
            P(("cases", "circ", "lat")),
            P(("cases", "circ", "lat")),
            P(("cases", "circ", "lat"), None, None),
        ),
        out_specs=(P(None, ("cases", "circ"), "lat"), P(("cases", "circ", "lat"))),
        check_vma=False,
    )
```

```python
import functools

import jax
import jax.numpy as jnp
from jax import lax
from jax.experimental import pallas as pl
from jax.experimental.pallas import tpu as pltpu
from jax.sharding import PartitionSpec as P

F32 = jnp.float32
BF16 = jnp.bfloat16
I32 = jnp.int32
LANES = 128
CG_FIRST = 3
CG_AGAIN = 4
CG_STEPS = 40
CG_STOP = 2e-14
FIRST_STOP = 1e-12
TRUE_STOP = 4e-13


def log2(value):
    assert value > 0 and value & (value - 1) == 0
    return value.bit_length() - 1


def thirds(x):
    high = x.astype(BF16).astype(F32)
    rest = x - high
    mid = rest.astype(BF16).astype(F32)
    return high, mid, rest - mid


def iota(shape, axis):
    return lax.broadcasted_iota(I32, shape, axis)


def wide(ref, first, count):
    return jnp.concatenate([ref[i : i + 1, :] for i in range(first, first + count)], axis=1)


def shifted(u):
    rows, cols = u.shape
    row, col = iota(u.shape, 0), iota(u.shape, 1)
    return (
        jnp.where(row == rows - 1, 0.0, pltpu.roll(u, rows - 1, 0)),
        jnp.where(row == 0, 0.0, pltpu.roll(u, 1, 0)),
        jnp.where(col == cols - 1, 0.0, pltpu.roll(u, cols - 1, 1)),
        jnp.where(col == 0, 0.0, pltpu.roll(u, 1, 1)),
    )


def edges(u):
    rows, cols = u.shape
    turned = u.T
    return [u[0:1, :], u[rows - 1 : rows, :], turned[0:1, :], turned[cols - 1 : cols, :]]


def pack_kernel(
    axes, count, spin, node, dest, slot, stiff, disp, load, road, active, block,
    send, trial, near, nodes, owner, slots, roads, actives, blocks,
    u, springs, loads, dests, sems,
):
    circs, lats = axes
    owners = send.shape[0]
    rows, cols = disp.shape[1:]
    chunks = node.shape[0]
    pairs = [
        (node, nodes), (dest, dests), (slot, slots), (stiff, springs), (disp, u), (load, loads), (road, roads), (active, actives),
        (block, blocks),
    ]
    copies = [pltpu.make_async_copy(a, b, sems.at[i]) for i, (a, b) in enumerate(pairs)]
    for copy in copies:
        copy.start()
    for copy in copies[:3]:
        copy.wait()

    width = 2 * LANES if chunks % 2 == 0 else LANES
    step = width // LANES
    to, tos = [], []
    for i in range(chunks):
        live = iota((1, LANES), 1) + i * LANES < count[0]
        target = jnp.where(live, dests[i : i + 1, :], -1)
        owner[i : i + 1, :] = target
        to.append(iota((owners, LANES), 0) == target)
        tos.append(to[i].astype(F32).astype(BF16))
    before = iota((LANES, 2 * LANES), 0) < iota((LANES, 2 * LANES), 1)
    ranks = jnp.dot(
        jnp.concatenate(tos, axis=0), before.astype(F32).astype(BF16), preferred_element_type=F32
    )
    passed = jnp.zeros((owners, LANES), F32)
    right = []
    for i in range(chunks):
        mine = ranks[i * owners : (i + 1) * owners]
        rank = jnp.sum(
            jnp.where(to[i], mine[:, :LANES] + passed, 0.0), axis=0, keepdims=True
        ).astype(I32)
        passed = passed + mine[:, LANES:]
        right.append((iota((LANES, LANES), 0) == rank).astype(F32).astype(BF16))

    for copy in copies[3:6]:
        copy.wait()
    kc = springs[0] - spin[0]
    kl = springs[1]
    diag_k = 2.0 * kc + 2.0 * kl + 0.5
    near[0] = kc
    near[1] = kl
    near[2] = diag_k
    for c in range(3):
        own = u[c]
        u_next, u_prev, u_right, u_left = shifted(own)
        force = kc * (2.0 * own - u_next - u_prev) + kl * (2.0 * own - u_right - u_left) + 0.5 * own
        trial[c] = own + (loads[c] - force) / diag_k
    table = jnp.concatenate(
        [jnp.concatenate(thirds(x), axis=1) for x in (trial[2], kc, kl)], axis=0
    ).astype(BF16)
    left = []
    for first in range(0, chunks, step):
        place = wide(nodes, first, step)
        circ = place >> log2(cols)
        lat = place & (cols - 1)
        one_lat = (iota((cols, width), 0) == lat).astype(F32).astype(BF16)
        picked = jnp.dot(
            table, jnp.concatenate([one_lat] * 3, axis=0), preferred_element_type=F32
        )
        one_circ = iota((rows, width), 0) == circ
        pieces = []
        for k in range(3):
            found = picked[k * rows : (k + 1) * rows]
            pieces += thirds(jnp.sum(jnp.where(one_circ, found, 0.0), axis=0, keepdims=True))
        where = wide(slots, first, step)
        low = where & (LANES - 1)
        pieces += [x.astype(F32) for x in (circ * cols, lat, where - low, low)]
        here = jnp.concatenate(to[first : first + step], axis=1)
        left.append(
            jnp.concatenate([jnp.where(here, x, 0.0) for x in pieces], axis=0).astype(BF16)
        )
    spread = lax.dot_general(
        jnp.concatenate(left, axis=1),
        jnp.concatenate(right, axis=1),
        (((1,), (1,)), ((), ())),
        preferred_element_type=F32,
    )
    part = [spread[i * owners : (i + 1) * owners] for i in range(13)]
    for v in range(3):
        send[:, 0, v, :] = part[3 * v] + part[3 * v + 1] + part[3 * v + 2]
    send[:, 0, 3, :] = part[9] + part[10]
    send[:, 2, 0, :] = part[11] + part[12]

    my_circ, my_lat = lax.axis_index("circ"), lax.axis_index("lat")
    me = my_circ * lats + my_lat
    after = jnp.where(my_circ == circs - 1, my_lat, me + lats)
    prior = jnp.where(my_circ == 0, (circs - 1) * lats + my_lat, me - lats)
    east = jnp.where(my_lat < lats - 1, me + 1, -1)
    west = jnp.where(my_lat > 0, me - 1, -1)
    device = iota((owners, LANES), 0)
    for c in range(3):
        layers = edges(u[c])
        lacks = jnp.zeros((owners, LANES), F32)
        for layer, reader in zip(layers, (prior, after, west, east)):
            lacks = jnp.where(device == reader, layer, lacks)
        send[:, 2, 1 + c, :] = lacks
        if c == 2:
            for t, layer in enumerate(layers):
                send[:, 1, t, :] = jnp.broadcast_to(layer, (owners, LANES))
    for copy in copies[6:]:
        copy.wait()


def column(row):
    return jnp.broadcast_to(row, (LANES, row.shape[1])).T


def patch_system(lats, got, road, active, rowed, layered):
    owners = got.shape[0]
    rows = cols = LANES
    size = 4 * LANES
    group = 16
    total = jnp.zeros((4 * group, LANES), F32)
    for first in range(0, owners, group):
        some = slice(first, first + group)
        w, kc, kl, node = [got[some, 0, v, :] for v in range(4)]
        slot = got[some, 2, 0, :].astype(I32)
        node = node.astype(I32)
        lat = node & (cols - 1)
        sender = jnp.where(kc > 0.0, iota(kc.shape, 0) + first, 0)
        pieces = thirds(w) + thirds(kc) + thirds(kl)
        pieces += tuple(x.astype(F32) for x in (node - lat, lat, sender))
        for p, piece in enumerate(pieces):
            rowed[p] = piece
        rowed[12] = (slot >> log2(LANES)).astype(F32)
        rowed[13] = (slot & (LANES - 1)).astype(F32)
        rowed[14:16] = jnp.zeros((2,) + kc.shape, F32)
        left, right = [], []
        for d in range(group):
            stack = rowed[:, d, :]
            high, low = stack[12:13, :], stack[13:14, :]
            left.append(
                jnp.concatenate(
                    [jnp.where(high == float(h), stack, 0.0) for h in range(4)], axis=0
                ).astype(BF16)
            )
            right.append(
                (iota((LANES, LANES), 0) == low.astype(I32)).astype(F32).astype(BF16)
            )
        total = total + lax.dot_general(
            jnp.concatenate(left, axis=1),
            jnp.concatenate(right, axis=1),
            (((1,), (1,)), ((), ())),
            preferred_element_type=F32,
        )
    values = []
    for at in ((0, 1, 2), (3, 4, 5), (6, 7, 8), (9, 10), (10,), (11,)):
        strips = []
        for h in range(4):
            strip = total[group * h + at[0] : group * h + at[0] + 1, :]
            for p in at[1:]:
                strip = strip + total[group * h + p : group * h + p + 1, :]
            strips.append(strip)
        values.append(jnp.concatenate(strips, axis=1))
    w, kc, kl = values[:3]
    node, lat, sender = [x.astype(I32) for x in values[3:]]
    circ = node >> log2(cols)
    after = sender + lats
    after = jnp.where(after >= owners, after - owners, after)
    before = sender - lats
    before = jnp.where(before < 0, before + owners, before)
    side = sender & (lats - 1)
    from_circ = jnp.where(
        circ == rows - 1, after, jnp.where(circ == 0, before + owners, -1)
    )
    from_lat = jnp.where(
        (lat == cols - 1) & (side < lats - 1),
        sender + 1 + 2 * owners,
        jnp.where((lat == 0) & (side > 0), sender - 1 + 3 * owners, -1),
    )
    for t in range(4):
        layered[t] = got[:, 1, t, :]
    layers = layered[...].reshape(owners * 4, LANES)
    layers = jnp.concatenate(thirds(layers), axis=1).astype(BF16)

    def pick(high, low):
        one = (iota((LANES, size), 0) == low).astype(F32).astype(BF16)
        found = jnp.dot(layers, jnp.concatenate([one] * 3, axis=0), preferred_element_type=F32)
        return jnp.sum(
            jnp.where(iota((owners * 4, size), 0) == high, found, 0.0), axis=0, keepdims=True
        )

    diag_k = 2.0 * kc + 2.0 * kl + 0.5
    w = w + (kc * pick(from_circ, lat) + kl * pick(from_lat, circ)) / diag_k
    mask = wide(active, 0, 4).astype(F32)
    return mask, mask * (w - wide(road, 0, 4)), 1.0 / diag_k


def factor_solve(block, mask, rhs, soft, work, press):
    size = rhs.shape[1]
    row = iota((size, 1), 0)
    lane = iota((1, LANES), 1)
    down = column(mask)
    for t in range(size // LANES):
        part = slice(t * LANES, (t + 1) * LANES)
        on = row == lane + t * LANES
        live = mask[:, part]
        work[:, part] = down * live * (block[:, part] + jnp.where(on, soft[:, part], 0.0)) + (
            jnp.where(on, 1.0 - live, 0.0)
        )
    work[:, size:] = column(rhs)
    place = iota((1, size), 1)

    def eliminate(j, carry):
        pivot_row = work[pl.ds(j, 1), :]
        pivot = jnp.sum(jnp.where(place == j, pivot_row[:, :size], 0.0), axis=1, keepdims=True)
        start = pl.multiple_of((j >> log2(LANES)) << log2(LANES), LANES)
        tile = work[:, pl.ds(start, LANES)]
        below = jnp.sum(jnp.where(lane == j - start, tile, 0.0), axis=1, keepdims=True)
        ratio = jnp.where(row > j, below / pivot, 0.0)
        work[...] = work[...] - ratio * pivot_row
        return carry

    lax.fori_loop(0, size, eliminate, 0)

    def substitute(step, x):
        j = size - 1 - step
        now = work[pl.ds(j, 1), :]
        upper = now[:, :size]
        pivot = jnp.sum(jnp.where(place == j, upper, 0.0), axis=1, keepdims=True)
        known = jnp.sum(upper * x, axis=1, keepdims=True)
        return jnp.where(place == j, (now[:, size : size + 1] - known) / pivot, x)

    press[...] = lax.fori_loop(0, size, substitute, jnp.zeros((1, size), F32))


def over(top, bottom):
    return jnp.where(bottom > 0.0, top / bottom, 0.0)


def dot(a, b):
    return jnp.sum(a * b, axis=1, keepdims=True)


def times(block, u, mask, soft):
    size = u.shape[1]
    parts = [jnp.zeros((8, LANES), F32)] * (size // LANES)
    for i in range(0, size, LANES):
        down = column(u[:, i : i + LANES])
        for k in range(size // LANES):
            tile = block[i : i + LANES, k * LANES : (k + 1) * LANES] * down
            parts[k] = parts[k] + jnp.sum(tile.reshape(LANES // 8, 8, LANES), axis=0)
    parts = [jnp.sum(part, axis=0, keepdims=True) for part in parts]
    return mask * (jnp.concatenate(parts, axis=1) + soft * u)


def solve_kernel(
    lats, got, road, active, block, send, work, press, rowed, layered
):
    size = 4 * LANES
    mask, rhs, soft = patch_system(lats, got, road, active, rowed, layered)
    square = iota((LANES, LANES), 0) == iota((LANES, LANES), 1)
    diagonal = jnp.concatenate(
        [
            jnp.sum(
                jnp.where(square, block[i : i + LANES, i : i + LANES], 0.0), axis=0, keepdims=True
            )
            for i in range(0, size, LANES)
        ],
        axis=1,
    )
    scale = mask / (diagonal + soft)
    start = dot(rhs, scale * rhs)
    zero = jnp.zeros((1, size), F32)
    none = jnp.zeros((1, 1), F32)

    def begin(x, r):
        u = scale * r
        return x, r, u, times(block, u, mask, soft), zero, zero, zero, zero, none, none

    def advance(x, r, u, w, z, q, s, p, norm, alpha):
        m = scale * w
        n = times(block, m, mask, soft)
        now = dot(r, u)
        beta = over(now, norm)
        alpha = over(now, dot(w, u) - over(beta * now, alpha))
        z = n + beta * z
        q = m + beta * q
        s = w + beta * s
        p = u + beta * p
        x, r, u, w = x + alpha * p, r - alpha * s, u - alpha * q, w - alpha * z
        return x, r, u, w, z, q, s, p, now, alpha

    def finish(x):
        press[...] = x
        for j in range(4):
            part = x[:, j * LANES : (j + 1) * LANES]
            send[:, j, :] = jnp.broadcast_to(part, (send.shape[0], LANES))

    def gap(x):
        return rhs - times(block, x, mask, soft)

    def small(r, bound):
        return dot(r, scale * r)[0, 0] <= bound * start[0, 0]

    state = begin(zero, rhs)
    for _ in range(CG_FIRST):
        state = advance(*state)
    state = begin(state[0], gap(state[0]))
    for _ in range(CG_AGAIN):
        state = advance(*state)
    first, rest = state[:2]
    finish(first)

    @pl.when(jnp.logical_not(small(rest, FIRST_STOP)))
    def _():
        def going(state):
            step, norm = state[0], state[9]
            return (step < CG_STEPS) & ((step == 0) | (norm[0, 0] > CG_STOP * start[0, 0]))

        def body(state):
            return (state[0] + 1,) + advance(*state[1:])

        x = lax.while_loop(going, body, (0,) + begin(first, gap(first)))[1]
        finish(x)

        @pl.when(jnp.logical_not(small(gap(x), TRUE_STOP)))
        def _():
            def refine(step, x):
                factor_solve(block, mask, gap(x), soft, work, press)
                return x + press[...]

            finish(lax.fori_loop(0, 2, refine, zero))


def finish_kernel(axes, trial, near, node, owner, slot, got, back, out, pressure):
    circs, lats = axes
    owners = got.shape[0]
    rows, cols = trial.shape[1:]
    chunks = node.shape[0]
    my_circ, my_lat = lax.axis_index("circ"), lax.axis_index("lat")
    me = my_circ * lats + my_lat
    after = jnp.where(my_circ == circs - 1, my_lat, me + lats)
    before = jnp.where(my_circ == 0, (circs - 1) * lats + my_lat, me - lats)
    right_dev = jnp.minimum(me + 1, owners - 1)
    left_dev = jnp.maximum(me - 1, 0)
    kc, kl, diag_k = near[0], near[1], near[2]
    row, col = iota((rows, cols), 0), iota((rows, cols), 1)
    for c in range(3):
        down, up = got[after, 2, 1 + c : 2 + c, :], got[before, 2, 1 + c : 2 + c, :]
        east, west = got[right_dev, 2, 1 + c : 2 + c, :], got[left_dev, 2, 1 + c : 2 + c, :]
        east = jnp.where(my_lat < lats - 1, east, 0.0)
        west = jnp.where(my_lat > 0, west, 0.0)
        circ_in = jnp.where(row == rows - 1, down, jnp.where(row == 0, up, 0.0))
        lat_in = jnp.where(
            col == cols - 1, column(east), jnp.where(col == 0, column(west), 0.0)
        )
        out[c] = trial[c] + (kc * circ_in + kl * lat_in) / diag_k

    pressure[...] = back[me]
    answers = jnp.concatenate([back[:, j, :] for j in range(4)], axis=0)
    answers = jnp.concatenate(thirds(answers), axis=1).astype(BF16)
    step = 2 if chunks % 2 == 0 else 1
    span = step * LANES
    left, right = [], []
    for first in range(0, chunks, step):
        nodes = wide(node, first, step)
        where = wide(slot, first, step)
        device = wide(owner, first, step)
        low = where & (LANES - 1)
        source = jnp.where(device < 0, -1, (where >> log2(LANES)) * owners + device)
        one_low = (iota((LANES, span), 0) == low).astype(F32).astype(BF16)
        found = jnp.dot(
            answers, jnp.concatenate([one_low] * 3, axis=0), preferred_element_type=F32
        )
        push = jnp.sum(
            jnp.where(iota((4 * owners, span), 0) == source, found, 0.0), axis=0, keepdims=True
        )
        one_circ = iota((rows, span), 0) == nodes >> log2(cols)
        left.append(
            jnp.concatenate(
                [jnp.where(one_circ, x, 0.0) for x in thirds(push)], axis=0
            ).astype(BF16)
        )
        right.append((iota((cols, span), 0) == (nodes & (cols - 1))).astype(F32).astype(BF16))
    force = lax.dot_general(
        jnp.concatenate(left, axis=1),
        jnp.concatenate(right, axis=1),
        (((1,), (1,)), ((), ())),
        preferred_element_type=F32,
    )
    force = force[:rows] + force[rows : 2 * rows] + force[2 * rows :]
    out[2] = out[2] - force / diag_k


def shards(
    disp, stiff, spin, load, foot_node, foot_dest, foot_slot, foot_count, road, active, influence
):
    circs, lats = lax.axis_size("circ"), lax.axis_size("lat")
    owners = circs * lats
    size = road.shape[0]
    rows, cols = disp.shape[1:]
    assert rows == cols == LANES and size == 4 * LANES and circs > 2 and owners % 16 == 0
    anywhere = pl.BlockSpec(memory_space=pltpu.HBM)
    block = pl.BlockSpec(memory_space=pltpu.VMEM)
    params = pltpu.CompilerParams(vmem_limit_bytes=32 * 1024 * 1024)
    lists = [x.reshape(-1, LANES) for x in (foot_node, foot_dest, foot_slot)]
    listed = jax.ShapeDtypeStruct(lists[0].shape, I32)
    strip = (4, LANES)
    send, trial, near, nodes, owner, slots, roads, actives, blocks = pl.pallas_call(
        functools.partial(pack_kernel, (circs, lats)),
        in_specs=[pl.BlockSpec(memory_space=pltpu.SMEM)] * 2 + [anywhere] * 9,
        out_specs=[block] * 9,
        out_shape=[
            jax.ShapeDtypeStruct((owners, 3, 4, LANES), F32),
            jax.ShapeDtypeStruct((3, rows, cols), F32),
            jax.ShapeDtypeStruct((3, rows, cols), F32),
            listed,
            listed,
            listed,
            jax.ShapeDtypeStruct(strip, F32),
            jax.ShapeDtypeStruct(strip, I32),
            jax.ShapeDtypeStruct((size, size), F32),
        ],
        scratch_shapes=[
            pltpu.VMEM((3, rows, cols), F32),
            pltpu.VMEM((2, rows, cols), F32),
            pltpu.VMEM((3, rows, cols), F32),
            pltpu.VMEM(lists[0].shape, I32),
            pltpu.SemaphoreType.DMA((9,)),
        ],
        compiler_params=params,
        name="pack_rows",
    )(
        foot_count, spin,
        *[
            pltpu.with_memory_space_constraint(x, pltpu.HBM)
            for x in (
                *lists, stiff, disp, load, road.reshape(strip), active.reshape(strip), influence[0]
            )
        ]
    )
    got = lax.all_to_all(send, ("circ", "lat"), split_axis=0, concat_axis=0, tiled=True)
    reply = pl.pallas_call(
        functools.partial(solve_kernel, lats),
        in_specs=[block] * 4,
        out_specs=block,
        out_shape=jax.ShapeDtypeStruct((owners,) + strip, F32),
        scratch_shapes=[
            pltpu.VMEM((size, size + LANES), F32),
            pltpu.VMEM((1, size), F32),
            pltpu.VMEM((16, 16, LANES), F32),
            pltpu.VMEM((4, owners, LANES), F32),
        ],
        compiler_params=params,
        name="solve_patch",
    )(got, roads, actives, blocks)
    back = lax.all_to_all(reply, ("circ", "lat"), split_axis=0, concat_axis=0, tiled=True)
    new_disp, pressure = pl.pallas_call(
        functools.partial(finish_kernel, (circs, lats)),
        in_specs=[block] * 7,
        out_specs=[block, block],
        out_shape=[
            jax.ShapeDtypeStruct(disp.shape, F32),
            jax.ShapeDtypeStruct(strip, F32),
        ],
        compiler_params=params,
        name="finish_nodes",
    )(trial, near, nodes, owner, slots, got, back)
    return (new_disp, pressure.reshape(size))


def solution(mesh):
    return jax.shard_map(
        shards,
        mesh=mesh,
        in_specs=(
            P(None, ("cases", "circ"), "lat"),
            P(None, ("cases", "circ"), "lat"),
            P("cases"),
            P(None, ("cases", "circ"), "lat"),
            P(("cases", "circ", "lat")),
            P(("cases", "circ", "lat")),
            P(("cases", "circ", "lat")),
            P(("cases", "circ", "lat")),
            P(("cases", "circ", "lat")),
            P(("cases", "circ", "lat")),
            P(("cases", "circ", "lat"), None, None),
        ),
        out_specs=(P(None, ("cases", "circ"), "lat"), P(("cases", "circ", "lat"))),
        check_vma=False,
    )
```

```python
import functools

import jax
import jax.numpy as jnp
from jax import lax
from jax.experimental import pallas as pl
from jax.experimental.pallas import tpu as pltpu
from jax.sharding import PartitionSpec as P

F32 = jnp.float32
BF16 = jnp.bfloat16
I32 = jnp.int32
LANES = 128
CG_FIRST = 3
CG_AGAIN = 4
CG_STEPS = 40
CG_STOP = 2e-14
FIRST_STOP = 1e-12
TRUE_STOP = 4e-13


def log2(value):
    assert value > 0 and value & (value - 1) == 0
    return value.bit_length() - 1


def thirds(x):
    high = x.astype(BF16).astype(F32)
    rest = x - high
    mid = rest.astype(BF16).astype(F32)
    return high, mid, rest - mid


def iota(shape, axis):
    return lax.broadcasted_iota(I32, shape, axis)


def wide(ref, first, count):
    return jnp.concatenate([ref[i : i + 1, :] for i in range(first, first + count)], axis=1)


def shifted(u):
    rows, cols = u.shape
    row, col = iota(u.shape, 0), iota(u.shape, 1)
    return (
        jnp.where(row == rows - 1, 0.0, pltpu.roll(u, rows - 1, 0)),
        jnp.where(row == 0, 0.0, pltpu.roll(u, 1, 0)),
        jnp.where(col == cols - 1, 0.0, pltpu.roll(u, cols - 1, 1)),
        jnp.where(col == 0, 0.0, pltpu.roll(u, 1, 1)),
    )


def edges(u):
    rows, cols = u.shape
    turned = u.T
    return [u[0:1, :], u[rows - 1 : rows, :], turned[0:1, :], turned[cols - 1 : cols, :]]


def pack_kernel(
    axes, count, spin, node, dest, slot, stiff, disp, load, road, active, block,
    send, trial, near, nodes, owner, slots, roads, actives, blocks,
    u, springs, loads, dests, sems,
):
    circs, lats = axes
    owners = send.shape[0]
    rows, cols = disp.shape[1:]
    chunks = node.shape[0]
    pairs = [
        (node, nodes), (dest, dests), (slot, slots), (stiff, springs), (disp, u), (load, loads), (road, roads), (active, actives),
        (block, blocks),
    ]
    copies = [pltpu.make_async_copy(a, b, sems.at[i]) for i, (a, b) in enumerate(pairs)]
    for copy in copies:
        copy.start()
    for copy in copies[:3]:
        copy.wait()

    width = 2 * LANES if chunks % 2 == 0 else LANES
    step = width // LANES
    to, tos = [], []
    for i in range(chunks):
        live = iota((1, LANES), 1) + i * LANES < count[0]
        target = jnp.where(live, dests[i : i + 1, :], -1)
        owner[i : i + 1, :] = target
        to.append(iota((owners, LANES), 0) == target)
        tos.append(to[i].astype(F32).astype(BF16))
    before = iota((LANES, 2 * LANES), 0) < iota((LANES, 2 * LANES), 1)
    ranks = jnp.dot(
        jnp.concatenate(tos, axis=0), before.astype(F32).astype(BF16), preferred_element_type=F32
    )
    passed = jnp.zeros((owners, LANES), F32)
    right = []
    for i in range(chunks):
        mine = ranks[i * owners : (i + 1) * owners]
        rank = jnp.sum(
            jnp.where(to[i], mine[:, :LANES] + passed, 0.0), axis=0, keepdims=True
        ).astype(I32)
        passed = passed + mine[:, LANES:]
        right.append((iota((LANES, LANES), 0) == rank).astype(F32).astype(BF16))

    for copy in copies[3:6]:
        copy.wait()
    kc = springs[0] - spin[0]
    kl = springs[1]
    diag_k = 2.0 * kc + 2.0 * kl + 0.5
    near[0] = kc
    near[1] = kl
    near[2] = diag_k
    for c in range(3):
        own = u[c]
        u_next, u_prev, u_right, u_left = shifted(own)
        force = kc * (2.0 * own - u_next - u_prev) + kl * (2.0 * own - u_right - u_left) + 0.5 * own
        trial[c] = own + (loads[c] - force) / diag_k
    table = jnp.concatenate(
        [jnp.concatenate(thirds(x), axis=1) for x in (trial[2], kc, kl)], axis=0
    ).astype(BF16)
    left = []
    for first in range(0, chunks, step):
        place = wide(nodes, first, step)
        circ = place >> log2(cols)
        lat = place & (cols - 1)
        one_lat = (iota((cols, width), 0) == lat).astype(F32).astype(BF16)
        picked = jnp.dot(
            table, jnp.concatenate([one_lat] * 3, axis=0), preferred_element_type=F32
        )
        one_circ = iota((rows, width), 0) == circ
        pieces = []
        for k in range(3):
            found = picked[k * rows : (k + 1) * rows]
            pieces += thirds(jnp.sum(jnp.where(one_circ, found, 0.0), axis=0, keepdims=True))
        where = wide(slots, first, step)
        low = where & (LANES - 1)
        pieces += [x.astype(F32) for x in (circ * cols, lat, where - low, low)]
        here = jnp.concatenate(to[first : first + step], axis=1)
        left.append(
            jnp.concatenate([jnp.where(here, x, 0.0) for x in pieces], axis=0).astype(BF16)
        )
    spread = lax.dot_general(
        jnp.concatenate(left, axis=1),
        jnp.concatenate(right, axis=1),
        (((1,), (1,)), ((), ())),
        preferred_element_type=F32,
    )
    part = [spread[i * owners : (i + 1) * owners] for i in range(13)]
    for v in range(3):
        send[:, v, 0, :] = part[3 * v] + part[3 * v + 1] + part[3 * v + 2]
    send[:, 3, 0, :] = part[9] + part[10]
    send[:, 8, 0, :] = part[11] + part[12]

    my_circ, my_lat = lax.axis_index("circ"), lax.axis_index("lat")
    me = my_circ * lats + my_lat
    after = jnp.where(my_circ == circs - 1, my_lat, me + lats)
    prior = jnp.where(my_circ == 0, (circs - 1) * lats + my_lat, me - lats)
    east = jnp.where(my_lat < lats - 1, me + 1, -1)
    west = jnp.where(my_lat > 0, me - 1, -1)
    device = iota((owners, LANES), 0)
    for c in range(3):
        layers = edges(u[c])
        if c == 2:
            for t, layer in enumerate(layers):
                send[:, 4 + t, 0, :] = jnp.broadcast_to(layer, (owners, LANES))
            continue
        lacks = jnp.zeros((owners, LANES), F32)
        for layer, reader in zip(layers, (prior, after, west, east)):
            lacks = jnp.where(device == reader, layer, lacks)
        send[:, 9 + c, 0, :] = lacks
    for copy in copies[6:]:
        copy.wait()


def column(row):
    return jnp.broadcast_to(row, (LANES, row.shape[1])).T


def patch_system(lats, got, road, active, rowed, layered):
    owners = got.shape[0]
    rows = cols = LANES
    size = 4 * LANES
    group = 16
    total = jnp.zeros((4 * group, LANES), F32)
    for first in range(0, owners, group):
        some = slice(first, first + group)
        w, kc, kl, node = [got[some, v, 0, :] for v in range(4)]
        slot = got[some, 8, 0, :].astype(I32)
        node = node.astype(I32)
        lat = node & (cols - 1)
        sender = jnp.where(kc > 0.0, iota(kc.shape, 0) + first, 0)
        pieces = thirds(w) + thirds(kc) + thirds(kl)
        pieces += tuple(x.astype(F32) for x in (node - lat, lat, sender))
        for p, piece in enumerate(pieces):
            rowed[p] = piece
        rowed[12] = (slot >> log2(LANES)).astype(F32)
        rowed[13] = (slot & (LANES - 1)).astype(F32)
        rowed[14:16] = jnp.zeros((2,) + kc.shape, F32)
        left, right = [], []
        for d in range(group):
            stack = rowed[:, d, :]
            high, low = stack[12:13, :], stack[13:14, :]
            left.append(
                jnp.concatenate(
                    [jnp.where(high == float(h), stack, 0.0) for h in range(4)], axis=0
                ).astype(BF16)
            )
            right.append(
                (iota((LANES, LANES), 0) == low.astype(I32)).astype(F32).astype(BF16)
            )
        total = total + lax.dot_general(
            jnp.concatenate(left, axis=1),
            jnp.concatenate(right, axis=1),
            (((1,), (1,)), ((), ())),
            preferred_element_type=F32,
        )
    values = []
    for at in ((0, 1, 2), (3, 4, 5), (6, 7, 8), (9, 10), (10,), (11,)):
        strips = []
        for h in range(4):
            strip = total[group * h + at[0] : group * h + at[0] + 1, :]
            for p in at[1:]:
                strip = strip + total[group * h + p : group * h + p + 1, :]
            strips.append(strip)
        values.append(jnp.concatenate(strips, axis=1))
    w, kc, kl = values[:3]
    node, lat, sender = [x.astype(I32) for x in values[3:]]
    circ = node >> log2(cols)
    after = sender + lats
    after = jnp.where(after >= owners, after - owners, after)
    before = sender - lats
    before = jnp.where(before < 0, before + owners, before)
    side = sender & (lats - 1)
    from_circ = jnp.where(
        circ == rows - 1, after, jnp.where(circ == 0, before + owners, -1)
    )
    from_lat = jnp.where(
        (lat == cols - 1) & (side < lats - 1),
        sender + 1 + 2 * owners,
        jnp.where((lat == 0) & (side > 0), sender - 1 + 3 * owners, -1),
    )
    for t in range(4):
        layered[t] = got[:, 4 + t, 0, :]
    layers = layered[...].reshape(owners * 4, LANES)
    layers = jnp.concatenate(thirds(layers), axis=1).astype(BF16)

    def pick(high, low):
        one = (iota((LANES, size), 0) == low).astype(F32).astype(BF16)
        found = jnp.dot(layers, jnp.concatenate([one] * 3, axis=0), preferred_element_type=F32)
        return jnp.sum(
            jnp.where(iota((owners * 4, size), 0) == high, found, 0.0), axis=0, keepdims=True
        )

    diag_k = 2.0 * kc + 2.0 * kl + 0.5
    w = w + (kc * pick(from_circ, lat) + kl * pick(from_lat, circ)) / diag_k
    mask = wide(active, 0, 4).astype(F32)
    return mask, mask * (w - wide(road, 0, 4)), 1.0 / diag_k


def factor_solve(block, mask, rhs, soft, work, press):
    size = rhs.shape[1]
    row = iota((size, 1), 0)
    lane = iota((1, LANES), 1)
    down = column(mask)
    for t in range(size // LANES):
        part = slice(t * LANES, (t + 1) * LANES)
        on = row == lane + t * LANES
        live = mask[:, part]
        work[:, part] = down * live * (block[:, part] + jnp.where(on, soft[:, part], 0.0)) + (
            jnp.where(on, 1.0 - live, 0.0)
        )
    work[:, size:] = column(rhs)
    place = iota((1, size), 1)

    def eliminate(j, carry):
        pivot_row = work[pl.ds(j, 1), :]
        pivot = jnp.sum(jnp.where(place == j, pivot_row[:, :size], 0.0), axis=1, keepdims=True)
        start = pl.multiple_of((j >> log2(LANES)) << log2(LANES), LANES)
        tile = work[:, pl.ds(start, LANES)]
        below = jnp.sum(jnp.where(lane == j - start, tile, 0.0), axis=1, keepdims=True)
        ratio = jnp.where(row > j, below / pivot, 0.0)
        work[...] = work[...] - ratio * pivot_row
        return carry

    lax.fori_loop(0, size, eliminate, 0)

    def substitute(step, x):
        j = size - 1 - step
        now = work[pl.ds(j, 1), :]
        upper = now[:, :size]
        pivot = jnp.sum(jnp.where(place == j, upper, 0.0), axis=1, keepdims=True)
        known = jnp.sum(upper * x, axis=1, keepdims=True)
        return jnp.where(place == j, (now[:, size : size + 1] - known) / pivot, x)

    press[...] = lax.fori_loop(0, size, substitute, jnp.zeros((1, size), F32))


def over(top, bottom):
    return jnp.where(bottom > 0.0, top / bottom, 0.0)


def dot(a, b):
    return jnp.sum(a * b, axis=1, keepdims=True)


def times(block, u, mask, soft):
    size = u.shape[1]
    parts = [jnp.zeros((8, LANES), F32)] * (size // LANES)
    for i in range(0, size, LANES):
        down = column(u[:, i : i + LANES])
        for k in range(size // LANES):
            tile = block[i : i + LANES, k * LANES : (k + 1) * LANES] * down
            parts[k] = parts[k] + jnp.sum(tile.reshape(LANES // 8, 8, LANES), axis=0)
    parts = [jnp.sum(part, axis=0, keepdims=True) for part in parts]
    return mask * (jnp.concatenate(parts, axis=1) + soft * u)


def solve_kernel(
    lats, got, road, active, block, send, work, press, rowed, layered
):
    size = 4 * LANES
    mask, rhs, soft = patch_system(lats, got, road, active, rowed, layered)
    square = iota((LANES, LANES), 0) == iota((LANES, LANES), 1)
    diagonal = jnp.concatenate(
        [
            jnp.sum(
                jnp.where(square, block[i : i + LANES, i : i + LANES], 0.0), axis=0, keepdims=True
            )
            for i in range(0, size, LANES)
        ],
        axis=1,
    )
    scale = mask / (diagonal + soft)
    start = dot(rhs, scale * rhs)
    zero = jnp.zeros((1, size), F32)
    none = jnp.zeros((1, 1), F32)

    def begin(x, r):
        u = scale * r
        return x, r, u, times(block, u, mask, soft), zero, zero, zero, zero, none, none

    def advance(x, r, u, w, z, q, s, p, norm, alpha):
        m = scale * w
        n = times(block, m, mask, soft)
        now = dot(r, u)
        beta = over(now, norm)
        alpha = over(now, dot(w, u) - over(beta * now, alpha))
        z = n + beta * z
        q = m + beta * q
        s = w + beta * s
        p = u + beta * p
        x, r, u, w = x + alpha * p, r - alpha * s, u - alpha * q, w - alpha * z
        return x, r, u, w, z, q, s, p, now, alpha

    def finish(x):
        press[...] = x
        for j in range(4):
            part = x[:, j * LANES : (j + 1) * LANES]
            send[:, j, :] = jnp.broadcast_to(part, (send.shape[0], LANES))

    def gap(x):
        return rhs - times(block, x, mask, soft)

    def small(r, bound):
        return dot(r, scale * r)[0, 0] <= bound * start[0, 0]

    state = begin(zero, rhs)
    for _ in range(CG_FIRST):
        state = advance(*state)
    state = begin(state[0], gap(state[0]))
    for _ in range(CG_AGAIN):
        state = advance(*state)
    first, rest = state[:2]
    finish(first)

    @pl.when(jnp.logical_not(small(rest, FIRST_STOP)))
    def _():
        def going(state):
            step, norm = state[0], state[9]
            return (step < CG_STEPS) & ((step == 0) | (norm[0, 0] > CG_STOP * start[0, 0]))

        def body(state):
            return (state[0] + 1,) + advance(*state[1:])

        x = lax.while_loop(going, body, (0,) + begin(first, gap(first)))[1]
        finish(x)

        @pl.when(jnp.logical_not(small(gap(x), TRUE_STOP)))
        def _():
            def refine(step, x):
                factor_solve(block, mask, gap(x), soft, work, press)
                return x + press[...]

            finish(lax.fori_loop(0, 2, refine, zero))


def finish_kernel(axes, trial, near, node, owner, slot, got, back, out, pressure):
    circs, lats = axes
    owners = got.shape[0]
    rows, cols = trial.shape[1:]
    chunks = node.shape[0]
    my_circ, my_lat = lax.axis_index("circ"), lax.axis_index("lat")
    me = my_circ * lats + my_lat
    after = jnp.where(my_circ == circs - 1, my_lat, me + lats)
    before = jnp.where(my_circ == 0, (circs - 1) * lats + my_lat, me - lats)
    right_dev = jnp.minimum(me + 1, owners - 1)
    left_dev = jnp.maximum(me - 1, 0)
    kc, kl, diag_k = near[0], near[1], near[2]
    row, col = iota((rows, cols), 0), iota((rows, cols), 1)
    for c in range(3):
        rows_at = (9 + c,) * 4 if c < 2 else (4, 5, 6, 7)
        down, up, east, west = [
            got[device, at] for device, at in zip((after, before, right_dev, left_dev), rows_at)
        ]
        east = jnp.where(my_lat < lats - 1, east, 0.0)
        west = jnp.where(my_lat > 0, west, 0.0)
        circ_in = jnp.where(row == rows - 1, down, jnp.where(row == 0, up, 0.0))
        lat_in = jnp.where(
            col == cols - 1, column(east), jnp.where(col == 0, column(west), 0.0)
        )
        out[c] = trial[c] + (kc * circ_in + kl * lat_in) / diag_k

    pressure[...] = back[me]
    answers = jnp.concatenate([back[:, j, :] for j in range(4)], axis=0)
    answers = jnp.concatenate(thirds(answers), axis=1).astype(BF16)
    step = 2 if chunks % 2 == 0 else 1
    span = step * LANES
    left, right = [], []
    for first in range(0, chunks, step):
        nodes = wide(node, first, step)
        where = wide(slot, first, step)
        device = wide(owner, first, step)
        low = where & (LANES - 1)
        source = jnp.where(device < 0, -1, (where >> log2(LANES)) * owners + device)
        one_low = (iota((LANES, span), 0) == low).astype(F32).astype(BF16)
        found = jnp.dot(
            answers, jnp.concatenate([one_low] * 3, axis=0), preferred_element_type=F32
        )
        push = jnp.sum(
            jnp.where(iota((4 * owners, span), 0) == source, found, 0.0), axis=0, keepdims=True
        )
        one_circ = iota((rows, span), 0) == nodes >> log2(cols)
        left.append(
            jnp.concatenate(
                [jnp.where(one_circ, x, 0.0) for x in thirds(push)], axis=0
            ).astype(BF16)
        )
        right.append((iota((cols, span), 0) == (nodes & (cols - 1))).astype(F32).astype(BF16))
    force = lax.dot_general(
        jnp.concatenate(left, axis=1),
        jnp.concatenate(right, axis=1),
        (((1,), (1,)), ((), ())),
        preferred_element_type=F32,
    )
    force = force[:rows] + force[rows : 2 * rows] + force[2 * rows :]
    out[2] = out[2] - force / diag_k


def shards(
    disp, stiff, spin, load, foot_node, foot_dest, foot_slot, foot_count, road, active, influence
):
    circs, lats = lax.axis_size("circ"), lax.axis_size("lat")
    owners = circs * lats
    size = road.shape[0]
    rows, cols = disp.shape[1:]
    assert rows == cols == LANES and size == 4 * LANES and circs > 2 and owners % 16 == 0
    anywhere = pl.BlockSpec(memory_space=pltpu.HBM)
    block = pl.BlockSpec(memory_space=pltpu.VMEM)
    params = pltpu.CompilerParams(vmem_limit_bytes=32 * 1024 * 1024)
    lists = [x.reshape(-1, LANES) for x in (foot_node, foot_dest, foot_slot)]
    listed = jax.ShapeDtypeStruct(lists[0].shape, I32)
    strip = (4, LANES)
    send, trial, near, nodes, owner, slots, roads, actives, blocks = pl.pallas_call(
        functools.partial(pack_kernel, (circs, lats)),
        in_specs=[pl.BlockSpec(memory_space=pltpu.SMEM)] * 2 + [anywhere] * 9,
        out_specs=[block] * 9,
        out_shape=[
            jax.ShapeDtypeStruct((owners, 11, 1, LANES), F32),
            jax.ShapeDtypeStruct((3, rows, cols), F32),
            jax.ShapeDtypeStruct((3, rows, cols), F32),
            listed,
            listed,
            listed,
            jax.ShapeDtypeStruct(strip, F32),
            jax.ShapeDtypeStruct(strip, I32),
            jax.ShapeDtypeStruct((size, size), F32),
        ],
        scratch_shapes=[
            pltpu.VMEM((3, rows, cols), F32),
            pltpu.VMEM((2, rows, cols), F32),
            pltpu.VMEM((3, rows, cols), F32),
            pltpu.VMEM(lists[0].shape, I32),
            pltpu.SemaphoreType.DMA((9,)),
        ],
        compiler_params=params,
        name="pack_rows",
    )(
        foot_count, spin,
        *[
            pltpu.with_memory_space_constraint(x, pltpu.HBM)
            for x in (
                *lists, stiff, disp, load, road.reshape(strip), active.reshape(strip), influence[0]
            )
        ]
    )
    got = lax.all_to_all(send, ("circ", "lat"), split_axis=0, concat_axis=0, tiled=True)
    reply = pl.pallas_call(
        functools.partial(solve_kernel, lats),
        in_specs=[block] * 4,
        out_specs=block,
        out_shape=jax.ShapeDtypeStruct((owners,) + strip, F32),
        scratch_shapes=[
            pltpu.VMEM((size, size + LANES), F32),
            pltpu.VMEM((1, size), F32),
            pltpu.VMEM((16, 16, LANES), F32),
            pltpu.VMEM((4, owners, LANES), F32),
        ],
        compiler_params=params,
        name="solve_patch",
    )(got, roads, actives, blocks)
    back = lax.all_to_all(reply, ("circ", "lat"), split_axis=0, concat_axis=0, tiled=True)
    new_disp, pressure = pl.pallas_call(
        functools.partial(finish_kernel, (circs, lats)),
        in_specs=[block] * 7,
        out_specs=[block, block],
        out_shape=[
            jax.ShapeDtypeStruct(disp.shape, F32),
            jax.ShapeDtypeStruct(strip, F32),
        ],
        compiler_params=params,
        name="finish_nodes",
    )(trial, near, nodes, owner, slots, got, back)
    return (new_disp, pressure.reshape(size))


def solution(mesh):
    return jax.shard_map(
        shards,
        mesh=mesh,
        in_specs=(
            P(None, ("cases", "circ"), "lat"),
            P(None, ("cases", "circ"), "lat"),
            P("cases"),
            P(None, ("cases", "circ"), "lat"),
            P(("cases", "circ", "lat")),
            P(("cases", "circ", "lat")),
            P(("cases", "circ", "lat")),
            P(("cases", "circ", "lat")),
            P(("cases", "circ", "lat")),
            P(("cases", "circ", "lat")),
            P(("cases", "circ", "lat"), None, None),
        ),
        out_specs=(P(None, ("cases", "circ"), "lat"), P(("cases", "circ", "lat"))),
        check_vma=False,
    )
```

```python
import functools

import jax
import jax.numpy as jnp
from jax import lax
from jax.experimental import pallas as pl
from jax.experimental.pallas import tpu as pltpu
from jax.sharding import PartitionSpec as P

F32 = jnp.float32
BF16 = jnp.bfloat16
I32 = jnp.int32
LANES = 128
CG_FIRST = 3
CG_AGAIN = 4
CG_STEPS = 40
CG_STOP = 2e-14
FIRST_STOP = 1e-12
TRUE_STOP = 4e-13


def log2(value):
    assert value > 0 and value & (value - 1) == 0
    return value.bit_length() - 1


def thirds(x):
    high = x.astype(BF16).astype(F32)
    rest = x - high
    mid = rest.astype(BF16).astype(F32)
    return high, mid, rest - mid


def iota(shape, axis):
    return lax.broadcasted_iota(I32, shape, axis)


def wide(ref, first, count):
    return jnp.concatenate([ref[i : i + 1, :] for i in range(first, first + count)], axis=1)


def shifted(u):
    rows, cols = u.shape
    row, col = iota(u.shape, 0), iota(u.shape, 1)
    return (
        jnp.where(row == rows - 1, 0.0, pltpu.roll(u, rows - 1, 0)),
        jnp.where(row == 0, 0.0, pltpu.roll(u, 1, 0)),
        jnp.where(col == cols - 1, 0.0, pltpu.roll(u, cols - 1, 1)),
        jnp.where(col == 0, 0.0, pltpu.roll(u, 1, 1)),
    )


def edges(u):
    rows, cols = u.shape
    turned = u.T
    return [u[0:1, :], u[rows - 1 : rows, :], turned[0:1, :], turned[cols - 1 : cols, :]]


def pack_kernel(
    axes, count, spin, node, dest, slot, stiff, disp, load, road, active, block,
    send, trial, near, nodes, owner, slots, roads, actives, blocks, late,
    u, springs, loads, dests, sems,
):
    circs, lats = axes
    owners = send.shape[0]
    rows, cols = disp.shape[1:]
    chunks = node.shape[0]
    pairs = [
        (node, nodes), (dest, dests), (slot, slots), (stiff, springs), (disp, u), (load, loads), (road, roads), (active, actives),
        (block, blocks),
    ]
    copies = [pltpu.make_async_copy(a, b, sems.at[i]) for i, (a, b) in enumerate(pairs)]
    for copy in copies:
        copy.start()
    for copy in copies[:3]:
        copy.wait()

    width = 2 * LANES if chunks % 2 == 0 else LANES
    step = width // LANES
    to, tos = [], []
    for i in range(chunks):
        live = iota((1, LANES), 1) + i * LANES < count[0]
        target = jnp.where(live, dests[i : i + 1, :], -1)
        owner[i : i + 1, :] = target
        to.append(iota((owners, LANES), 0) == target)
        tos.append(to[i].astype(F32).astype(BF16))
    before = iota((LANES, 2 * LANES), 0) < iota((LANES, 2 * LANES), 1)
    ranks = jnp.dot(
        jnp.concatenate(tos, axis=0), before.astype(F32).astype(BF16), preferred_element_type=F32
    )
    passed = jnp.zeros((owners, LANES), F32)
    right = []
    for i in range(chunks):
        mine = ranks[i * owners : (i + 1) * owners]
        rank = jnp.sum(
            jnp.where(to[i], mine[:, :LANES] + passed, 0.0), axis=0, keepdims=True
        ).astype(I32)
        passed = passed + mine[:, LANES:]
        right.append((iota((LANES, LANES), 0) == rank).astype(F32).astype(BF16))

    for copy in copies[3:6]:
        copy.wait()
    kc = springs[0] - spin[0]
    kl = springs[1]
    diag_k = 2.0 * kc + 2.0 * kl + 0.5
    near[0] = kc
    near[1] = kl
    near[2] = diag_k
    for c in range(3):
        own = u[c]
        u_next, u_prev, u_right, u_left = shifted(own)
        force = kc * (2.0 * own - u_next - u_prev) + kl * (2.0 * own - u_right - u_left) + 0.5 * own
        trial[c] = own + (loads[c] - force) / diag_k
    table = jnp.concatenate(
        [jnp.concatenate(thirds(x), axis=1) for x in (trial[2], kc, kl)], axis=0
    ).astype(BF16)
    left = []
    for first in range(0, chunks, step):
        place = wide(nodes, first, step)
        circ = place >> log2(cols)
        lat = place & (cols - 1)
        one_lat = (iota((cols, width), 0) == lat).astype(F32).astype(BF16)
        picked = jnp.dot(
            table, jnp.concatenate([one_lat] * 3, axis=0), preferred_element_type=F32
        )
        one_circ = iota((rows, width), 0) == circ
        pieces = []
        for k in range(3):
            found = picked[k * rows : (k + 1) * rows]
            pieces += thirds(jnp.sum(jnp.where(one_circ, found, 0.0), axis=0, keepdims=True))
        where = wide(slots, first, step)
        low = where & (LANES - 1)
        pieces += [x.astype(F32) for x in (circ * cols, lat, where - low, low)]
        here = jnp.concatenate(to[first : first + step], axis=1)
        left.append(
            jnp.concatenate([jnp.where(here, x, 0.0) for x in pieces], axis=0).astype(BF16)
        )
    spread = lax.dot_general(
        jnp.concatenate(left, axis=1),
        jnp.concatenate(right, axis=1),
        (((1,), (1,)), ((), ())),
        preferred_element_type=F32,
    )
    part = [spread[i * owners : (i + 1) * owners] for i in range(13)]
    for v in range(3):
        send[:, v, 0, :] = part[3 * v] + part[3 * v + 1] + part[3 * v + 2]
    send[:, 3, 0, :] = part[9] + part[10]
    send[:, 8, 0, :] = part[11] + part[12]

    my_circ, my_lat = lax.axis_index("circ"), lax.axis_index("lat")
    me = my_circ * lats + my_lat
    after = jnp.where(my_circ == circs - 1, my_lat, me + lats)
    prior = jnp.where(my_circ == 0, (circs - 1) * lats + my_lat, me - lats)
    east = jnp.where(my_lat < lats - 1, me + 1, -1)
    west = jnp.where(my_lat > 0, me - 1, -1)
    device = iota((owners, LANES), 0)
    for c in range(3):
        layers = edges(u[c])
        if c == 2:
            for t, layer in enumerate(layers):
                send[:, 4 + t, 0, :] = jnp.broadcast_to(layer, (owners, LANES))
            continue
        lacks = jnp.zeros((owners, LANES), F32)
        for layer, reader in zip(layers, (prior, after, west, east)):
            lacks = jnp.where(device == reader, layer, lacks)
        late[c] = lacks
    for copy in copies[6:]:
        copy.wait()


def column(row):
    return jnp.broadcast_to(row, (LANES, row.shape[1])).T


def patch_system(lats, got, road, active, rowed, layered):
    owners = got.shape[0]
    rows = cols = LANES
    size = 4 * LANES
    group = 16
    total = jnp.zeros((4 * group, LANES), F32)
    for first in range(0, owners, group):
        some = slice(first, first + group)
        w, kc, kl, node = [got[some, v, 0, :] for v in range(4)]
        slot = got[some, 8, 0, :].astype(I32)
        node = node.astype(I32)
        lat = node & (cols - 1)
        sender = jnp.where(kc > 0.0, iota(kc.shape, 0) + first, 0)
        pieces = thirds(w) + thirds(kc) + thirds(kl)
        pieces += tuple(x.astype(F32) for x in (node - lat, lat, sender))
        for p, piece in enumerate(pieces):
            rowed[p] = piece
        rowed[12] = (slot >> log2(LANES)).astype(F32)
        rowed[13] = (slot & (LANES - 1)).astype(F32)
        rowed[14:16] = jnp.zeros((2,) + kc.shape, F32)
        left, right = [], []
        for d in range(group):
            stack = rowed[:, d, :]
            high, low = stack[12:13, :], stack[13:14, :]
            left.append(
                jnp.concatenate(
                    [jnp.where(high == float(h), stack, 0.0) for h in range(4)], axis=0
                ).astype(BF16)
            )
            right.append(
                (iota((LANES, LANES), 0) == low.astype(I32)).astype(F32).astype(BF16)
            )
        total = total + lax.dot_general(
            jnp.concatenate(left, axis=1),
            jnp.concatenate(right, axis=1),
            (((1,), (1,)), ((), ())),
            preferred_element_type=F32,
        )
    values = []
    for at in ((0, 1, 2), (3, 4, 5), (6, 7, 8), (9, 10), (10,), (11,)):
        strips = []
        for h in range(4):
            strip = total[group * h + at[0] : group * h + at[0] + 1, :]
            for p in at[1:]:
                strip = strip + total[group * h + p : group * h + p + 1, :]
            strips.append(strip)
        values.append(jnp.concatenate(strips, axis=1))
    w, kc, kl = values[:3]
    node, lat, sender = [x.astype(I32) for x in values[3:]]
    circ = node >> log2(cols)
    after = sender + lats
    after = jnp.where(after >= owners, after - owners, after)
    before = sender - lats
    before = jnp.where(before < 0, before + owners, before)
    side = sender & (lats - 1)
    from_circ = jnp.where(
        circ == rows - 1, after, jnp.where(circ == 0, before + owners, -1)
    )
    from_lat = jnp.where(
        (lat == cols - 1) & (side < lats - 1),
        sender + 1 + 2 * owners,
        jnp.where((lat == 0) & (side > 0), sender - 1 + 3 * owners, -1),
    )
    for t in range(4):
        layered[t] = got[:, 4 + t, 0, :]
    layers = layered[...].reshape(owners * 4, LANES)
    layers = jnp.concatenate(thirds(layers), axis=1).astype(BF16)

    def pick(high, low):
        one = (iota((LANES, size), 0) == low).astype(F32).astype(BF16)
        found = jnp.dot(layers, jnp.concatenate([one] * 3, axis=0), preferred_element_type=F32)
        return jnp.sum(
            jnp.where(iota((owners * 4, size), 0) == high, found, 0.0), axis=0, keepdims=True
        )

    diag_k = 2.0 * kc + 2.0 * kl + 0.5
    w = w + (kc * pick(from_circ, lat) + kl * pick(from_lat, circ)) / diag_k
    mask = wide(active, 0, 4).astype(F32)
    return mask, mask * (w - wide(road, 0, 4)), 1.0 / diag_k


def factor_solve(block, mask, rhs, soft, work, press):
    size = rhs.shape[1]
    row = iota((size, 1), 0)
    lane = iota((1, LANES), 1)
    down = column(mask)
    for t in range(size // LANES):
        part = slice(t * LANES, (t + 1) * LANES)
        on = row == lane + t * LANES
        live = mask[:, part]
        work[:, part] = down * live * (block[:, part] + jnp.where(on, soft[:, part], 0.0)) + (
            jnp.where(on, 1.0 - live, 0.0)
        )
    work[:, size:] = column(rhs)
    place = iota((1, size), 1)

    def eliminate(j, carry):
        pivot_row = work[pl.ds(j, 1), :]
        pivot = jnp.sum(jnp.where(place == j, pivot_row[:, :size], 0.0), axis=1, keepdims=True)
        start = pl.multiple_of((j >> log2(LANES)) << log2(LANES), LANES)
        tile = work[:, pl.ds(start, LANES)]
        below = jnp.sum(jnp.where(lane == j - start, tile, 0.0), axis=1, keepdims=True)
        ratio = jnp.where(row > j, below / pivot, 0.0)
        work[...] = work[...] - ratio * pivot_row
        return carry

    lax.fori_loop(0, size, eliminate, 0)

    def substitute(step, x):
        j = size - 1 - step
        now = work[pl.ds(j, 1), :]
        upper = now[:, :size]
        pivot = jnp.sum(jnp.where(place == j, upper, 0.0), axis=1, keepdims=True)
        known = jnp.sum(upper * x, axis=1, keepdims=True)
        return jnp.where(place == j, (now[:, size : size + 1] - known) / pivot, x)

    press[...] = lax.fori_loop(0, size, substitute, jnp.zeros((1, size), F32))


def over(top, bottom):
    return jnp.where(bottom > 0.0, top / bottom, 0.0)


def dot(a, b):
    return jnp.sum(a * b, axis=1, keepdims=True)


def times(block, u, mask, soft):
    size = u.shape[1]
    parts = [jnp.zeros((8, LANES), F32)] * (size // LANES)
    for i in range(0, size, LANES):
        down = column(u[:, i : i + LANES])
        for k in range(size // LANES):
            tile = block[i : i + LANES, k * LANES : (k + 1) * LANES] * down
            parts[k] = parts[k] + jnp.sum(tile.reshape(LANES // 8, 8, LANES), axis=0)
    parts = [jnp.sum(part, axis=0, keepdims=True) for part in parts]
    return mask * (jnp.concatenate(parts, axis=1) + soft * u)


def solve_kernel(
    lats, got, road, active, block, late, send, work, press, rowed, layered
):
    size = 4 * LANES
    for c in range(2):
        send[:, 4 + c, 0, :] = late[c]
    mask, rhs, soft = patch_system(lats, got, road, active, rowed, layered)
    square = iota((LANES, LANES), 0) == iota((LANES, LANES), 1)
    diagonal = jnp.concatenate(
        [
            jnp.sum(
                jnp.where(square, block[i : i + LANES, i : i + LANES], 0.0), axis=0, keepdims=True
            )
            for i in range(0, size, LANES)
        ],
        axis=1,
    )
    scale = mask / (diagonal + soft)
    start = dot(rhs, scale * rhs)
    zero = jnp.zeros((1, size), F32)
    none = jnp.zeros((1, 1), F32)

    def begin(x, r):
        u = scale * r
        return x, r, u, times(block, u, mask, soft), zero, zero, zero, zero, none, none

    def advance(x, r, u, w, z, q, s, p, norm, alpha):
        m = scale * w
        n = times(block, m, mask, soft)
        now = dot(r, u)
        beta = over(now, norm)
        alpha = over(now, dot(w, u) - over(beta * now, alpha))
        z = n + beta * z
        q = m + beta * q
        s = w + beta * s
        p = u + beta * p
        x, r, u, w = x + alpha * p, r - alpha * s, u - alpha * q, w - alpha * z
        return x, r, u, w, z, q, s, p, now, alpha

    def finish(x):
        press[...] = x
        for j in range(4):
            part = x[:, j * LANES : (j + 1) * LANES]
            send[:, j, 0, :] = jnp.broadcast_to(part, (send.shape[0], LANES))

    def gap(x):
        return rhs - times(block, x, mask, soft)

    def small(r, bound):
        return dot(r, scale * r)[0, 0] <= bound * start[0, 0]

    state = begin(zero, rhs)
    for _ in range(CG_FIRST):
        state = advance(*state)
    state = begin(state[0], gap(state[0]))
    for _ in range(CG_AGAIN):
        state = advance(*state)
    first, rest = state[:2]
    finish(first)

    @pl.when(jnp.logical_not(small(rest, FIRST_STOP)))
    def _():
        def going(state):
            step, norm = state[0], state[9]
            return (step < CG_STEPS) & ((step == 0) | (norm[0, 0] > CG_STOP * start[0, 0]))

        def body(state):
            return (state[0] + 1,) + advance(*state[1:])

        x = lax.while_loop(going, body, (0,) + begin(first, gap(first)))[1]
        finish(x)

        @pl.when(jnp.logical_not(small(gap(x), TRUE_STOP)))
        def _():
            def refine(step, x):
                factor_solve(block, mask, gap(x), soft, work, press)
                return x + press[...]

            finish(lax.fori_loop(0, 2, refine, zero))


def finish_kernel(axes, trial, near, node, owner, slot, got, back, out, pressure):
    circs, lats = axes
    owners = got.shape[0]
    rows, cols = trial.shape[1:]
    chunks = node.shape[0]
    my_circ, my_lat = lax.axis_index("circ"), lax.axis_index("lat")
    me = my_circ * lats + my_lat
    after = jnp.where(my_circ == circs - 1, my_lat, me + lats)
    before = jnp.where(my_circ == 0, (circs - 1) * lats + my_lat, me - lats)
    right_dev = jnp.minimum(me + 1, owners - 1)
    left_dev = jnp.maximum(me - 1, 0)
    kc, kl, diag_k = near[0], near[1], near[2]
    row, col = iota((rows, cols), 0), iota((rows, cols), 1)
    for c in range(3):
        source = back if c < 2 else got
        rows_at = (4 + c,) * 4 if c < 2 else (4, 5, 6, 7)
        down, up, east, west = [
            source[device, at] for device, at in zip((after, before, right_dev, left_dev), rows_at)
        ]
        east = jnp.where(my_lat < lats - 1, east, 0.0)
        west = jnp.where(my_lat > 0, west, 0.0)
        circ_in = jnp.where(row == rows - 1, down, jnp.where(row == 0, up, 0.0))
        lat_in = jnp.where(
            col == cols - 1, column(east), jnp.where(col == 0, column(west), 0.0)
        )
        out[c] = trial[c] + (kc * circ_in + kl * lat_in) / diag_k

    for j in range(4):
        pressure[j : j + 1, :] = back[me, j]
    answers = jnp.concatenate([back[:, j, 0, :] for j in range(4)], axis=0)
    answers = jnp.concatenate(thirds(answers), axis=1).astype(BF16)
    step = 2 if chunks % 2 == 0 else 1
    span = step * LANES
    left, right = [], []
    for first in range(0, chunks, step):
        nodes = wide(node, first, step)
        where = wide(slot, first, step)
        device = wide(owner, first, step)
        low = where & (LANES - 1)
        source = jnp.where(device < 0, -1, (where >> log2(LANES)) * owners + device)
        one_low = (iota((LANES, span), 0) == low).astype(F32).astype(BF16)
        found = jnp.dot(
            answers, jnp.concatenate([one_low] * 3, axis=0), preferred_element_type=F32
        )
        push = jnp.sum(
            jnp.where(iota((4 * owners, span), 0) == source, found, 0.0), axis=0, keepdims=True
        )
        one_circ = iota((rows, span), 0) == nodes >> log2(cols)
        left.append(
            jnp.concatenate(
                [jnp.where(one_circ, x, 0.0) for x in thirds(push)], axis=0
            ).astype(BF16)
        )
        right.append((iota((cols, span), 0) == (nodes & (cols - 1))).astype(F32).astype(BF16))
    force = lax.dot_general(
        jnp.concatenate(left, axis=1),
        jnp.concatenate(right, axis=1),
        (((1,), (1,)), ((), ())),
        preferred_element_type=F32,
    )
    force = force[:rows] + force[rows : 2 * rows] + force[2 * rows :]
    out[2] = out[2] - force / diag_k


def shards(
    disp, stiff, spin, load, foot_node, foot_dest, foot_slot, foot_count, road, active, influence
):
    circs, lats = lax.axis_size("circ"), lax.axis_size("lat")
    owners = circs * lats
    size = road.shape[0]
    rows, cols = disp.shape[1:]
    assert rows == cols == LANES and size == 4 * LANES and circs > 2 and owners % 16 == 0
    anywhere = pl.BlockSpec(memory_space=pltpu.HBM)
    block = pl.BlockSpec(memory_space=pltpu.VMEM)
    params = pltpu.CompilerParams(vmem_limit_bytes=32 * 1024 * 1024)
    lists = [x.reshape(-1, LANES) for x in (foot_node, foot_dest, foot_slot)]
    listed = jax.ShapeDtypeStruct(lists[0].shape, I32)
    strip = (4, LANES)
    send, trial, near, nodes, owner, slots, roads, actives, blocks, late = pl.pallas_call(
        functools.partial(pack_kernel, (circs, lats)),
        in_specs=[pl.BlockSpec(memory_space=pltpu.SMEM)] * 2 + [anywhere] * 9,
        out_specs=[block] * 10,
        out_shape=[
            jax.ShapeDtypeStruct((owners, 9, 1, LANES), F32),
            jax.ShapeDtypeStruct((3, rows, cols), F32),
            jax.ShapeDtypeStruct((3, rows, cols), F32),
            listed,
            listed,
            listed,
            jax.ShapeDtypeStruct(strip, F32),
            jax.ShapeDtypeStruct(strip, I32),
            jax.ShapeDtypeStruct((size, size), F32),
            jax.ShapeDtypeStruct((2, owners, LANES), F32),
        ],
        scratch_shapes=[
            pltpu.VMEM((3, rows, cols), F32),
            pltpu.VMEM((2, rows, cols), F32),
            pltpu.VMEM((3, rows, cols), F32),
            pltpu.VMEM(lists[0].shape, I32),
            pltpu.SemaphoreType.DMA((9,)),
        ],
        compiler_params=params,
        name="pack_rows",
    )(
        foot_count, spin,
        *[
            pltpu.with_memory_space_constraint(x, pltpu.HBM)
            for x in (
                *lists, stiff, disp, load, road.reshape(strip), active.reshape(strip), influence[0]
            )
        ]
    )
    got = lax.all_to_all(send, ("circ", "lat"), split_axis=0, concat_axis=0, tiled=True)
    reply = pl.pallas_call(
        functools.partial(solve_kernel, lats),
        in_specs=[block] * 5,
        out_specs=block,
        out_shape=jax.ShapeDtypeStruct((owners, 6, 1, LANES), F32),
        scratch_shapes=[
            pltpu.VMEM((size, size + LANES), F32),
            pltpu.VMEM((1, size), F32),
            pltpu.VMEM((16, 16, LANES), F32),
            pltpu.VMEM((4, owners, LANES), F32),
        ],
        compiler_params=params,
        name="solve_patch",
    )(got, roads, actives, blocks, late)
    back = lax.all_to_all(reply, ("circ", "lat"), split_axis=0, concat_axis=0, tiled=True)
    new_disp, pressure = pl.pallas_call(
        functools.partial(finish_kernel, (circs, lats)),
        in_specs=[block] * 7,
        out_specs=[block, block],
        out_shape=[
            jax.ShapeDtypeStruct(disp.shape, F32),
            jax.ShapeDtypeStruct(strip, F32),
        ],
        compiler_params=params,
        name="finish_nodes",
    )(trial, near, nodes, owner, slots, got, back)
    return (new_disp, pressure.reshape(size))


def solution(mesh):
    return jax.shard_map(
        shards,
        mesh=mesh,
        in_specs=(
            P(None, ("cases", "circ"), "lat"),
            P(None, ("cases", "circ"), "lat"),
            P("cases"),
            P(None, ("cases", "circ"), "lat"),
            P(("cases", "circ", "lat")),
            P(("cases", "circ", "lat")),
            P(("cases", "circ", "lat")),
            P(("cases", "circ", "lat")),
            P(("cases", "circ", "lat")),
            P(("cases", "circ", "lat")),
            P(("cases", "circ", "lat"), None, None),
        ),
        out_specs=(P(None, ("cases", "circ"), "lat"), P(("cases", "circ", "lat"))),
        check_vma=False,
    )
```
